128 devices in a mesh: fsdp: 4 (over y), ctx: 32 (over x, z, core).
Axes of the slice: x: 4, y: 4, z: 4, core: 2. Of those that a mesh axis runs over, the one named last changes fastest.
Arguments:
- hidden_in: bfloat16 [4, 4096, 576], P('fsdp', 'ctx'), may hold values from -6 to 6
- positions: int32 [4, 4096], P('fsdp', 'ctx'), may hold values from 0 to 4095, as said below
- params: bfloat16 [2, 6144, 576], P(None, ('fsdp', 'ctx')), may hold values from -3 to 3, as said below
- gains: bfloat16 [2, 1152], P(None, ('fsdp', 'ctx')), may hold values from 0.796875 to 1.1953125
- cotangent: bfloat16 [4, 4096, 576], P('fsdp', 'ctx'), may hold values from -6 to 6
Outputs:
- hidden_out: bfloat16 [4, 4096, 576], P('fsdp', 'ctx')
- grad_in: float32 [4, 4096, 576], P('fsdp', 'ctx')
- grad_params: float32 [2, 6144, 576], P(None, ('fsdp', 'ctx'))
- grad_gains: float32 [2, 1152], P(None, ('fsdp', 'ctx'))
The draws below stay inside these ranges and needn't reach their ends.
Inputs may be any that keep to these rules, and one draw needn't show every extreme that they name: In each sequence every position of 0 to 4095 appears once; the 128 tokens of one device of ctx are the 64 consecutive positions of some block b and then those of block 63 - b, in order, b differing between devices. `params`: the layers' projection entries laid out as the steps state.
All inputs are finite; a program needn't handle non-finite values.
Results may differ from the reference program's by a relative error of at most 0.025.
Values may be sent and summed in bfloat16 or wider, within the bound.
A program may use at most 192 MiB of HBM per device.

```python
import jax
import jax.numpy as jnp
from jax import lax

MODEL_WIDTH = 576
FEEDFORWARD_SIZE = 1536
QUERY_HEADS = 9
KEY_VALUE_HEADS = 3
HEAD_SIZE = 64
TOK_DEV = 128
LAYERS = 2
SEQS = 4
SEQ_LEN = 4096


def draw_positions(key, part):
    key = jax.random.fold_in(key, 5)
    block_total = SEQ_LEN // TOK_DEV
    half_size = TOK_DEV // 2
    orders = jax.vmap(lambda sub_key: jax.random.permutation(sub_key, block_total))(jax.random.split(key, SEQS))
    index_all = jnp.arange(SEQ_LEN)
    device_of = index_all // TOK_DEV
    within = index_all % TOK_DEV
    pairs = orders[:, device_of]
    chosen = jnp.where(within[None, :] < half_size, pairs, 2 * block_total - 1 - pairs)
    return (chosen * half_size + (within % half_size)[None, :]).astype(jnp.int32)


def draw_params(key, part):
    key = jax.random.fold_in(key, 11)
    row_counts = [QUERY_HEADS * HEAD_SIZE, KEY_VALUE_HEADS * HEAD_SIZE, KEY_VALUE_HEADS * HEAD_SIZE, QUERY_HEADS * HEAD_SIZE, FEEDFORWARD_SIZE, FEEDFORWARD_SIZE, FEEDFORWARD_SIZE]
    factors = [MODEL_WIDTH ** (-0.5), MODEL_WIDTH ** (-0.5), MODEL_WIDTH ** (-0.5), 8.0 * (QUERY_HEADS * HEAD_SIZE) ** (-0.5), MODEL_WIDTH ** (-0.5), MODEL_WIDTH ** (-0.5), 2.0 * FEEDFORWARD_SIZE ** (-0.5)]
    layer_rows = []
    for layer_index in range(LAYERS):
        layer_key = jax.random.fold_in(key, layer_index)
        pieces = []
        for piece_index in range(len(row_counts)):
            piece_key = jax.random.fold_in(layer_key, piece_index)
            layout = (row_counts[piece_index], MODEL_WIDTH)
            factor = factors[piece_index]
            pieces.append(factor * jax.random.truncated_normal(piece_key, -4.0, 4.0, layout, jnp.float32))
        layer_rows.append(jnp.concatenate(pieces, 0))
    return jnp.stack(layer_rows).astype(jnp.bfloat16)


def block_levels(rng, dims, cuts, low, high):
    def one(dim, parts):
        steps = jax.random.uniform(jax.random.fold_in(jax.random.fold_in(rng, 6), dim), (parts,), jnp.float32, low / len(cuts), high / len(cuts))
        return jnp.repeat(jnp.exp(steps), dims[dim] // parts).reshape((-1,) + (1,) * (len(dims) - dim - 1))

    loudness = one(*cuts[0])
    for cut in cuts[1:]:
        loudness = loudness * one(*cut)
    return loudness


def gaussian(own_key, dims, deviation, limit, shards=(), dtype=jnp.bfloat16):
    result = jax.random.normal(own_key, dims, jnp.float32) * deviation
    if len(shards) > 0:
        result = block_levels(own_key, dims, shards, -0.22, 0.18) * result
    return jnp.clip(result, min=-limit, max=limit).astype(dtype)


def setup_inputs(seed: int = 0) -> dict:
    keys = jax.random.split(jax.random.key(seed), 6)
    return {
        "hidden_in": gaussian(keys[0], (SEQS, SEQ_LEN, MODEL_WIDTH), 1.0, 6.0, ((0, 4), (1, 32))),
        "positions": draw_positions(jax.random.fold_in(keys[5], 71), 0),
        "params": draw_params(jax.random.fold_in(keys[5], 71), 0),
        "gains": jnp.clip(1.0 + 0.04 * jax.random.normal(keys[3], (LAYERS, 2 * MODEL_WIDTH), jnp.float32), 0.796875, 1.1953125).astype(jnp.bfloat16),
        "cotangent": gaussian(keys[4], (SEQS, SEQ_LEN, MODEL_WIDTH), 1.0, 6.0, ((0, 4), (1, 32))),
    }


EPSILON = 1e-05
THETA = 100000.0
MASKED = -1e+30
HIGHEST = lax.Precision.HIGHEST

@jax.custom_vjp
def low(v):
    return lax.optimization_barrier(v.astype(jnp.bfloat16)).astype(jnp.float32)

@jax.custom_vjp
def low_back(v):
    return v

def low_keep(v):
    return (low(v), None)

def low_pass(kept, grad):
    return (grad,)

def back_keep(v):
    return (v, None)

def back_low(kept, grad):
    return (low(grad),)
low.defvjp(low_keep, low_pass)
low_back.defvjp(back_keep, back_low)

def unpack(weight_rows):
    row_counts = [QUERY_HEADS * HEAD_SIZE, KEY_VALUE_HEADS * HEAD_SIZE, KEY_VALUE_HEADS * HEAD_SIZE, QUERY_HEADS * HEAD_SIZE, FEEDFORWARD_SIZE, FEEDFORWARD_SIZE, FEEDFORWARD_SIZE]
    pieces = []
    offset = 0
    for amount in row_counts:
        pieces.append(weight_rows[offset:offset + amount])
        offset += amount
    return pieces

def angle_tables(places):
    frequency = 1.0 / THETA ** (jnp.arange(0, HEAD_SIZE, 2).astype(jnp.float32) / HEAD_SIZE)
    phases = places.astype(jnp.float32)[:, None] * frequency[None, :]
    return (jnp.cos(phases)[:, None, :], jnp.sin(phases)[:, None, :])

def apply_rotation(shaped, cosine_lookup, sine_lookup):
    half_size = shaped.shape[-1] // 2
    first_half = shaped[..., :half_size]
    second_half = shaped[..., half_size:]
    return jnp.concatenate([first_half * cosine_lookup - second_half * sine_lookup, second_half * cosine_lookup + first_half * sine_lookup], -1)

def times_transposed(left_side, stored_rows):
    return jnp.dot(left_side, stored_rows.T, precision=HIGHEST)

def matrix_multiply(left_side, right_side):
    return jnp.dot(left_side, right_side, precision=HIGHEST)

def rms_gain(values, gain):
    return values * lax.rsqrt(lax.optimization_barrier(jnp.mean(values * values, -1, keepdims=True)) + EPSILON) * gain

def attention(queries, rows_of_keys, rows_of_values, places):
    sequence_rows = queries.shape[0]
    heads_per_group = QUERY_HEADS // KEY_VALUE_HEADS
    keys_wide = jnp.repeat(rows_of_keys, heads_per_group, axis=1)
    values_wide = jnp.repeat(rows_of_values, heads_per_group, axis=1)
    block_rows = min(512, sequence_rows)
    block_count = sequence_rows // block_rows
    score_scale = HEAD_SIZE ** (-0.5)

    def one_block(operands):
        query_block, place_block = operands
        scores = low_back(jnp.einsum('qhd,khd->hqk', query_block, keys_wide, precision=HIGHEST) * score_scale)
        allowed = places[None, None, :] <= place_block[None, :, None]
        scores = jnp.where(allowed, scores, MASKED)
        weights = low(jax.nn.softmax(scores, axis=-1))
        return jnp.einsum('hqk,khd->qhd', weights, values_wide, precision=HIGHEST)
    outputs = lax.map(jax.checkpoint(one_block), (queries.reshape(block_count, block_rows, QUERY_HEADS, HEAD_SIZE), places.reshape(block_count, block_rows)))
    return outputs.reshape(sequence_rows, QUERY_HEADS * HEAD_SIZE)

def one_layer(hidden, weight_rows, gain_row, places, cosine_lookup, sine_lookup):
    query_t, key_t, value_t, w_out, gate_t, up_t, w_down = unpack(weight_rows)
    gain_one = gain_row[:MODEL_WIDTH]
    gain_two = gain_row[MODEL_WIDTH:]
    sequence_rows = hidden.shape[0]
    first_normalized = low(rms_gain(hidden, gain_one))
    queries = low(apply_rotation(low_back(times_transposed(first_normalized, query_t)).reshape(sequence_rows, QUERY_HEADS, HEAD_SIZE), cosine_lookup, sine_lookup))
    rows_of_keys = low(apply_rotation(low_back(times_transposed(first_normalized, key_t)).reshape(sequence_rows, KEY_VALUE_HEADS, HEAD_SIZE), cosine_lookup, sine_lookup))
    rows_of_values = low(low_back(times_transposed(first_normalized, value_t))).reshape(sequence_rows, KEY_VALUE_HEADS, HEAD_SIZE)
    mixed = low(low_back(attention(queries, rows_of_keys, rows_of_values, places)))
    middle = hidden + low_back(matrix_multiply(mixed, w_out))
    normed_two = low(rms_gain(middle, gain_two))
    gate_values = low_back(times_transposed(normed_two, gate_t))
    up_values = low_back(times_transposed(normed_two, up_t))
    product = low(jax.nn.silu(gate_values) * up_values)
    return middle + low_back(matrix_multiply(product, w_down))

def reference(hidden_in, positions, params, gains, cotangent):
    start_values = hidden_in.astype(jnp.float32)
    weights_all = params.astype(jnp.float32)
    gains_all = gains.astype(jnp.float32)
    seed_grad = cotangent.astype(jnp.float32)

    def forward(inputs, weights, gain_rows):

        def per_sequence(carry, operands):
            sequence, places = operands
            cosine_lookup, sine_lookup = angle_tables(places)
            for layer_index in range(LAYERS):
                sequence = one_layer(sequence, weights[layer_index], gain_rows[layer_index], places, cosine_lookup, sine_lookup)
            return (carry, sequence)
        return lax.scan(per_sequence, jnp.zeros((), jnp.float32), (inputs, positions))[1]
    outputs, pullback = jax.vjp(forward, start_values, weights_all, gains_all)
    grad_input, grad_weights, grad_gain_rows = pullback(seed_grad)
    return (outputs.astype(jnp.bfloat16), grad_input, grad_weights, grad_gain_rows)
```

```python
import functools

import jax
import jax.numpy as jnp
from jax import lax
from jax.experimental import pallas as pl
from jax.experimental.pallas import tpu as pltpu
from jax.sharding import PartitionSpec as P

MODEL_WIDTH = 576
FEEDFORWARD_SIZE = 1536
QUERY_HEADS = 9
KEY_VALUE_HEADS = 3
HEAD_SIZE = 64
LAYERS = 2
KV_WIDTH = 2 * KEY_VALUE_HEADS * HEAD_SIZE

EPSILON = 1e-05
THETA = 100000.0
MASKED = -1e30
HIGHEST = lax.Precision.HIGHEST
MESH = pl.DeviceIdType.MESH
RING = 4


def place():
    t = lax.axis_index("ctx")
    return (lax.axis_index("fsdp"), t // 8, (t // 2) % 4, t % 2)


def device(y, x, z, c):
    return (y, x * 8 + z * 2 + c)


def moved(me, axis, step):
    other = list(me)
    other[axis] = (me[axis] + step) % RING
    return tuple(other)


def sibling(me):
    return (me[0], me[1], me[2], 1 - me[3])


def greet(peers):
    barrier = pltpu.get_barrier_semaphore()
    for peer in peers:
        pl.semaphore_signal(barrier, inc=1, device_id=device(*peer), device_id_type=MESH)
    pl.semaphore_wait(barrier, len(peers))


def gather_weights_kernel(params, extra, whole0, whole1, extras, sends, recvs, swap_sends, swap_recvs, own_sems):
    me = place()
    greet([moved(me, a, s) for a in range(3) for s in (1, 2, 3)] + [sibling(me)])
    streams = [
        (params.at[layer], whole, ((k, (k + 1) % 3, (k + 2) % 3)), (pl.ds(16 * k, 16),))
        for layer, whole in ((0, whole0), (1, whole1))
        for k in range(3)
    ]
    streams.insert(3, (extra, extras, (2, 1, 0), ()))
    count = len(streams)

    def region(n, phase, at, core):
        _, whole, axes, rows = streams[n]
        index = [at[0], at[1], at[2]]
        for axis in axes[:phase]:
            index[axis] = slice(None)
        return whole.at[tuple(index) + (core,) + rows]

    def copy(src, dst, n, phase, s, peer):
        return pltpu.make_async_remote_copy(
            src_ref=src, dst_ref=dst,
            send_sem=sends.at[n, phase, s - 1], recv_sem=recvs.at[n, phase, s - 1],
            device_id=device(*peer), device_id_type=MESH)

    def send(n, phase, s):
        source, _, axes, rows = streams[n]
        spot = region(n, phase, me, me[3])
        src = spot if phase else (source.at[rows] if rows else source)
        return copy(src, spot, n, phase, s, moved(me, axes[phase], s))

    def landed(n, phase, s):
        axis = streams[n][2][phase]
        spot = region(n, phase, moved(me, axis, -s), me[3])
        return copy(spot, spot, n, phase, s, moved(me, axis, s))

    def swap(n, s, core):
        spot = region(n, 2, moved(me, streams[n][2][2], -s), core)
        return pltpu.make_async_remote_copy(
            src_ref=spot, dst_ref=spot,
            send_sem=swap_sends.at[n, s], recv_sem=swap_recvs.at[n, s],
            device_id=device(*sibling(me)), device_id_type=MESH)

    own = [
        pltpu.make_async_copy(params.at[0], whole0.at[me], own_sems.at[0]),
        pltpu.make_async_copy(params.at[1], whole1.at[me], own_sems.at[1]),
        pltpu.make_async_copy(extra, extras.at[me], own_sems.at[2]),
    ]
    for n in range(count):
        for s in (2, 1, 3):
            send(n, 0, s).start()
    for c in own:
        c.start()
    for c in own:
        c.wait()
    for phase in (1, 2):
        for n in range(count):
            for s in (1, 2, 3):
                landed(n, phase - 1, s).wait_recv()
            for s in (2, 1, 3):
                send(n, phase, s).start()
            if phase == 2:
                swap(n, 0, me[3]).start()
    for n in range(count):
        for s in (1, 3, 2):
            landed(n, 2, s).wait_recv()
            swap(n, s, me[3]).start()
    for n in range(count):
        for phase in range(3):
            for s in (1, 2, 3):
                send(n, phase, s).wait_send()
        for s in range(4):
            swap(n, s, me[3]).wait_send()
            swap(n, s, 1 - me[3]).wait_recv()


def gather_weights(params, extra):
    whole = jax.ShapeDtypeStruct((4, 4, 4, 2, 48, MODEL_WIDTH), jnp.bfloat16)
    return pl.pallas_call(
        gather_weights_kernel,
        out_shape=(whole, whole, jax.ShapeDtypeStruct((4, 4, 4, 2, 16, 128), jnp.bfloat16)),
        in_specs=[pl.BlockSpec(memory_space=pl.ANY)] * 2,
        out_specs=(pl.BlockSpec(memory_space=pl.ANY),) * 3,
        scratch_shapes=[
            pltpu.SemaphoreType.DMA((7, 3, 3)),
            pltpu.SemaphoreType.DMA((7, 3, 3)),
            pltpu.SemaphoreType.DMA((7, 4)),
            pltpu.SemaphoreType.DMA((7, 4)),
            pltpu.SemaphoreType.DMA((3,)),
        ],
        compiler_params=pltpu.CompilerParams(collective_id=1, has_side_effects=True),
        name="gather_weights",
    )(params, extra)


def gather_rows_kernel(rows, whole, sends, recvs, swap_sends, swap_recvs, own_sem):
    me = place()
    greet([moved(me, a, s) for a in (1, 2) for s in (1, 2, 3)] + [sibling(me)])

    def region(k, phase, at, core):
        index = [at[1], at[2]]
        if phase >= 1:
            index[k] = slice(None)
        return whole.at[tuple(index) + (core, pl.ds(64 * k, 64))]

    own = pltpu.make_async_copy(rows, whole.at[me[1], me[2], me[3]], own_sem)
    own.start()

    def send(k, phase, s):
        axis = 1 + (k + phase) % 2
        src = rows.at[pl.ds(64 * k, 64)] if phase == 0 else region(k, phase, me, me[3])
        return pltpu.make_async_remote_copy(
            src_ref=src, dst_ref=region(k, phase, me, me[3]),
            send_sem=sends.at[k, phase, s - 1], recv_sem=recvs.at[k, phase, s - 1],
            device_id=device(*moved(me, axis, s)), device_id_type=MESH)

    def landed(k, phase, s):
        axis = 1 + (k + phase) % 2
        spot = region(k, phase, moved(me, axis, -s), me[3])
        return pltpu.make_async_remote_copy(
            src_ref=spot, dst_ref=spot,
            send_sem=sends.at[k, phase, s - 1], recv_sem=recvs.at[k, phase, s - 1],
            device_id=device(*moved(me, axis, s)), device_id_type=MESH)

    def swap(k, s, core):
        spot = region(k, 1, moved(me, 1 + (k + 1) % 2, -s), core)
        return pltpu.make_async_remote_copy(
            src_ref=spot, dst_ref=spot,
            send_sem=swap_sends.at[k, s], recv_sem=swap_recvs.at[k, s],
            device_id=device(*sibling(me)), device_id_type=MESH)

    for k in range(2):
        for s in (2, 1, 3):
            send(k, 0, s).start()
    own.wait()
    for k in range(2):
        for s in (1, 3, 2):
            landed(k, 0, s).wait_recv()
        for s in (2, 1, 3):
            send(k, 1, s).start()
    for k in range(2):
        swap(k, 0, me[3]).start()
    for s in (1, 3, 2):
        for k in range(2):
            landed(k, 1, s).wait_recv()
            swap(k, s, me[3]).start()
    for k in range(2):
        for phase in range(2):
            for s in (1, 2, 3):
                send(k, phase, s).wait_send()
        for s in range(4):
            swap(k, s, me[3]).wait_send()
            swap(k, s, 1 - me[3]).wait_recv()


def gather_rows(rows):
    return pl.pallas_call(
        gather_rows_kernel,
        out_shape=jax.ShapeDtypeStruct((4, 4, 2) + rows.shape, rows.dtype),
        in_specs=[pl.BlockSpec(memory_space=pl.ANY)],
        out_specs=pl.BlockSpec(memory_space=pl.ANY),
        scratch_shapes=[
            pltpu.SemaphoreType.DMA((2, 2, 3)),
            pltpu.SemaphoreType.DMA((2, 2, 3)),
            pltpu.SemaphoreType.DMA((2, 4)),
            pltpu.SemaphoreType.DMA((2, 4)),
            pltpu.SemaphoreType.DMA,
        ],
        compiler_params=pltpu.CompilerParams(collective_id=2, has_side_effects=True),
        name="gather_rows",
    )(rows)


def reduce_weights_kernel(
    gq, gk, gv, mixed, ggate, gup, product, n1, gb, n2, gd, gains,
    out, gains_out,
    grads, halves, first, landed_a, sum_a, landed_b, sum_b, landed_c, gain_in, gain_sum,
    swap_sends, swap_recvs, sends, recvs, gain_sends, gain_recvs,
):
    me = place()
    greet([moved(me, a, s) for a in range(3) for s in (1, 2, 3)] + [sibling(me)])

    def outer(left, right):
        return lax.dot_general(
            left, right, (((0,), (0,)), ((), ())), preferred_element_type=jnp.float32
        ).astype(jnp.bfloat16)

    def swap(y):
        return pltpu.make_async_remote_copy(
            src_ref=grads.at[y, :, :, 1 - me[3]], dst_ref=halves.at[y],
            send_sem=swap_sends.at[y], recv_sem=swap_recvs.at[y],
            device_id=device(*sibling(me)), device_id_type=MESH)

    def gain_copy(stage, s, peer):
        return pltpu.make_async_remote_copy(
            src_ref=gain_sum.at[stage], dst_ref=gain_in.at[stage, s - 1],
            send_sem=gain_sends.at[stage, s - 1], recv_sem=gain_recvs.at[stage, s - 1],
            device_id=device(*peer), device_id_type=MESH)

    gain_sum[0] = gains[...]
    gain_copy(0, 1, sibling(me)).start()
    for y, parts in (
        (1, ((ggate, n2),)),
        (2, ((gup, n2),)),
        (3, ((product, gd),)),
        (0, ((gq, n1), (gk, n1), (gv, n1), (mixed, gb))),
    ):
        at = 0
        for left, right in parts:
            flat = outer(left[...], right[...])
            count = flat.shape[0] // 48
            cut = flat.reshape(count, 48, MODEL_WIDTH)
            for i in range(count):
                j = at + i
                grads[y, j // 8, (j // 2) % 4, j % 2] = cut[i]
            at += count
        swap(y).start()

    axes = ((2, 1, 0), (0, 2, 1), (1, 0, 2))

    def send_a(k, s):
        peer = moved(me, axes[k][0], s)
        index = [slice(None)] * 3
        index[axes[k][0]] = peer[axes[k][0]]
        return pltpu.make_async_remote_copy(
            src_ref=first.at[tuple(index) + (pl.ds(16 * k, 16),)], dst_ref=landed_a.at[k, s - 1],
            send_sem=sends.at[0, k, s - 1], recv_sem=recvs.at[0, k, s - 1],
            device_id=device(*peer), device_id_type=MESH)

    def send_b(k, s):
        peer = moved(me, axes[k][1], s)
        rest = sorted(axes[k][1:])
        index = [slice(None)] * 2
        index[rest.index(axes[k][1])] = peer[axes[k][1]]
        return pltpu.make_async_remote_copy(
            src_ref=sum_a.at[(k,) + tuple(index)], dst_ref=landed_b.at[k, s - 1],
            send_sem=sends.at[1, k, s - 1], recv_sem=recvs.at[1, k, s - 1],
            device_id=device(*peer), device_id_type=MESH)

    def send_c(k, s):
        peer = moved(me, axes[k][2], s)
        return pltpu.make_async_remote_copy(
            src_ref=sum_b.at[k, peer[axes[k][2]]], dst_ref=landed_c.at[k, s - 1],
            send_sem=sends.at[2, k, s - 1], recv_sem=recvs.at[2, k, s - 1],
            device_id=device(*peer), device_id_type=MESH)

    def gain_stage(stage, axis):
        total = gain_sum[stage]
        for s in ((1,) if stage == 0 else (1, 2, 3)):
            gain_copy(stage, s, me).wait_recv()
            total = total + gain_in[stage, s - 1]
        if axis is None:
            gains_out[...] = total
            return
        gain_sum[stage + 1] = total
        for s in (1, 2, 3):
            gain_copy(stage + 1, s, moved(me, axis, s)).start()

    for y in (1, 2, 3, 0):
        swap(y).wait_recv()
        for x in range(4):
            for z in range(4):
                first[y, x, z] = (
                    grads[y, x, z, me[3]].astype(jnp.float32) + halves[y, x, z].astype(jnp.float32)
                ).astype(jnp.bfloat16)
    for k in range(3):
        for s in (2, 1, 3):
            send_a(k, s).start()
    gain_stage(0, 2)
    for k in range(3):
        for s in (1, 3, 2):
            send_a(k, s).wait_recv()
        axis = axes[k][0]
        index = [slice(None)] * 3
        index[axis] = me[axis]
        for i in range(4):
            for j in range(4):
                at = [i, j]
                at.insert(axis, me[axis])
                total = first[tuple(at) + (pl.ds(16 * k, 16),)].astype(jnp.float32)
                for s in range(3):
                    total = total + landed_a[k, s, i, j].astype(jnp.float32)
                sum_a[k, i, j] = total.astype(jnp.bfloat16)
        for s in (2, 1, 3):
            send_b(k, s).start()
    gain_stage(1, 1)
    for k in range(3):
        for s in (1, 3, 2):
            send_b(k, s).wait_recv()
        rest = sorted(axes[k][1:])
        for i in range(4):
            at = [i, i]
            at[rest.index(axes[k][1])] = me[axes[k][1]]
            total = sum_a[(k,) + tuple(at)].astype(jnp.float32)
            for s in range(3):
                total = total + landed_b[k, s, i].astype(jnp.float32)
            sum_b[k, i] = total.astype(jnp.bfloat16)
        for s in (2, 1, 3):
            send_c(k, s).start()
    gain_stage(2, 0)
    for k in range(3):
        for s in (1, 3, 2):
            send_c(k, s).wait_recv()
        total = sum_b[k, me[axes[k][2]]].astype(jnp.float32)
        for s in range(3):
            total = total + landed_c[k, s].astype(jnp.float32)
        out[pl.ds(16 * k, 16)] = total
    gain_stage(3, None)
    for y in range(4):
        swap(y).wait_send()
    for k in range(3):
        for s in (1, 2, 3):
            send_a(k, s).wait_send()
            send_b(k, s).wait_send()
            send_c(k, s).wait_send()
    gain_copy(0, 1, sibling(me)).wait_send()
    for stage, axis in ((1, 2), (2, 1), (3, 0)):
        for s in (1, 2, 3):
            gain_copy(stage, s, moved(me, axis, s)).wait_send()


def reduce_weights(lefts, rights, gains):
    bf = jnp.bfloat16
    w = MODEL_WIDTH
    return pl.pallas_call(
        reduce_weights_kernel,
        out_shape=(
            jax.ShapeDtypeStruct((48, w), jnp.float32),
            jax.ShapeDtypeStruct((16, 128), jnp.float32),
        ),
        in_specs=[pl.BlockSpec(memory_space=pltpu.VMEM)] * 12,
        out_specs=(pl.BlockSpec(memory_space=pltpu.VMEM),) * 2,
        scratch_shapes=[
            pltpu.VMEM((4, 4, 4, 2, 48, w), bf),
            pltpu.VMEM((4, 4, 4, 48, w), bf),
            pltpu.VMEM((4, 4, 4, 48, w), bf),
            pltpu.VMEM((3, 3, 4, 4, 16, w), bf),
            pltpu.VMEM((3, 4, 4, 16, w), bf),
            pltpu.VMEM((3, 3, 4, 16, w), bf),
            pltpu.VMEM((3, 4, 16, w), bf),
            pltpu.VMEM((3, 3, 16, w), bf),
            pltpu.VMEM((4, 3, 16, 128), jnp.float32),
            pltpu.VMEM((4, 16, 128), jnp.float32),
            pltpu.SemaphoreType.DMA((4,)),
            pltpu.SemaphoreType.DMA((4,)),
            pltpu.SemaphoreType.DMA((3, 3, 3)),
            pltpu.SemaphoreType.DMA((3, 3, 3)),
            pltpu.SemaphoreType.DMA((4, 3)),
            pltpu.SemaphoreType.DMA((4, 3)),
        ],
        compiler_params=pltpu.CompilerParams(
            collective_id=3, has_side_effects=True, vmem_limit_bytes=56 * 2**20
        ),
        name="reduce_weights",
    )(*lefts, *rights, gains)


def reduce_rows_kernel(
    terms, out, halves, first, landed_a, sum_a, landed_b,
    swap_sends, swap_recvs, sends, recvs,
):
    me = place()
    greet([moved(me, a, s) for a in (1, 2) for s in (1, 2, 3)] + [sibling(me)])

    def swap(k, x):
        return pltpu.make_async_remote_copy(
            src_ref=terms.at[x, :, 1 - me[3]], dst_ref=halves.at[x],
            send_sem=swap_sends.at[x], recv_sem=swap_recvs.at[x],
            device_id=device(*sibling(me)), device_id_type=MESH)

    for x in range(4):
        swap(0, x).start()
    axes = ((2, 1), (1, 2))

    def send_a(k, s):
        peer = moved(me, axes[k][0], s)
        index = [slice(None)] * 2
        index[axes[k][0] - 1] = peer[axes[k][0]]
        return pltpu.make_async_remote_copy(
            src_ref=first.at[tuple(index) + (pl.ds(64 * k, 64),)], dst_ref=landed_a.at[k, s - 1],
            send_sem=sends.at[0, k, s - 1], recv_sem=recvs.at[0, k, s - 1],
            device_id=device(*peer), device_id_type=MESH)

    def send_b(k, s):
        peer = moved(me, axes[k][1], s)
        return pltpu.make_async_remote_copy(
            src_ref=sum_a.at[k, peer[axes[k][1]]], dst_ref=landed_b.at[k, s - 1],
            send_sem=sends.at[1, k, s - 1], recv_sem=recvs.at[1, k, s - 1],
            device_id=device(*peer), device_id_type=MESH)

    for x in range(4):
        swap(0, x).wait_recv()
        for z in range(4):
            first[x, z] = (
                terms[x, z, me[3]].astype(jnp.float32) + halves[x, z].astype(jnp.float32)
            ).astype(jnp.bfloat16)
    for k in range(2):
        for s in (2, 1, 3):
            send_a(k, s).start()
    for k in range(2):
        for s in (1, 3, 2):
            send_a(k, s).wait_recv()
        axis = axes[k][0]
        for i in range(4):
            at = [i]
            at.insert(axis - 1, me[axis])
            total = first[tuple(at) + (pl.ds(64 * k, 64),)].astype(jnp.float32)
            for s in range(3):
                total = total + landed_a[k, s, i].astype(jnp.float32)
            sum_a[k, i] = total.astype(jnp.bfloat16)
        for s in (2, 1, 3):
            send_b(k, s).start()
    for k in range(2):
        for s in (1, 3, 2):
            send_b(k, s).wait_recv()
        total = sum_a[k, me[axes[k][1]]].astype(jnp.float32)
        for s in range(3):
            total = total + landed_b[k, s].astype(jnp.float32)
        out[pl.ds(64 * k, 64)] = total
    for x in range(4):
        swap(0, x).wait_send()
    for k in range(2):
        for s in (1, 2, 3):
            send_a(k, s).wait_send()
            send_b(k, s).wait_send()


def reduce_rows(terms):
    bf = jnp.bfloat16
    return pl.pallas_call(
        reduce_rows_kernel,
        out_shape=jax.ShapeDtypeStruct((128, KV_WIDTH), jnp.float32),
        in_specs=[pl.BlockSpec(memory_space=pltpu.VMEM)],
        out_specs=pl.BlockSpec(memory_space=pltpu.VMEM),
        scratch_shapes=[
            pltpu.VMEM((4, 4, 128, KV_WIDTH), bf),
            pltpu.VMEM((4, 4, 128, KV_WIDTH), bf),
            pltpu.VMEM((2, 3, 4, 64, KV_WIDTH), bf),
            pltpu.VMEM((2, 4, 64, KV_WIDTH), bf),
            pltpu.VMEM((2, 3, 64, KV_WIDTH), bf),
            pltpu.SemaphoreType.DMA((4,)),
            pltpu.SemaphoreType.DMA((4,)),
            pltpu.SemaphoreType.DMA((2, 2, 3)),
            pltpu.SemaphoreType.DMA((2, 2, 3)),
        ],
        compiler_params=pltpu.CompilerParams(
            collective_id=4, has_side_effects=True, vmem_limit_bytes=48 * 2**20
        ),
        name="reduce_rows",
    )(terms)


TILES = 33
CHUNK = 11
LANES = 384


def head_lanes():
    return lax.broadcasted_iota(jnp.int32, (1, LANES), 1) % 128 >= 64


def roll_heads(rows):
    return jnp.concatenate(
        [pltpu.roll(rows[:, 128 * h : 128 * h + 128], 64, 1) for h in range(3)], axis=1
    )


def pack_tile(lo, hi, keep_lo, use_a, use_b):
    lo = lo.astype(jnp.float32)
    hi = hi.astype(jnp.float32)
    zero = jnp.zeros_like(lo)
    a = jnp.where(use_a, lo, zero)
    b = jnp.where(use_b, hi, zero)
    if not keep_lo:
        lo = zero
    left = lax.broadcasted_iota(jnp.int32, (64, 128), 1) < 64
    keys = [jnp.where(left, lo, pltpu.roll(a, 64, 1)), jnp.where(left, b, zero)]
    values = [jnp.where(left, pltpu.roll(lo, 64, 1), a), jnp.where(left, pltpu.roll(b, 64, 1), zero)]
    return (
        jnp.concatenate(keys, axis=1).astype(jnp.bfloat16),
        jnp.concatenate(values, axis=1).astype(jnp.bfloat16),
    )


def pack_all(kv, own, tall, keys, values):
    def one(t, carry):
        use_a = jnp.broadcast_to(tall[t][:1] > 0.5, (64, 128))
        k, v = pack_tile(kv[t, :64], kv[t, 64:], True, use_a, jnp.logical_not(use_a))
        spot = pl.ds(pl.multiple_of(t * 64, 64), 64)
        keys[spot] = k
        values[spot] = v
        return carry

    lax.fori_loop(0, TILES - 1, one, 0)
    yes = jnp.full((64, 128), True)
    k, v = pack_tile(own[:64], own[64:], False, yes, jnp.logical_not(yes))
    keys[pl.ds(64 * (TILES - 1), 64)] = k
    values[pl.ds(64 * (TILES - 1), 64)] = v


def dot_cols(left, right):
    return lax.dot_general(
        left, right, (((1,), (1,)), ((), ())), preferred_element_type=jnp.float32
    )


def dot_rows(left, right):
    return lax.dot_general(
        left, right, (((0,), (0,)), ((), ())), preferred_element_type=jnp.float32
    )


def score_all(keys, queries, scores):
    for c in range(TILES // CHUNK):
        rows = pl.ds(64 * CHUNK * c, 64 * CHUNK)
        scores[rows] = dot_cols(keys[rows], queries)
    at = lax.broadcasted_iota(jnp.int32, (64, LANES), 0)
    lane = lax.broadcasted_iota(jnp.int32, (64, LANES), 1) % 128
    causal = jnp.logical_and(lane < 64, at <= lane)
    mine = pl.ds(pl.multiple_of(lax.axis_index("ctx") * 64, 64), 64)
    scores[mine] = jnp.where(jnp.logical_or(lane >= 64, causal), scores[mine], MASKED)
    last = pl.ds(64 * (TILES - 1), 64)
    scores[last] = jnp.where(causal, scores[last], MASKED)


def tile_rows(flags, row):
    crossed = jnp.where(head_lanes(), row, roll_heads(row))
    return jnp.where(flags[...] > 0.5, row, crossed)


def joined(rows, flags, merge, empty):
    straight = jnp.where(jnp.logical_or(head_lanes(), flags[...] > 0.5), rows, empty)
    crossed = jnp.where(jnp.logical_or(head_lanes(), flags[...] > 0.5), empty, rows)
    down = jnp.max if merge is jnp.maximum else jnp.sum
    one = down(straight, axis=0, keepdims=True)
    other = roll_heads(down(crossed, axis=0, keepdims=True))
    return merge(one, other)


def fold_lanes(product):
    return jnp.where(
        head_lanes(), product[:64] + roll_heads(product[128:192]), product[64:128]
    )


def attend_kernel(kv, own, queries, flags, tall, out, lse, keys, values, scores, rows):
    pack_all(kv, own, tall, keys, values)
    score_all(keys, queries[0], scores)
    rows[...] = jnp.full(rows.shape, MASKED, jnp.float32)

    for t in range(TILES):
        rows[pl.ds(t, 1)] = jnp.max(scores[pl.ds(64 * t, 64)], axis=0, keepdims=True)
    top = joined(rows[...], flags, jnp.maximum, MASKED)
    rows[...] = tile_rows(flags, top)
    total = jnp.zeros((256, LANES), jnp.float32)
    sums = []
    for c in range(TILES // CHUNK):
        parts = []
        for i in range(CHUNK):
            t = c * CHUNK + i
            raised = jnp.exp(scores[pl.ds(64 * t, 64)] - rows[pl.ds(t, 1)])
            sums.append(jnp.sum(raised, axis=0, keepdims=True))
            parts.append(raised.astype(jnp.bfloat16))
        spot = pl.ds(64 * CHUNK * c, 64 * CHUNK)
        total = total + dot_rows(values[spot], jnp.concatenate(parts, axis=0))
    rows[...] = jnp.zeros(rows.shape, jnp.float32)
    for t in range(TILES):
        rows[pl.ds(t, 1)] = sums[t]
    amount = joined(rows[...], flags, jnp.add, 0.0)
    out[0] = fold_lanes(total) / amount
    lse[0] = jnp.broadcast_to(top + jnp.log(amount), (8, LANES))


def attend(kv, own, queries, flags):
    return pl.pallas_call(
        attend_kernel,
        grid=(3,),
        out_shape=(
            jax.ShapeDtypeStruct((3, 64, LANES), jnp.float32),
            jax.ShapeDtypeStruct((3, 8, LANES), jnp.float32),
        ),
        in_specs=[
            pl.BlockSpec((32, 128, 128), lambda g: (0, 0, g)),
            pl.BlockSpec((128, 128), lambda g: (0, g)),
            pl.BlockSpec((1, LANES, 256), lambda g: (g, 0, 0)),
            pl.BlockSpec((40, LANES), lambda g: (0, 0)),
            pl.BlockSpec((40, 8, 128), lambda g: (0, 0, 0)),
        ],
        out_specs=(
            pl.BlockSpec((1, 64, LANES), lambda g: (g, 0, 0)),
            pl.BlockSpec((1, 8, LANES), lambda g: (g, 0, 0)),
        ),
        scratch_shapes=[
            pltpu.VMEM((64 * TILES, 256), jnp.bfloat16),
            pltpu.VMEM((64 * TILES, 256), jnp.bfloat16),
            pltpu.VMEM((64 * TILES, LANES), jnp.float32),
            pltpu.VMEM((40, LANES), jnp.float32),
        ],
        compiler_params=pltpu.CompilerParams(vmem_limit_bytes=40 * 2**20),
        name="attend",
    )(kv, own, queries, *flags)


def attend_back_kernel(
    kv, own, queries, grads, lse, inner, flags, tall, dq, dkv, keys, values, scores, lse_rows, inner_rows
):
    pack_all(kv, own, tall, keys, values)
    score_all(keys, queries[0], scores)
    lse_rows[...] = tile_rows(flags, lse[0, :1])
    inner_rows[...] = tile_rows(flags, inner[0, :1])
    total = jnp.zeros((256, LANES), jnp.float32)
    for c in range(TILES // CHUNK):
        spot = pl.ds(64 * CHUNK * c, 64 * CHUNK)
        grad_probs = dot_cols(values[spot], grads[0])
        probs, rest = [], []
        for i in range(CHUNK):
            t = c * CHUNK + i
            p = jnp.exp(scores[pl.ds(64 * t, 64)] - lse_rows[pl.ds(t, 1)])
            probs.append(p.astype(jnp.bfloat16))
            rest.append(
                (p * (grad_probs[64 * i : 64 * i + 64] - inner_rows[pl.ds(t, 1)])).astype(jnp.bfloat16)
            )
        probs = jnp.concatenate(probs, axis=0)
        rest = jnp.concatenate(rest, axis=0)
        total = total + dot_rows(keys[spot], rest)
        to_keys = jnp.dot(rest, queries[0], preferred_element_type=jnp.float32)
        to_values = jnp.dot(probs, grads[0], preferred_element_type=jnp.float32)
        left = lax.broadcasted_iota(jnp.int32, (64, 128), 1) < 64
        for i in range(CHUNK):
            t = c * CHUNK + i
            k0 = to_keys[64 * i : 64 * i + 64, :128]
            k1 = to_keys[64 * i : 64 * i + 64, 128:]
            v0 = to_values[64 * i : 64 * i + 64, :128]
            v1 = to_values[64 * i : 64 * i + 64, 128:]
            a = jnp.where(left, pltpu.roll(k0, 64, 1), v0)
            if t < TILES - 1:
                use_a = jnp.broadcast_to(tall[t][:1] > 0.5, (64, 128))
                lo = jnp.where(left, k0, pltpu.roll(v0, 64, 1)) + jnp.where(use_a, a, 0.0)
                hi = jnp.where(use_a, 0.0, jnp.where(left, k1, pltpu.roll(v1, 64, 1)))
                dkv[t, :64] = lo.astype(jnp.bfloat16)
                dkv[t, 64:] = hi.astype(jnp.bfloat16)
            else:
                me = lax.axis_index("ctx")
                dkv[me, :64] = (dkv[me, :64].astype(jnp.float32) + a).astype(jnp.bfloat16)
    dq[0] = fold_lanes(total)


def attend_back(kv, own, queries, grads, lse, inner, flags):
    return pl.pallas_call(
        attend_back_kernel,
        grid=(3,),
        out_shape=(
            jax.ShapeDtypeStruct((3, 64, LANES), jnp.float32),
            jax.ShapeDtypeStruct((32, 128, KV_WIDTH), jnp.bfloat16),
        ),
        in_specs=[
            pl.BlockSpec((32, 128, 128), lambda g: (0, 0, g)),
            pl.BlockSpec((128, 128), lambda g: (0, g)),
            pl.BlockSpec((1, LANES, 256), lambda g: (g, 0, 0)),
            pl.BlockSpec((1, LANES, 256), lambda g: (g, 0, 0)),
            pl.BlockSpec((1, 8, LANES), lambda g: (g, 0, 0)),
            pl.BlockSpec((1, 8, LANES), lambda g: (g, 0, 0)),
            pl.BlockSpec((40, LANES), lambda g: (0, 0)),
            pl.BlockSpec((40, 8, 128), lambda g: (0, 0, 0)),
        ],
        out_specs=(
            pl.BlockSpec((1, 64, LANES), lambda g: (g, 0, 0)),
            pl.BlockSpec((32, 128, 128), lambda g: (0, 0, g)),
        ),
        scratch_shapes=[
            pltpu.VMEM((64 * TILES, 256), jnp.bfloat16),
            pltpu.VMEM((64 * TILES, 256), jnp.bfloat16),
            pltpu.VMEM((64 * TILES, LANES), jnp.float32),
            pltpu.VMEM((40, LANES), jnp.float32),
            pltpu.VMEM((40, LANES), jnp.float32),
        ],
        compiler_params=pltpu.CompilerParams(vmem_limit_bytes=48 * 2**20),
        name="attend_back",
    )(kv, own, queries, grads, lse, inner, *flags)


def rotation_parts(places, heads):
    feature_width = heads * HEAD_SIZE
    half_size = HEAD_SIZE // 2
    feature_index = jnp.arange(feature_width)
    within = feature_index % HEAD_SIZE
    pair_index = within % half_size
    frequency = 1.0 / THETA ** ((2 * pair_index).astype(jnp.float32) / HEAD_SIZE)
    phases = places.astype(jnp.float32)[:, None] * frequency[None, :]
    head_of = feature_index // HEAD_SIZE
    same_head = head_of[:, None] == head_of[None, :]
    lower_target = within[None, :] < half_size
    from_upper = (within[:, None] == within[None, :] + half_size) & lower_target
    from_lower = (within[:, None] + half_size == within[None, :]) & jnp.logical_not(lower_target)
    swapper = jnp.where(
        same_head & from_upper, -1.0, jnp.where(same_head & from_lower, 1.0, 0.0)
    ).astype(jnp.float32)
    return (jnp.cos(phases), jnp.sin(phases), swapper)


def apply_rotation(values, parts):
    cosine_wide, sine_wide, swapper = parts
    swapped = jnp.dot(values, swapper, precision=HIGHEST)
    return values * cosine_wide + swapped * sine_wide


def inverse_rotation(values, parts):
    cosine_wide, sine_wide, swapper = parts
    swapped = jnp.dot(values, swapper, precision=HIGHEST)
    return values * cosine_wide - swapped * sine_wide


def rms_inverse(values):
    return lax.rsqrt(jnp.mean(values * values, -1, keepdims=True) + EPSILON)


def norm_backward(grad_normed, values, inverse, gain):
    unit_rows = values * inverse
    grad_gain = jnp.sum(grad_normed * unit_rows, 0)
    scaled = grad_normed * gain.astype(jnp.float32)
    grad_values = inverse * (scaled - unit_rows * jnp.mean(scaled * unit_rows, -1, keepdims=True))
    return (grad_values, grad_gain)


def unpack(weight_rows):
    ends = (576, 768, 960, 1536, 3072, 4608)
    return jnp.split(weight_rows, ends, axis=0)


def by_group(rows):
    return rows.reshape(128, QUERY_HEADS, HEAD_SIZE).transpose(1, 0, 2).reshape(3, LANES, HEAD_SIZE)


def spread(rows):
    parts = rows.reshape(128, QUERY_HEADS, HEAD_SIZE).transpose(1, 0, 2)
    lo, hi = parts[:, :64], parts[:, 64:]
    zero = jnp.zeros_like(lo)
    top = jnp.concatenate([zero, lo, hi, zero], -1)
    low = jnp.concatenate([hi, zero, zero, zero], -1)
    return jnp.concatenate([top, low], 1).reshape(3, LANES, 256)


def by_token(turned):
    return turned.reshape(3, HEAD_SIZE, 3, 128).transpose(3, 0, 2, 1).reshape(128, MODEL_WIDTH)


def paired(keys, values):
    both = jnp.stack([keys.reshape(128, 3, 64), values.reshape(128, 3, 64)], 2)
    return both.reshape(128, KV_WIDTH)


def layer_forward(hidden, weight_rows, gain_row, flags, query_parts, key_parts):
    query_t, key_t, value_t, w_out, gate_t, up_t, w_down = unpack(weight_rows)
    gain_one = gain_row[:MODEL_WIDTH]
    gain_two = gain_row[MODEL_WIDTH:]
    inverse_one = rms_inverse(hidden)
    normed_one = (hidden * inverse_one * gain_one.astype(jnp.float32)).astype(jnp.bfloat16)
    query_rows = apply_rotation(dot_cols(normed_one, query_t), query_parts).astype(jnp.bfloat16)
    key_rows = apply_rotation(dot_cols(normed_one, key_t), key_parts).astype(jnp.bfloat16)
    value_rows = dot_cols(normed_one, value_t).astype(jnp.bfloat16)
    own = paired(key_rows, value_rows)
    kv = gather_rows(own).reshape(32, 128, KV_WIDTH)
    queries = spread(query_rows * jnp.bfloat16(HEAD_SIZE ** (-0.5)))
    turned, lse = attend(kv, own, queries, flags)
    mixed = by_token(turned).astype(jnp.bfloat16)
    middle = hidden + jnp.dot(mixed, w_out, preferred_element_type=jnp.float32)
    inverse_two = rms_inverse(middle)
    normed_two = (middle * inverse_two * gain_two.astype(jnp.float32)).astype(jnp.bfloat16)
    gate_values = dot_cols(normed_two, gate_t)
    up_values = dot_cols(normed_two, up_t)
    product = (jax.nn.silu(gate_values) * up_values).astype(jnp.bfloat16)
    result = middle + jnp.dot(product, w_down, preferred_element_type=jnp.float32)
    kept = (
        hidden, inverse_one, normed_one, queries, own, kv, turned, lse, mixed,
        middle, inverse_two, normed_two, gate_values, up_values, product,
    )
    return result, kept


def layer_backward(grad_result, kept, weight_rows, gain_row, flags, query_parts, key_parts):
    (
        hidden, inverse_one, normed_one, queries, own, kv, turned, lse, mixed,
        middle, inverse_two, normed_two, gate_values, up_values, product,
    ) = kept
    query_t, key_t, value_t, w_out, gate_t, up_t, w_down = unpack(weight_rows)
    gain_one = gain_row[:MODEL_WIDTH]
    gain_two = gain_row[MODEL_WIDTH:]
    grad_down = grad_result.astype(jnp.bfloat16)
    grad_product = dot_cols(grad_down, w_down)
    sigmoid_values = jax.nn.sigmoid(gate_values)
    grad_gate = (
        grad_product * up_values * (sigmoid_values * (1.0 + gate_values * (1.0 - sigmoid_values)))
    ).astype(jnp.bfloat16)
    grad_up = (grad_product * (gate_values * sigmoid_values)).astype(jnp.bfloat16)
    grad_normed_two = jnp.dot(grad_gate, gate_t, preferred_element_type=jnp.float32) + jnp.dot(
        grad_up, up_t, preferred_element_type=jnp.float32
    )
    grad_middle, grad_gain_two = norm_backward(grad_normed_two, middle, inverse_two, gain_two)
    grad_middle = grad_middle + grad_result
    grad_branch = grad_middle.astype(jnp.bfloat16)
    grad_mixed = dot_cols(grad_branch, w_out).astype(jnp.bfloat16)
    inner = jnp.sum(
        turned * by_group(grad_mixed).astype(jnp.float32).transpose(0, 2, 1), 1, keepdims=True
    )
    inner = jnp.broadcast_to(inner, (3, 8, LANES))
    dq, dkv = attend_back(kv, own, queries, spread(grad_mixed), lse, inner, flags)
    sums = reduce_rows(dkv.reshape(4, 4, 2, 128, KV_WIDTH)).reshape(128, 3, 2, 64)
    key_sums = sums[:, :, 0].reshape(128, 192)
    value_sums = sums[:, :, 1].reshape(128, 192)
    grad_query = by_token(dq) * HEAD_SIZE ** (-0.5)
    grad_query = inverse_rotation(grad_query, query_parts).astype(jnp.bfloat16)
    key_gradient = inverse_rotation(key_sums, key_parts).astype(jnp.bfloat16)
    value_gradient = value_sums.astype(jnp.bfloat16)
    grad_normed_one = (
        jnp.dot(grad_query, query_t, preferred_element_type=jnp.float32)
        + jnp.dot(key_gradient, key_t, preferred_element_type=jnp.float32)
        + jnp.dot(value_gradient, value_t, preferred_element_type=jnp.float32)
    )
    grad_hidden, grad_gain_one = norm_backward(grad_normed_one, hidden, inverse_one, gain_one)
    grad_hidden = grad_hidden + grad_middle
    gain_terms = jnp.concatenate([grad_gain_one, grad_gain_two, jnp.zeros(896, jnp.float32)])
    owned, gain_sums = reduce_weights(
        (grad_query, key_gradient, value_gradient, mixed, grad_gate, grad_up, product),
        (normed_one, grad_branch, normed_two, grad_down),
        gain_terms.reshape(16, 128),
    )
    index = lax.axis_index("fsdp") * 32 + lax.axis_index("ctx")
    owned_gains = lax.dynamic_slice(gain_sums.reshape(-1), (index * 9,), (9,))
    return grad_hidden, owned, owned_gains


def on_device(hidden_in, positions, params, gains, cotangent):
    places = positions[0]
    block = places[0] // 64
    turn = block >= 32
    block = jnp.minimum(block, 63 - block)

    def lo_first(rows):
        return jnp.where(turn, jnp.concatenate([rows[64:], rows[:64]], 0), rows)

    places = lo_first(places)
    extra = jnp.concatenate(
        [jnp.pad(gains, ((0, 0), (0, 119))), jnp.full((14, 128), block, jnp.bfloat16)], 0
    )
    whole0, whole1, extras = gather_weights(params, extra)
    weights = (whole0.reshape(6144, MODEL_WIDTH), whole1.reshape(6144, MODEL_WIDTH))
    extras = extras.reshape(128, 16, 128)
    gain_rows = [extras[:, layer, :9].reshape(-1) for layer in range(LAYERS)]
    blocks = lax.dynamic_slice(
        extras[:, 2, 0], (lax.axis_index("fsdp") * 32,), (32,)
    ).astype(jnp.int32)
    flags = jnp.concatenate([blocks < block, jnp.full((8,), True)]).astype(jnp.float32)
    flags = (
        jnp.broadcast_to(flags[:, None], (40, LANES)),
        jnp.broadcast_to(flags[:, None, None], (40, 8, 128)),
    )
    query_parts = rotation_parts(places, QUERY_HEADS)
    key_parts = rotation_parts(places, KEY_VALUE_HEADS)
    hidden = lo_first(hidden_in[0]).astype(jnp.float32)
    kept = []
    for layer in range(LAYERS):
        hidden, state = layer_forward(
            hidden, weights[layer], gain_rows[layer], flags, query_parts, key_parts
        )
        kept.append(state)
    output_rows = lo_first(hidden.astype(jnp.bfloat16))
    grad_hidden = lo_first(cotangent[0]).astype(jnp.float32)
    owned = [None] * LAYERS
    owned_gains = [None] * LAYERS
    for layer in reversed(range(LAYERS)):
        grad_hidden, owned[layer], owned_gains[layer] = layer_backward(
            grad_hidden, kept[layer], weights[layer], gain_rows[layer], flags,
            query_parts, key_parts,
        )
    return (
        output_rows[None],
        lo_first(grad_hidden)[None],
        jnp.stack(owned),
        jnp.stack(owned_gains),
    )


def solution(mesh):
    return jax.shard_map(
        on_device,
        mesh=mesh,
        in_specs=(
            P("fsdp", "ctx", None),
            P("fsdp", "ctx"),
            P(None, ("fsdp", "ctx"), None),
            P(None, ("fsdp", "ctx")),
            P("fsdp", "ctx", None),
        ),
        out_specs=(
            P("fsdp", "ctx", None),
            P("fsdp", "ctx", None),
            P(None, ("fsdp", "ctx"), None),
            P(None, ("fsdp", "ctx")),
        ),
        check_vma=False,
    )
```

```python
import functools

import jax
import jax.numpy as jnp
from jax import lax
from jax.experimental import pallas as pl
from jax.experimental.pallas import tpu as pltpu
from jax.sharding import PartitionSpec as P

MODEL_WIDTH = 576
FEEDFORWARD_SIZE = 1536
QUERY_HEADS = 9
KEY_VALUE_HEADS = 3
HEAD_SIZE = 64
LAYERS = 2
KV_WIDTH = 2 * KEY_VALUE_HEADS * HEAD_SIZE

EPSILON = 1e-05
THETA = 100000.0
MASKED = -1e30
HIGHEST = lax.Precision.HIGHEST
MESH = pl.DeviceIdType.MESH
RING = 4


def place():
    t = lax.axis_index("ctx")
    return (lax.axis_index("fsdp"), t // 8, (t // 2) % 4, t % 2)


def device(y, x, z, c):
    return (y, x * 8 + z * 2 + c)


def moved(me, axis, step):
    other = list(me)
    other[axis] = (me[axis] + step) % RING
    return tuple(other)


def sibling(me):
    return (me[0], me[1], me[2], 1 - me[3])


def greet(peers):
    barrier = pltpu.get_barrier_semaphore()
    for peer in peers:
        pl.semaphore_signal(barrier, inc=1, device_id=device(*peer), device_id_type=MESH)
    pl.semaphore_wait(barrier, len(peers))


TILES = 33
CHUNK = 11
LANES = 384


def head_lanes():
    return lax.broadcasted_iota(jnp.int32, (1, LANES), 1) % 128 >= 64


def roll_heads(rows):
    return jnp.concatenate(
        [pltpu.roll(rows[:, 128 * h : 128 * h + 128], 64, 1) for h in range(3)], axis=1
    )


def pack_tile(lo, hi, keep_lo, use_a, use_b):
    lo = lo.astype(jnp.float32)
    hi = hi.astype(jnp.float32)
    zero = jnp.zeros_like(lo)
    a = jnp.where(use_a, lo, zero)
    b = jnp.where(use_b, hi, zero)
    if not keep_lo:
        lo = zero
    left = lax.broadcasted_iota(jnp.int32, (64, 128), 1) < 64
    keys = [jnp.where(left, lo, pltpu.roll(a, 64, 1)), jnp.where(left, b, zero)]
    values = [jnp.where(left, pltpu.roll(lo, 64, 1), a), jnp.where(left, pltpu.roll(b, 64, 1), zero)]
    return (
        jnp.concatenate(keys, axis=1).astype(jnp.bfloat16),
        jnp.concatenate(values, axis=1).astype(jnp.bfloat16),
    )


def pack_all(g, kv, own, tall, keys, values):
    def one(t, carry):
        at = kv[g, t // 8, (t // 2) % 4, t % 2]
        use_a = jnp.broadcast_to(tall[t][:1] > 0.5, (64, 128))
        k, v = pack_tile(at[:64], at[64:], True, use_a, jnp.logical_not(use_a))
        spot = pl.ds(pl.multiple_of(t * 64, 64), 64)
        keys[spot] = k
        values[spot] = v
        return carry

    lax.fori_loop(0, TILES - 1, one, 0)
    yes = jnp.full((64, 128), True)
    k, v = pack_tile(own[g, :64], own[g, 64:], False, yes, jnp.logical_not(yes))
    keys[pl.ds(64 * (TILES - 1), 64)] = k
    values[pl.ds(64 * (TILES - 1), 64)] = v


def dot_cols(left, right):
    return lax.dot_general(
        left, right, (((1,), (1,)), ((), ())), preferred_element_type=jnp.float32
    )


def dot_rows(left, right):
    return lax.dot_general(
        left, right, (((0,), (0,)), ((), ())), preferred_element_type=jnp.float32
    )


def score_all(keys, queries, scores):
    for c in range(TILES // CHUNK):
        rows = pl.ds(64 * CHUNK * c, 64 * CHUNK)
        scores[rows] = dot_cols(keys[rows], queries)
    at = lax.broadcasted_iota(jnp.int32, (64, LANES), 0)
    lane = lax.broadcasted_iota(jnp.int32, (64, LANES), 1) % 128
    causal = jnp.logical_and(lane < 64, at <= lane)
    mine = pl.ds(pl.multiple_of(lax.axis_index("ctx") * 64, 64), 64)
    scores[mine] = jnp.where(jnp.logical_or(lane >= 64, causal), scores[mine], MASKED)
    last = pl.ds(64 * (TILES - 1), 64)
    scores[last] = jnp.where(causal, scores[last], MASKED)


def tile_rows(flags, row):
    crossed = jnp.where(head_lanes(), row, roll_heads(row))
    return jnp.where(flags[...] > 0.5, row, crossed)


def joined(rows, flags, merge, empty):
    straight = jnp.where(jnp.logical_or(head_lanes(), flags[...] > 0.5), rows, empty)
    crossed = jnp.where(jnp.logical_or(head_lanes(), flags[...] > 0.5), empty, rows)
    down = jnp.max if merge is jnp.maximum else jnp.sum
    one = down(straight, axis=0, keepdims=True)
    other = roll_heads(down(crossed, axis=0, keepdims=True))
    return merge(one, other)


def fold_lanes(product):
    return jnp.where(
        head_lanes(), product[:64] + roll_heads(product[128:192]), product[64:128]
    )


def attend_group(g, own, kv, queries, flags, tall, out, lse, keys, values, scores, rows):
    pack_all(g, kv, own, tall, keys, values)
    score_all(keys, queries[g], scores)
    rows[...] = jnp.full(rows.shape, MASKED, jnp.float32)

    for t in range(TILES):
        rows[pl.ds(t, 1)] = jnp.max(scores[pl.ds(64 * t, 64)], axis=0, keepdims=True)
    top = joined(rows[...], flags, jnp.maximum, MASKED)
    rows[...] = tile_rows(flags, top)
    total = jnp.zeros((256, LANES), jnp.float32)
    sums = []
    for c in range(TILES // CHUNK):
        parts = []
        for i in range(CHUNK):
            t = c * CHUNK + i
            raised = jnp.exp(scores[pl.ds(64 * t, 64)] - rows[pl.ds(t, 1)])
            sums.append(jnp.sum(raised, axis=0, keepdims=True))
            parts.append(raised.astype(jnp.bfloat16))
        spot = pl.ds(64 * CHUNK * c, 64 * CHUNK)
        total = total + dot_rows(values[spot], jnp.concatenate(parts, axis=0))
    rows[...] = jnp.zeros(rows.shape, jnp.float32)
    for t in range(TILES):
        rows[pl.ds(t, 1)] = sums[t]
    amount = joined(rows[...], flags, jnp.add, 0.0)
    out[g] = fold_lanes(total) / amount
    lse[g] = jnp.broadcast_to(top + jnp.log(amount), (8, LANES))


def attend_back_group(
    g, me, kv, own, queries, grads, lse, inner, flags, tall, dq, dkv,
    keys, values, scores, lse_rows, inner_rows,
):
    pack_all(g, kv, own, tall, keys, values)
    score_all(keys, queries[g], scores)
    lse_rows[...] = tile_rows(flags, lse[g][:1])
    inner_rows[...] = tile_rows(flags, inner[g][:1])
    total = jnp.zeros((256, LANES), jnp.float32)
    for c in range(TILES // CHUNK):
        spot = pl.ds(64 * CHUNK * c, 64 * CHUNK)
        grad_probs = dot_cols(values[spot], grads[g])
        probs, rest = [], []
        for i in range(CHUNK):
            t = c * CHUNK + i
            p = jnp.exp(scores[pl.ds(64 * t, 64)] - lse_rows[pl.ds(t, 1)])
            probs.append(p.astype(jnp.bfloat16))
            rest.append(
                (p * (grad_probs[64 * i : 64 * i + 64] - inner_rows[pl.ds(t, 1)])).astype(jnp.bfloat16)
            )
        probs = jnp.concatenate(probs, axis=0)
        rest = jnp.concatenate(rest, axis=0)
        total = total + dot_rows(keys[spot], rest)
        to_keys = jnp.dot(rest, queries[g], preferred_element_type=jnp.float32)
        to_values = jnp.dot(probs, grads[g], preferred_element_type=jnp.float32)
        left = lax.broadcasted_iota(jnp.int32, (64, 128), 1) < 64
        for i in range(CHUNK):
            t = c * CHUNK + i
            k0 = to_keys[64 * i : 64 * i + 64, :128]
            k1 = to_keys[64 * i : 64 * i + 64, 128:]
            v0 = to_values[64 * i : 64 * i + 64, :128]
            v1 = to_values[64 * i : 64 * i + 64, 128:]
            a = jnp.where(left, pltpu.roll(k0, 64, 1), v0)
            if t < TILES - 1:
                use_a = jnp.broadcast_to(tall[t][:1] > 0.5, (64, 128))
                lo = jnp.where(left, k0, pltpu.roll(v0, 64, 1)) + jnp.where(use_a, a, 0.0)
                hi = jnp.where(use_a, 0.0, jnp.where(left, k1, pltpu.roll(v1, 64, 1)))
                dkv[g, t // 8, (t // 2) % 4, t % 2, :64] = lo.astype(jnp.bfloat16)
                dkv[g, t // 8, (t // 2) % 4, t % 2, 64:] = hi.astype(jnp.bfloat16)
            else:
                spot = (g, me[1], me[2], me[3], pl.ds(0, 64))
                dkv[spot] = (dkv[spot].astype(jnp.float32) + a).astype(jnp.bfloat16)
    dq[g] = fold_lanes(total)


def weight_gather(me, source, whole, sends, recvs, swap_sends, swap_recvs, own_sem):
    def region(k, phase, at, core):
        index = [at[0], at[1], at[2]]
        for i in range(phase):
            index[(k + i) % 3] = slice(None)
        return whole.at[tuple(index) + (core, pl.ds(16 * k, 16))]

    def copy(src, dst, k, phase, s):
        return pltpu.make_async_remote_copy(
            src_ref=src, dst_ref=dst,
            send_sem=sends.at[k, phase, s - 1], recv_sem=recvs.at[k, phase, s - 1],
            device_id=device(*moved(me, (k + phase) % 3, s)), device_id_type=MESH)

    def send(k, phase, s):
        spot = region(k, phase, me, me[3])
        return copy(spot if phase else source.at[pl.ds(16 * k, 16)], spot, k, phase, s)

    def landed(k, phase, s):
        spot = region(k, phase, moved(me, (k + phase) % 3, -s), me[3])
        return copy(spot, spot, k, phase, s)

    def swap(k, s, core):
        spot = region(k, 2, moved(me, (k + 2) % 3, -s), core)
        return pltpu.make_async_remote_copy(
            src_ref=spot, dst_ref=spot,
            send_sem=swap_sends.at[k, s], recv_sem=swap_recvs.at[k, s],
            device_id=device(*sibling(me)), device_id_type=MESH)

    def begin():
        own = pltpu.make_async_copy(source, whole.at[me], own_sem)
        own.start()
        for k in range(3):
            for s in (2, 1, 3):
                send(k, 0, s).start()
        own.wait()

    def forward(phase):
        for k in range(3):
            for s in (1, 3, 2):
                landed(k, phase - 1, s).wait_recv()
            for s in (2, 1, 3):
                send(k, phase, s).start()
            if phase == 2:
                swap(k, 0, me[3]).start()

    def exchange():
        for s in (1, 3, 2):
            for k in range(3):
                landed(k, 2, s).wait_recv()
                swap(k, s, me[3]).start()

    def finish():
        for k in range(3):
            for phase in range(3):
                for s in (1, 2, 3):
                    send(k, phase, s).wait_send()
            for s in range(4):
                swap(k, s, me[3]).wait_send()
                swap(k, s, 1 - me[3]).wait_recv()

    return begin, forward, exchange, finish


WEIGHT_GATHER_SEMS = [
    pltpu.SemaphoreType.DMA((3, 3, 3)),
    pltpu.SemaphoreType.DMA((3, 3, 3)),
    pltpu.SemaphoreType.DMA((3, 4)),
    pltpu.SemaphoreType.DMA((3, 4)),
    pltpu.SemaphoreType.DMA,
]
WHOLE = jax.ShapeDtypeStruct((4, 4, 4, 2, 48, MODEL_WIDTH), jnp.bfloat16)
ALL_PEERS = tuple((a, s) for a in range(3) for s in (1, 2, 3))


def greet_all(me):
    greet([moved(me, a, s) for a, s in ALL_PEERS] + [sibling(me)])


def row_gather(me, own, kv, sends, recvs, swap_sends, swap_recvs, own_sems):
    def region(g, k, phase, at, core):
        index = [at[1], at[2]]
        if phase >= 1:
            index[1 - k] = slice(None)
        return kv.at[(g,) + tuple(index) + (core, pl.ds(64 * k, 64))]

    def axis_of(k, phase):
        return 1 + (1 - k + phase) % 2

    def copy(src, dst, g, k, phase, s):
        return pltpu.make_async_remote_copy(
            src_ref=src, dst_ref=dst,
            send_sem=sends.at[g, k, phase, s - 1], recv_sem=recvs.at[g, k, phase, s - 1],
            device_id=device(*moved(me, axis_of(k, phase), s)), device_id_type=MESH)

    def send(g, k, phase, s):
        spot = region(g, k, phase, me, me[3])
        return copy(spot if phase else own.at[g, pl.ds(64 * k, 64)], spot, g, k, phase, s)

    def landed(g, k, phase, s):
        spot = region(g, k, phase, moved(me, axis_of(k, phase), -s), me[3])
        return copy(spot, spot, g, k, phase, s)

    def swap(g, k, s, core):
        spot = region(g, k, 1, moved(me, axis_of(k, 1), -s), core)
        return pltpu.make_async_remote_copy(
            src_ref=spot, dst_ref=spot,
            send_sem=swap_sends.at[g, k, s], recv_sem=swap_recvs.at[g, k, s],
            device_id=device(*sibling(me)), device_id_type=MESH)

    def keep(g):
        return pltpu.make_async_copy(own.at[g], kv.at[g, me[1], me[2], me[3]], own_sems.at[g])

    def begin(g):
        for s in (2, 1, 3):
            for k in range(2):
                send(g, k, 0, s).start()
        keep(g).start()

    def forward(g):
        keep(g).wait()
        for k in range(2):
            for s in (1, 3, 2):
                landed(g, k, 0, s).wait_recv()
            for s in (2, 1, 3):
                send(g, k, 1, s).start()
            swap(g, k, 0, me[3]).start()

    def arrive(g):
        for s in (1, 3, 2):
            for k in range(2):
                landed(g, k, 1, s).wait_recv()
                swap(g, k, s, me[3]).start()
        for k in range(2):
            for s in range(4):
                swap(g, k, s, 1 - me[3]).wait_recv()

    def finish(g):
        for k in range(2):
            for phase in range(2):
                for s in (1, 2, 3):
                    send(g, k, phase, s).wait_send()
            for s in range(4):
                swap(g, k, s, me[3]).wait_send()

    return begin, forward, arrive, finish


def forward_kernel(
    own, queries, flags, tall, source, out, lse, kv, whole,
    keys, values, scores, rows, *sems
):
    me = place()
    greet_all(me)
    begin, forward, arrive, finish = row_gather(me, own, kv, *sems[:5])
    w_begin, w_forward, w_exchange, w_finish = weight_gather(me, source, whole, *sems[5:])
    for g in range(3):
        begin(g)
    w_begin()
    for g in range(3):
        forward(g)
    w_forward(1)

    def one(g, carry):
        arrive(g)

        @pl.when(g == 1)
        def _():
            w_forward(2)

        attend_group(g, own, kv, queries, flags, tall, out, lse, keys, values, scores, rows)
        return carry

    lax.fori_loop(0, 3, one, 0)
    w_exchange()
    for g in range(3):
        finish(g)
    w_finish()


def attention_forward(own, queries, flags, source):
    vmem = pl.BlockSpec(memory_space=pltpu.VMEM)
    hbm = pl.BlockSpec(memory_space=pl.ANY)
    return pl.pallas_call(
        forward_kernel,
        out_shape=(
            jax.ShapeDtypeStruct((3, 64, LANES), jnp.float32),
            jax.ShapeDtypeStruct((3, 8, LANES), jnp.float32),
            jax.ShapeDtypeStruct((3, 4, 4, 2, 128, 128), jnp.bfloat16),
            WHOLE,
        ),
        in_specs=[vmem, vmem, vmem, vmem, hbm],
        out_specs=(vmem, vmem, vmem, hbm),
        scratch_shapes=[
            pltpu.VMEM((64 * TILES, 256), jnp.bfloat16),
            pltpu.VMEM((64 * TILES, 256), jnp.bfloat16),
            pltpu.VMEM((64 * TILES, LANES), jnp.float32),
            pltpu.VMEM((40, LANES), jnp.float32),
            pltpu.SemaphoreType.DMA((3, 2, 2, 3)),
            pltpu.SemaphoreType.DMA((3, 2, 2, 3)),
            pltpu.SemaphoreType.DMA((3, 2, 4)),
            pltpu.SemaphoreType.DMA((3, 2, 4)),
            pltpu.SemaphoreType.DMA((3,)),
        ] + WEIGHT_GATHER_SEMS,
        compiler_params=pltpu.CompilerParams(
            collective_id=2, has_side_effects=True, vmem_limit_bytes=40 * 2**20
        ),
        name="attention_forward",
    )(own, queries, *flags, source)


def weight_reduce(
    me, planes, out, grads, halves, first, landed_a, sum_a, landed_b, sum_b, landed_c,
    swap_sends, swap_recvs, sends, recvs,
):
    axes = ((2, 1, 0), (0, 2, 1), (1, 0, 2))

    def outer(left, right):
        return dot_rows(left, right).astype(jnp.bfloat16)

    def swap(y):
        return pltpu.make_async_remote_copy(
            src_ref=grads.at[y, :, :, 1 - me[3]], dst_ref=halves.at[y],
            send_sem=swap_sends.at[y], recv_sem=swap_recvs.at[y],
            device_id=device(*sibling(me)), device_id_type=MESH)

    def multiply(y):
        at = 0
        for left, right in planes[y]:
            flat = outer(left[...], right[...])
            count = flat.shape[0] // 48
            cut = flat.reshape(count, 48, MODEL_WIDTH)
            for i in range(count):
                j = at + i
                grads[y, j // 8, (j // 2) % 4, j % 2] = cut[i]
            at += count
        swap(y).start()

    def copy(stage, src, dst, k, s, peer):
        return pltpu.make_async_remote_copy(
            src_ref=src, dst_ref=dst,
            send_sem=sends.at[stage, k, s - 1], recv_sem=recvs.at[stage, k, s - 1],
            device_id=device(*peer), device_id_type=MESH)

    def send(stage, k, s):
        axis = axes[k][stage]
        peer = moved(me, axis, s)
        if stage == 0:
            index = [slice(None)] * 3
            index[axis] = peer[axis]
            return copy(0, first.at[tuple(index) + (pl.ds(16 * k, 16),)], landed_a.at[k, s - 1], k, s, peer)
        if stage == 1:
            index = [slice(None)] * 2
            index[sorted(axes[k][1:]).index(axis)] = peer[axis]
            return copy(1, sum_a.at[(k,) + tuple(index)], landed_b.at[k, s - 1], k, s, peer)
        return copy(2, sum_b.at[k, peer[axis]], landed_c.at[k, s - 1], k, s, peer)

    def halve(y):
        swap(y).wait_recv()
        for x in range(4):
            for z in range(4):
                first[y, x, z] = (
                    grads[y, x, z, me[3]].astype(jnp.float32) + halves[y, x, z].astype(jnp.float32)
                ).astype(jnp.bfloat16)

    def begin():
        for k in range(3):
            for s in (2, 1, 3):
                send(0, k, s).start()

    def second():
        for k in range(3):
            for s in (1, 3, 2):
                send(0, k, s).wait_recv()
            axis = axes[k][0]
            for i in range(4):
                for j in range(4):
                    at = [i, j]
                    at.insert(axis, me[axis])
                    total = first[tuple(at) + (pl.ds(16 * k, 16),)].astype(jnp.float32)
                    for s in range(3):
                        total = total + landed_a[k, s, i, j].astype(jnp.float32)
                    sum_a[k, i, j] = total.astype(jnp.bfloat16)
            for s in (2, 1, 3):
                send(1, k, s).start()

    def third():
        for k in range(3):
            for s in (1, 3, 2):
                send(1, k, s).wait_recv()
            rest = sorted(axes[k][1:])
            for i in range(4):
                at = [i, i]
                at[rest.index(axes[k][1])] = me[axes[k][1]]
                total = sum_a[(k,) + tuple(at)].astype(jnp.float32)
                for s in range(3):
                    total = total + landed_b[k, s, i].astype(jnp.float32)
                sum_b[k, i] = total.astype(jnp.bfloat16)
            for s in (2, 1, 3):
                send(2, k, s).start()

    def finish():
        for k in range(3):
            for s in (1, 3, 2):
                send(2, k, s).wait_recv()
            total = sum_b[k, me[axes[k][2]]].astype(jnp.float32)
            for s in range(3):
                total = total + landed_c[k, s].astype(jnp.float32)
            out[pl.ds(16 * k, 16)] = total
        for y in sorted(planes):
            swap(y).wait_send()
        for stage in range(3):
            for k in range(3):
                for s in (1, 2, 3):
                    send(stage, k, s).wait_send()

    return multiply, halve, begin, second, third, finish


def weight_reduce_scratch():
    bf, w = jnp.bfloat16, MODEL_WIDTH
    return [
        pltpu.VMEM((4, 4, 4, 2, 48, w), bf),
        pltpu.VMEM((4, 4, 4, 48, w), bf),
        pltpu.VMEM((4, 4, 4, 48, w), bf),
        pltpu.VMEM((3, 3, 4, 4, 16, w), bf),
        pltpu.VMEM((3, 4, 4, 16, w), bf),
        pltpu.VMEM((3, 3, 4, 16, w), bf),
        pltpu.VMEM((3, 4, 16, w), bf),
        pltpu.VMEM((3, 3, 16, w), bf),
        pltpu.SemaphoreType.DMA((4,)),
        pltpu.SemaphoreType.DMA((4,)),
        pltpu.SemaphoreType.DMA((3, 3, 3)),
        pltpu.SemaphoreType.DMA((3, 3, 3)),
    ]


def row_reduce(
    me, terms, out, halves, first, landed_a, sum_a, landed_b, swap_sends, swap_recvs, sends, recvs
):
    axes = ((2, 1), (1, 2))

    def swap(g):
        return pltpu.make_async_remote_copy(
            src_ref=terms.at[g, :, :, 1 - me[3]], dst_ref=halves.at[g],
            send_sem=swap_sends.at[g], recv_sem=swap_recvs.at[g],
            device_id=device(*sibling(me)), device_id_type=MESH)

    def send(stage, g, k, s):
        axis = axes[k][stage]
        peer = moved(me, axis, s)
        if stage == 0:
            index = [slice(None)] * 2
            index[axis - 1] = peer[axis]
            src = first.at[(g,) + tuple(index) + (pl.ds(64 * k, 64),)]
            dst = landed_a.at[g, k, s - 1]
        else:
            src = sum_a.at[g, k, peer[axis]]
            dst = landed_b.at[g, k, s - 1]
        return pltpu.make_async_remote_copy(
            src_ref=src, dst_ref=dst,
            send_sem=sends.at[stage, g, k, s - 1], recv_sem=recvs.at[stage, g, k, s - 1],
            device_id=device(*peer), device_id_type=MESH)

    def begin(g):
        swap(g).start()

    def second(g):
        swap(g).wait_recv()
        for x in range(4):
            for z in range(4):
                first[g, x, z] = (
                    terms[g, x, z, me[3]].astype(jnp.float32) + halves[g, x, z].astype(jnp.float32)
                ).astype(jnp.bfloat16)
        for s in (2, 1, 3):
            for k in range(2):
                send(0, g, k, s).start()

    def third(g):
        for k in range(2):
            for s in (1, 3, 2):
                send(0, g, k, s).wait_recv()
            axis = axes[k][0]
            for i in range(4):
                at = [i]
                at.insert(axis - 1, me[axis])
                total = first[(g,) + tuple(at) + (pl.ds(64 * k, 64),)].astype(jnp.float32)
                for s in range(3):
                    total = total + landed_a[g, k, s, i].astype(jnp.float32)
                sum_a[g, k, i] = total.astype(jnp.bfloat16)
            for s in (2, 1, 3):
                send(1, g, k, s).start()

    def finish(g):
        for k in range(2):
            for s in (1, 3, 2):
                send(1, g, k, s).wait_recv()
            total = sum_a[g, k, me[axes[k][1]]].astype(jnp.float32)
            for s in range(3):
                total = total + landed_b[g, k, s].astype(jnp.float32)
            out[g, pl.ds(64 * k, 64)] = total

    def drain(g):
        swap(g).wait_send()
        for stage in range(2):
            for k in range(2):
                for s in (1, 2, 3):
                    send(stage, g, k, s).wait_send()

    return begin, second, third, finish, drain


def row_reduce_scratch():
    bf = jnp.bfloat16
    return [
        pltpu.VMEM((3, 4, 4, 128, 128), bf),
        pltpu.VMEM((3, 4, 4, 128, 128), bf),
        pltpu.VMEM((3, 2, 3, 4, 64, 128), bf),
        pltpu.VMEM((3, 2, 4, 64, 128), bf),
        pltpu.VMEM((3, 2, 3, 64, 128), bf),
        pltpu.SemaphoreType.DMA((3,)),
        pltpu.SemaphoreType.DMA((3,)),
        pltpu.SemaphoreType.DMA((2, 3, 2, 3)),
        pltpu.SemaphoreType.DMA((2, 3, 2, 3)),
    ]


def backward_kernel(shape, *refs):
    count = 1 + max(i for plane in shape.values() for pair in plane for i in pair)
    kv, own, queries, grads, lse, inner, flags, tall = refs[:8]
    arrays = refs[8 : 8 + count]
    dq, sums, owned = refs[8 + count : 11 + count]
    keys, values, scores, lse_rows, inner_rows, dkv = refs[11 + count : 17 + count]
    row_refs = refs[17 + count : 26 + count]
    weight_refs = refs[26 + count :]
    me = place()
    greet_all(me)
    planes = {
        y: [(arrays[i], arrays[j]) for i, j in pairs] for y, pairs in shape.items()
    }
    begin, second, third, finish, drain = row_reduce(me, dkv, sums, *row_refs)
    multiply, halve, w_begin, w_second, w_third, w_finish = weight_reduce(
        me, planes, owned, *weight_refs
    )
    first_sums = weight_refs[2]
    order = sorted(planes, key=lambda y: (y == 0, y))
    for y in order:
        multiply(y)

    def one(g, carry):
        attend_back_group(
            g, me, kv, own, queries, grads, lse, inner, flags, tall, dq, dkv,
            keys, values, scores, lse_rows, inner_rows,
        )
        begin(g)

        @pl.when(g == 0)
        def _():
            for y in order:
                halve(y)
            if 0 not in planes:
                first_sums[0] = jnp.zeros(first_sums.shape[1:], jnp.bfloat16)
            w_begin()

        @pl.when(g == 1)
        def _():
            second(0)

        @pl.when(g == 2)
        def _():
            third(0)
            second(1)
            w_second()

        return carry

    lax.fori_loop(0, 3, one, 0)
    second(2)
    third(1)
    w_third()
    third(2)
    w_finish()
    for g in range(3):
        finish(g)
    for g in range(3):
        drain(g)


def attention_backward(collective_id, shape, kv, own, queries, grads, lse, inner, flags, arrays):
    vmem = pl.BlockSpec(memory_space=pltpu.VMEM)
    return pl.pallas_call(
        functools.partial(backward_kernel, shape),
        out_shape=(
            jax.ShapeDtypeStruct((3, 64, LANES), jnp.float32),
            jax.ShapeDtypeStruct((3, 128, 128), jnp.float32),
            jax.ShapeDtypeStruct((48, MODEL_WIDTH), jnp.float32),
        ),
        in_specs=[vmem] * (8 + len(arrays)),
        out_specs=(vmem,) * 3,
        scratch_shapes=[
            pltpu.VMEM((64 * TILES, 256), jnp.bfloat16),
            pltpu.VMEM((64 * TILES, 256), jnp.bfloat16),
            pltpu.VMEM((64 * TILES, LANES), jnp.float32),
            pltpu.VMEM((40, LANES), jnp.float32),
            pltpu.VMEM((40, LANES), jnp.float32),
            pltpu.VMEM((3, 4, 4, 2, 128, 128), jnp.bfloat16),
        ] + row_reduce_scratch() + weight_reduce_scratch(),
        compiler_params=pltpu.CompilerParams(
            collective_id=collective_id, has_side_effects=True, vmem_limit_bytes=58 * 2**20
        ),
        name="attention_backward",
    )(kv, own, queries, grads, lse, inner, *flags, *arrays)


HALF_ROWS = ((0, 32), (32, 16))


def gather_first_kernel(
    source, extra, whole, extras, stage, sends, recvs, swap_sends, swap_recvs,
    y_sends, y_recvs, extra_sends, extra_recvs, own_sems
):
    me = place()
    greet_all(me)

    def y_copy(src, dst, n, s):
        return pltpu.make_async_remote_copy(
            src_ref=src, dst_ref=dst,
            send_sem=y_sends.at[n, s - 1], recv_sem=y_recvs.at[n, s - 1],
            device_id=device(*moved(me, 0, s)), device_id_type=MESH)

    def rows_along_y(s, y):
        return y_copy(source, stage.at[y], 0, s)

    def extra_region(phase, at, core):
        index = [at[0], at[1], at[2]]
        for axis in (0, 2, 1)[:phase]:
            index[axis] = slice(None)
        return extras.at[tuple(index) + (core,)]

    def extra_copy(phase, s, spot, src, peer):
        return pltpu.make_async_remote_copy(
            src_ref=src, dst_ref=spot,
            send_sem=extra_sends.at[phase, s], recv_sem=extra_recvs.at[phase, s],
            device_id=device(*peer), device_id_type=MESH)

    def extra_send(phase, s):
        spot = extra_region(phase, me, me[3])
        return extra_copy(phase, s, spot, spot if phase else extra, moved(me, (0, 2, 1)[phase], s))

    def extra_landed(phase, s):
        axis = (0, 2, 1)[phase]
        spot = extra_region(phase, moved(me, axis, -s), me[3])
        return extra_copy(phase, s, spot, spot, moved(me, axis, s))

    def extra_swap(core):
        spot = extra_region(3, me, core)
        return extra_copy(3, 0, spot, spot, sibling(me))

    def region(k, phase, at, core):
        index = [at[1], at[2]]
        if phase:
            index[k] = slice(None)
        return whole.at[tuple(index) + (core, pl.ds(*HALF_ROWS[k]))]

    def copy(src, dst, k, phase, s):
        return pltpu.make_async_remote_copy(
            src_ref=src, dst_ref=dst,
            send_sem=sends.at[k, phase, s - 1], recv_sem=recvs.at[k, phase, s - 1],
            device_id=device(*moved(me, 1 + (k + phase) % 2, s)), device_id_type=MESH)

    def send(k, phase, s):
        spot = region(k, phase, me, me[3])
        return copy(spot if phase else stage.at[0, pl.ds(*HALF_ROWS[k])], spot, k, phase, s)

    def landed(k, phase, s):
        spot = region(k, phase, moved(me, 1 + (k + phase) % 2, -s), me[3])
        return copy(spot, spot, k, phase, s)

    def swap(k, s, core):
        spot = region(k, 1, moved(me, 1 + (k + 1) % 2, -s), core)
        return pltpu.make_async_remote_copy(
            src_ref=spot, dst_ref=spot,
            send_sem=swap_sends.at[k, s], recv_sem=swap_recvs.at[k, s],
            device_id=device(*sibling(me)), device_id_type=MESH)

    for s in (2, 1, 3):
        rows_along_y(s, me[0]).start()
        extra_send(0, s).start()
    own = pltpu.make_async_copy(source, stage.at[me[0]], own_sems.at[0])
    own_extra = pltpu.make_async_copy(extra, extras.at[me], own_sems.at[1])
    own.start()
    own_extra.start()
    own.wait()
    own_extra.wait()
    for s in (1, 3, 2):
        rows_along_y(s, (me[0] - s) % RING).wait_recv()
    keep = pltpu.make_async_copy(stage.at[0], whole.at[me[1], me[2], me[3]], own_sems.at[2])
    keep.start()
    for k in range(2):
        for s in (2, 1, 3):
            send(k, 0, s).start()
    for s in (1, 3, 2):
        extra_landed(0, s).wait_recv()
    for s in (2, 1, 3):
        extra_send(1, s).start()
    keep.wait()
    for k in range(2):
        for s in (1, 3, 2):
            landed(k, 0, s).wait_recv()
        for s in (2, 1, 3):
            send(k, 1, s).start()
        swap(k, 0, me[3]).start()
    for s in (1, 3, 2):
        extra_landed(1, s).wait_recv()
    for s in (2, 1, 3):
        extra_send(2, s).start()
    for s in (1, 3, 2):
        for k in (1, 0):
            landed(k, 1, s).wait_recv()
            swap(k, s, me[3]).start()
    for s in (1, 3, 2):
        extra_landed(2, s).wait_recv()
    extra_swap(me[3]).start()
    for s in (1, 2, 3):
        rows_along_y(s, me[0]).wait_send()
        for phase in range(3):
            extra_send(phase, s).wait_send()
    for k in range(2):
        for phase in range(2):
            for s in (1, 2, 3):
                send(k, phase, s).wait_send()
        for s in range(4):
            swap(k, s, me[3]).wait_send()
            swap(k, s, 1 - me[3]).wait_recv()
    extra_swap(me[3]).wait_send()
    extra_swap(1 - me[3]).wait_recv()


def gather_first(source, extra):
    hbm = pl.BlockSpec(memory_space=pl.ANY)
    vmem = pl.BlockSpec(memory_space=pltpu.VMEM)
    return pl.pallas_call(
        gather_first_kernel,
        out_shape=(
            jax.ShapeDtypeStruct((4, 4, 2, 48, MODEL_WIDTH), jnp.bfloat16),
            jax.ShapeDtypeStruct((4, 4, 4, 2, 16, 128), jnp.bfloat16),
        ),
        in_specs=[hbm, hbm],
        out_specs=(hbm, hbm),
        scratch_shapes=[
            pltpu.VMEM((4, 48, MODEL_WIDTH), jnp.bfloat16),
            pltpu.SemaphoreType.DMA((2, 2, 3)),
            pltpu.SemaphoreType.DMA((2, 2, 3)),
            pltpu.SemaphoreType.DMA((2, 4)),
            pltpu.SemaphoreType.DMA((2, 4)),
            pltpu.SemaphoreType.DMA((1, 3)),
            pltpu.SemaphoreType.DMA((1, 3)),
            pltpu.SemaphoreType.DMA((4, 4)),
            pltpu.SemaphoreType.DMA((4, 4)),
            pltpu.SemaphoreType.DMA((3,)),
        ],
        compiler_params=pltpu.CompilerParams(collective_id=1, has_side_effects=True),
        name="gather_first",
    )(source, extra)


def reduce_last_kernel(
    gq, gk, gv, mixed, n1, gb, gains, out, gains_out,
    grads, halves, first, landed_a, sum_a, landed_b, sum_b, landed_y, gain_in, gain_sum,
    swap_sends, swap_recvs, sends, recvs, y_sends, y_recvs, gain_sends, gain_recvs
):
    me = place()
    greet_all(me)

    def gain_copy(stage, s, peer):
        return pltpu.make_async_remote_copy(
            src_ref=gain_sum.at[stage], dst_ref=gain_in.at[stage, s - 1],
            send_sem=gain_sends.at[stage, s - 1], recv_sem=gain_recvs.at[stage, s - 1],
            device_id=device(*peer), device_id_type=MESH)

    def gain_stage(stage, axis):
        total = gain_sum[stage]
        for s in (1,) if stage == 0 else (1, 2, 3):
            gain_copy(stage, s, me if stage else sibling(me)).wait_recv()
            total = total + gain_in[stage, s - 1]
        if axis is None:
            gains_out[...] = total
            return
        gain_sum[stage + 1] = total
        for s in (1, 2, 3):
            gain_copy(stage + 1, s, moved(me, axis, s)).start()

    def swap(x):
        return pltpu.make_async_remote_copy(
            src_ref=grads.at[x, :, 1 - me[3]], dst_ref=halves.at[x],
            send_sem=swap_sends.at[x], recv_sem=swap_recvs.at[x],
            device_id=device(*sibling(me)), device_id_type=MESH)

    def copy(stage, src, dst, k, s):
        return pltpu.make_async_remote_copy(
            src_ref=src, dst_ref=dst,
            send_sem=sends.at[stage, k, s - 1], recv_sem=recvs.at[stage, k, s - 1],
            device_id=device(*moved(me, 1 + (k + 1 + stage) % 2, s)), device_id_type=MESH)

    def send(stage, k, s):
        axis = 1 + (k + 1 + stage) % 2
        to = moved(me, axis, s)[axis]
        rows = pl.ds(*HALF_ROWS[k])
        if stage == 0:
            index = [slice(None)] * 2
            index[axis - 1] = to
            return copy(0, first.at[tuple(index) + (rows,)], landed_a.at[s - 1, :, rows], k, s)
        return copy(1, sum_a.at[to, rows], landed_b.at[s - 1, rows], k, s)

    def y_copy(s):
        return pltpu.make_async_remote_copy(
            src_ref=sum_b, dst_ref=landed_y.at[s - 1],
            send_sem=y_sends.at[s - 1], recv_sem=y_recvs.at[s - 1],
            device_id=device(*moved(me, 0, s)), device_id_type=MESH)

    gain_sum[0] = gains[...]
    gain_copy(0, 1, sibling(me)).start()
    at = 0
    for left, right in ((gq, n1), (gk, n1), (gv, n1), (mixed, gb)):
        flat = dot_rows(left[...], right[...]).astype(jnp.bfloat16)
        amount = flat.shape[0] // 48
        cut = flat.reshape(amount, 48, MODEL_WIDTH)
        for i in range(amount):
            j = at + i
            grads[j // 8, (j // 2) % 4, j % 2] = cut[i]
            if j % 8 == 7:
                swap(j // 8).start()
        at += amount
    gain_stage(0, 2)
    for x in range(4):
        swap(x).wait_recv()
        for z in range(4):
            first[x, z] = (
                grads[x, z, me[3]].astype(jnp.float32) + halves[x, z].astype(jnp.float32)
            ).astype(jnp.bfloat16)
    for k in range(2):
        for s in (2, 1, 3):
            send(0, k, s).start()
    gain_stage(1, 1)
    for k in (1, 0):
        rows = pl.ds(*HALF_ROWS[k])
        for s in (1, 3, 2):
            send(0, k, s).wait_recv()
        axis = 1 + (k + 1) % 2
        for i in range(4):
            spot = [i]
            spot.insert(axis - 1, me[axis])
            total = first[tuple(spot) + (rows,)].astype(jnp.float32)
            for s in range(3):
                total = total + landed_a[s, i, rows].astype(jnp.float32)
            sum_a[i, rows] = total.astype(jnp.bfloat16)
        for s in (2, 1, 3):
            send(1, k, s).start()
    gain_stage(2, 0)
    for k in (1, 0):
        rows = pl.ds(*HALF_ROWS[k])
        for s in (1, 3, 2):
            send(1, k, s).wait_recv()
        total = sum_a[me[1 + k % 2], rows].astype(jnp.float32)
        for s in range(3):
            total = total + landed_b[s, rows].astype(jnp.float32)
        sum_b[rows] = total.astype(jnp.bfloat16)
    for s in (2, 1, 3):
        y_copy(s).start()
    gain_stage(3, None)
    total = sum_b[...].astype(jnp.float32)
    for s in (1, 3, 2):
        y_copy(s).wait_recv()
        total = total + landed_y[s - 1].astype(jnp.float32)
    out[...] = total
    for x in range(4):
        swap(x).wait_send()
    for stage in range(2):
        for k in range(2):
            for s in (1, 2, 3):
                send(stage, k, s).wait_send()
    gain_copy(0, 1, sibling(me)).wait_send()
    for s in (1, 2, 3):
        y_copy(s).wait_send()
        for stage, axis in ((1, 2), (2, 1), (3, 0)):
            gain_copy(stage, s, moved(me, axis, s)).wait_send()


def reduce_last(arrays, gains):
    bf, w = jnp.bfloat16, MODEL_WIDTH
    vmem = pl.BlockSpec(memory_space=pltpu.VMEM)
    rows = gains.shape[0]
    return pl.pallas_call(
        reduce_last_kernel,
        out_shape=(
            jax.ShapeDtypeStruct((48, w), jnp.float32),
            jax.ShapeDtypeStruct(gains.shape, jnp.float32),
        ),
        in_specs=[vmem] * 7,
        out_specs=(vmem, vmem),
        scratch_shapes=[
            pltpu.VMEM((4, 4, 2, 48, w), bf),
            pltpu.VMEM((4, 4, 48, w), bf),
            pltpu.VMEM((4, 4, 48, w), bf),
            pltpu.VMEM((3, 4, 48, w), bf),
            pltpu.VMEM((4, 48, w), bf),
            pltpu.VMEM((3, 48, w), bf),
            pltpu.VMEM((48, w), bf),
            pltpu.VMEM((3, 48, w), bf),
            pltpu.VMEM((4, 3, rows, 128), jnp.float32),
            pltpu.VMEM((4, rows, 128), jnp.float32),
            pltpu.SemaphoreType.DMA((4,)),
            pltpu.SemaphoreType.DMA((4,)),
            pltpu.SemaphoreType.DMA((2, 2, 3)),
            pltpu.SemaphoreType.DMA((2, 2, 3)),
            pltpu.SemaphoreType.DMA((3,)),
            pltpu.SemaphoreType.DMA((3,)),
            pltpu.SemaphoreType.DMA((4, 3)),
            pltpu.SemaphoreType.DMA((4, 3)),
        ],
        compiler_params=pltpu.CompilerParams(
            collective_id=5, has_side_effects=True, vmem_limit_bytes=32 * 2**20
        ),
        name="reduce_last",
    )(*arrays, gains)


def rotation_parts(places, heads):
    feature_width = heads * HEAD_SIZE
    half_size = HEAD_SIZE // 2
    feature_index = jnp.arange(feature_width)
    within = feature_index % HEAD_SIZE
    pair_index = within % half_size
    frequency = 1.0 / THETA ** ((2 * pair_index).astype(jnp.float32) / HEAD_SIZE)
    phases = places.astype(jnp.float32)[:, None] * frequency[None, :]
    head_of = feature_index // HEAD_SIZE
    same_head = head_of[:, None] == head_of[None, :]
    lower_target = within[None, :] < half_size
    from_upper = (within[:, None] == within[None, :] + half_size) & lower_target
    from_lower = (within[:, None] + half_size == within[None, :]) & jnp.logical_not(lower_target)
    swapper = jnp.where(
        same_head & from_upper, -1.0, jnp.where(same_head & from_lower, 1.0, 0.0)
    ).astype(jnp.float32)
    return (jnp.cos(phases), jnp.sin(phases), swapper)


def apply_rotation(values, parts):
    cosine_wide, sine_wide, swapper = parts
    swapped = jnp.dot(values, swapper, precision=HIGHEST)
    return values * cosine_wide + swapped * sine_wide


def inverse_rotation(values, parts):
    cosine_wide, sine_wide, swapper = parts
    swapped = jnp.dot(values, swapper, precision=HIGHEST)
    return values * cosine_wide - swapped * sine_wide


def rms_inverse(values):
    return lax.rsqrt(jnp.mean(values * values, -1, keepdims=True) + EPSILON)


def norm_backward(grad_normed, values, inverse, gain):
    unit_rows = values * inverse
    grad_gain = jnp.sum(grad_normed * unit_rows, 0)
    scaled = grad_normed * gain.astype(jnp.float32)
    grad_values = inverse * (scaled - unit_rows * jnp.mean(scaled * unit_rows, -1, keepdims=True))
    return (grad_values, grad_gain)


def by_group(rows):
    return rows.reshape(128, QUERY_HEADS, HEAD_SIZE).transpose(1, 0, 2).reshape(3, LANES, HEAD_SIZE)


def spread(rows):
    parts = rows.reshape(128, QUERY_HEADS, HEAD_SIZE).transpose(1, 0, 2)
    lo, hi = parts[:, :64], parts[:, 64:]
    zero = jnp.zeros_like(lo)
    top = jnp.concatenate([zero, lo, hi, zero], -1)
    low = jnp.concatenate([hi, zero, zero, zero], -1)
    return jnp.concatenate([top, low], 1).reshape(3, LANES, 256)


def by_token(turned):
    return turned.reshape(3, HEAD_SIZE, 3, 128).transpose(3, 0, 2, 1).reshape(128, MODEL_WIDTH)


def paired(keys, values):
    both = jnp.stack([keys.reshape(128, 3, 64), values.reshape(128, 3, 64)], 2)
    return both.reshape(128, 3, 128).transpose(1, 0, 2)


def layer_forward(hidden, first, gains, flags, source, query_parts, key_parts):
    query_t, key_t, value_t, w_out = jnp.split(first, (576, 768, 960), axis=0)
    inverse_one = rms_inverse(hidden)
    normed_one = (hidden * inverse_one * gains[:MODEL_WIDTH].astype(jnp.float32)).astype(jnp.bfloat16)
    query_rows = apply_rotation(dot_cols(normed_one, query_t), query_parts).astype(jnp.bfloat16)
    key_rows = apply_rotation(dot_cols(normed_one, key_t), key_parts).astype(jnp.bfloat16)
    value_rows = dot_cols(normed_one, value_t).astype(jnp.bfloat16)
    own = paired(key_rows, value_rows)
    queries = spread(query_rows * jnp.bfloat16(HEAD_SIZE ** (-0.5)))
    turned, lse, kv, whole = attention_forward(own, queries, flags, source)
    whole = whole.reshape(4, 1536, MODEL_WIDTH)
    gate_t, up_t, w_down = whole[1], whole[2], whole[3]
    mixed = by_token(turned).astype(jnp.bfloat16)
    middle = hidden + jnp.dot(mixed, w_out, preferred_element_type=jnp.float32)
    inverse_two = rms_inverse(middle)
    normed_two = (middle * inverse_two * gains[MODEL_WIDTH:].astype(jnp.float32)).astype(jnp.bfloat16)
    gate_values = dot_cols(normed_two, gate_t)
    up_values = dot_cols(normed_two, up_t)
    product = (jax.nn.silu(gate_values) * up_values).astype(jnp.bfloat16)
    result = middle + jnp.dot(product, w_down, preferred_element_type=jnp.float32)
    kept = (
        hidden, inverse_one, normed_one, queries, own, kv, turned, lse, mixed,
        middle, inverse_two, normed_two, gate_values, up_values, product,
        (query_t, key_t, value_t, w_out, gate_t, up_t, w_down),
    )
    return result, kept, whole[0]


def layer_backward(grad_result, kept, gains, flags, more, query_parts, key_parts):
    (
        hidden, inverse_one, normed_one, queries, own, kv, turned, lse, mixed,
        middle, inverse_two, normed_two, gate_values, up_values, product,
        (query_t, key_t, value_t, w_out, gate_t, up_t, w_down),
    ) = kept
    grad_down = grad_result.astype(jnp.bfloat16)
    grad_product = dot_cols(grad_down, w_down)
    sigmoid_values = jax.nn.sigmoid(gate_values)
    grad_gate = (
        grad_product * up_values * (sigmoid_values * (1.0 + gate_values * (1.0 - sigmoid_values)))
    ).astype(jnp.bfloat16)
    grad_up = (grad_product * (gate_values * sigmoid_values)).astype(jnp.bfloat16)
    grad_normed_two = jnp.dot(grad_gate, gate_t, preferred_element_type=jnp.float32) + jnp.dot(
        grad_up, up_t, preferred_element_type=jnp.float32
    )
    grad_middle, grad_gain_two = norm_backward(
        grad_normed_two, middle, inverse_two, gains[MODEL_WIDTH:]
    )
    grad_middle = grad_middle + grad_result
    grad_branch = grad_middle.astype(jnp.bfloat16)
    grad_mixed = dot_cols(grad_branch, w_out).astype(jnp.bfloat16)
    inner = jnp.sum(
        turned * by_group(grad_mixed).astype(jnp.float32).transpose(0, 2, 1), 1, keepdims=True
    )
    inner = jnp.broadcast_to(inner, (3, 8, LANES))
    arrays = (grad_gate, grad_up, product, normed_two, grad_down)
    shape = {1: ((0, 3),), 2: ((1, 3),), 3: ((2, 4),)}
    if more is not None:
        arrays = arrays + more
        shape[0] = ((5, 9), (6, 9), (7, 9), (8, 10))
    dq, sums, owned = attention_backward(
        3 if more is None else 4, shape,
        kv, own, queries, spread(grad_mixed), lse, inner, flags, arrays,
    )
    sums = sums.transpose(1, 0, 2).reshape(128, 3, 2, 64)
    key_sums = sums[:, :, 0].reshape(128, 192)
    value_sums = sums[:, :, 1].reshape(128, 192)
    grad_query = by_token(dq) * HEAD_SIZE ** (-0.5)
    grad_query = inverse_rotation(grad_query, query_parts).astype(jnp.bfloat16)
    key_gradient = inverse_rotation(key_sums, key_parts).astype(jnp.bfloat16)
    value_gradient = value_sums.astype(jnp.bfloat16)
    grad_normed_one = (
        jnp.dot(grad_query, query_t, preferred_element_type=jnp.float32)
        + jnp.dot(key_gradient, key_t, preferred_element_type=jnp.float32)
        + jnp.dot(value_gradient, value_t, preferred_element_type=jnp.float32)
    )
    grad_hidden, grad_gain_one = norm_backward(
        grad_normed_one, hidden, inverse_one, gains[:MODEL_WIDTH]
    )
    grad_hidden = grad_hidden + grad_middle
    gain_terms = jnp.concatenate([grad_gain_one, grad_gain_two, jnp.zeros(896, jnp.float32)])
    left = (grad_query, key_gradient, value_gradient, mixed, normed_one, grad_branch)
    return grad_hidden, owned, left, gain_terms.reshape(16, 128)


def on_device(hidden_in, positions, params, gains, cotangent):
    places = positions[0]
    block = places[0] // 64
    turn = block >= 32
    block = jnp.minimum(block, 63 - block)

    def lo_first(rows):
        return jnp.where(turn, jnp.concatenate([rows[64:], rows[:64]], 0), rows)

    places = lo_first(places)
    extra = jnp.concatenate(
        [jnp.pad(gains, ((0, 0), (0, 119))), jnp.full((14, 128), block, jnp.bfloat16)], 0
    )
    at_front = lax.axis_index("fsdp") == 0
    sources = (jnp.where(at_front, params[1], params[0]), params[1])
    first, extras = gather_first(params[0], extra)
    first = first.reshape(1536, MODEL_WIDTH)
    extras = extras.reshape(128, 16, 128)
    gain_rows = [extras[:, layer, :9].reshape(-1) for layer in range(LAYERS)]
    blocks = lax.dynamic_slice(
        extras[:, 2, 0], (lax.axis_index("fsdp") * 32,), (32,)
    ).astype(jnp.int32)
    flags = jnp.concatenate([blocks < block, jnp.full((8,), True)]).astype(jnp.float32)
    flags = (
        jnp.broadcast_to(flags[:, None], (40, LANES)),
        jnp.broadcast_to(flags[:, None, None], (40, 8, 128)),
    )
    query_parts = rotation_parts(places, QUERY_HEADS)
    key_parts = rotation_parts(places, KEY_VALUE_HEADS)
    hidden = lo_first(hidden_in[0]).astype(jnp.float32)
    kept = []
    for layer in range(LAYERS):
        hidden, state, first = layer_forward(
            hidden, first, gain_rows[layer], flags, sources[layer], query_parts, key_parts
        )
        kept.append(state)
    output_rows = lo_first(hidden.astype(jnp.bfloat16))
    grad_hidden = lo_first(cotangent[0]).astype(jnp.float32)
    owned = [None] * LAYERS
    gain_terms = [None] * LAYERS
    left = None
    for layer in reversed(range(LAYERS)):
        grad_hidden, owned[layer], left, gain_terms[layer] = layer_backward(
            grad_hidden, kept[layer], gain_rows[layer], flags, left, query_parts, key_parts
        )
    last, gain_sums = reduce_last(left, jnp.concatenate(gain_terms, 0))
    owned = [jnp.where(at_front, last, owned[0]), jnp.where(at_front, owned[0], owned[1])]
    index = lax.axis_index("fsdp") * 32 + lax.axis_index("ctx")
    owned_gains = lax.dynamic_slice(gain_sums.reshape(LAYERS, 2048), (0, index * 9), (LAYERS, 9))
    return (
        output_rows[None],
        lo_first(grad_hidden)[None],
        jnp.stack(owned),
        owned_gains,
    )


def solution(mesh):
    return jax.shard_map(
        on_device,
        mesh=mesh,
        in_specs=(
            P("fsdp", "ctx", None),
            P("fsdp", "ctx"),
            P(None, ("fsdp", "ctx"), None),
            P(None, ("fsdp", "ctx")),
            P("fsdp", "ctx", None),
        ),
        out_specs=(
            P("fsdp", "ctx", None),
            P("fsdp", "ctx", None),
            P(None, ("fsdp", "ctx"), None),
            P(None, ("fsdp", "ctx")),
        ),
        check_vma=False,
    )
```

```python
import functools

import jax
import jax.numpy as jnp
from jax import lax
from jax.experimental import pallas as pl
from jax.experimental.pallas import tpu as pltpu
from jax.sharding import PartitionSpec as P

MODEL_WIDTH = 576
FEEDFORWARD_SIZE = 1536
QUERY_HEADS = 9
KEY_VALUE_HEADS = 3
HEAD_SIZE = 64
LAYERS = 2

EPSILON = 1e-05
THETA = 100000.0
MASKED = -1e30
MESH = pl.DeviceIdType.MESH
RING = 4


def place():
    t = lax.axis_index("ctx")
    return (lax.axis_index("fsdp"), t // 8, (t // 2) % 4, t % 2)


def device(y, x, z, c):
    return (y, x * 8 + z * 2 + c)


def moved(me, axis, step):
    other = list(me)
    other[axis] = (me[axis] + step) % RING
    return tuple(other)


def sibling(me):
    return (me[0], me[1], me[2], 1 - me[3])


def greet(peers):
    barrier = pltpu.get_barrier_semaphore()
    for peer in peers:
        pl.semaphore_signal(barrier, inc=1, device_id=device(*peer), device_id_type=MESH)
    pl.semaphore_wait(barrier, len(peers))


TILES = 33
CHUNK = 11
LANES = 384


def head_lanes():
    return lax.broadcasted_iota(jnp.int32, (1, LANES), 1) % 128 >= 64


def roll_heads(rows):
    return jnp.concatenate(
        [pltpu.roll(rows[:, 128 * h : 128 * h + 128], 64, 1) for h in range(3)], axis=1
    )


def pack_tile(lo, hi, keep_lo, use_a, use_b):
    lo = lo.astype(jnp.float32)
    hi = hi.astype(jnp.float32)
    zero = jnp.zeros_like(lo)
    a = jnp.where(use_a, lo, zero)
    b = jnp.where(use_b, hi, zero)
    if not keep_lo:
        lo = zero
    left = lax.broadcasted_iota(jnp.int32, (64, 128), 1) < 64
    keys = [jnp.where(left, lo, pltpu.roll(a, 64, 1)), jnp.where(left, b, zero)]
    values = [jnp.where(left, pltpu.roll(lo, 64, 1), a), jnp.where(left, pltpu.roll(b, 64, 1), zero)]
    return (
        jnp.concatenate(keys, axis=1).astype(jnp.bfloat16),
        jnp.concatenate(values, axis=1).astype(jnp.bfloat16),
    )


def pack_all(g, kv, own, tall, keys, values):
    def one(t, carry):
        at = kv[g, t // 8, (t // 2) % 4, t % 2]
        use_a = jnp.broadcast_to(tall[t][:1] > 0.5, (64, 128))
        k, v = pack_tile(at[:64], at[64:], True, use_a, jnp.logical_not(use_a))
        spot = pl.ds(pl.multiple_of(t * 64, 64), 64)
        keys[spot] = k
        values[spot] = v
        return carry

    lax.fori_loop(0, TILES - 1, one, 0)
    yes = jnp.full((64, 128), True)
    k, v = pack_tile(own[g, :64], own[g, 64:], False, yes, jnp.logical_not(yes))
    keys[pl.ds(64 * (TILES - 1), 64)] = k
    values[pl.ds(64 * (TILES - 1), 64)] = v


def dot_cols(left, right):
    return lax.dot_general(
        left, right, (((1,), (1,)), ((), ())), preferred_element_type=jnp.float32
    )


def dot_rows(left, right):
    return lax.dot_general(
        left, right, (((0,), (0,)), ((), ())), preferred_element_type=jnp.float32
    )


def score_all(keys, queries, scores):
    for c in range(TILES // CHUNK):
        rows = pl.ds(64 * CHUNK * c, 64 * CHUNK)
        scores[rows] = dot_cols(keys[rows], queries)
    at = lax.broadcasted_iota(jnp.int32, (64, LANES), 0)
    lane = lax.broadcasted_iota(jnp.int32, (64, LANES), 1) % 128
    causal = jnp.logical_and(lane < 64, at <= lane)
    mine = pl.ds(pl.multiple_of(lax.axis_index("ctx") * 64, 64), 64)
    scores[mine] = jnp.where(jnp.logical_or(lane >= 64, causal), scores[mine], MASKED)
    last = pl.ds(64 * (TILES - 1), 64)
    scores[last] = jnp.where(causal, scores[last], MASKED)


def tile_rows(flags, row):
    crossed = jnp.where(head_lanes(), row, roll_heads(row))
    return jnp.where(flags[...] > 0.5, row, crossed)


def joined(rows, flags, merge, empty):
    straight = jnp.where(jnp.logical_or(head_lanes(), flags[...] > 0.5), rows, empty)
    crossed = jnp.where(jnp.logical_or(head_lanes(), flags[...] > 0.5), empty, rows)
    down = jnp.max if merge is jnp.maximum else jnp.sum
    one = down(straight, axis=0, keepdims=True)
    other = roll_heads(down(crossed, axis=0, keepdims=True))
    return merge(one, other)


def fold_lanes(product):
    return jnp.where(
        head_lanes(), product[:64] + roll_heads(product[128:192]), product[64:128]
    )


def attend_group(
    g, own, kv, queries, flags, tall, out, lse, keys, values, scores, rows, between
):
    pack_all(g, kv, own, tall, keys, values)
    score_all(keys, queries[g], scores)
    between()
    rows[...] = jnp.full(rows.shape, MASKED, jnp.float32)

    for t in range(TILES):
        rows[pl.ds(t, 1)] = jnp.max(scores[pl.ds(64 * t, 64)], axis=0, keepdims=True)
    top = joined(rows[...], flags, jnp.maximum, MASKED)
    rows[...] = tile_rows(flags, top)
    total = jnp.zeros((256, LANES), jnp.float32)
    sums = []
    for c in range(TILES // CHUNK):
        parts = []
        for i in range(CHUNK):
            t = c * CHUNK + i
            raised = jnp.exp(scores[pl.ds(64 * t, 64)] - rows[pl.ds(t, 1)])
            sums.append(jnp.sum(raised, axis=0, keepdims=True))
            parts.append(raised.astype(jnp.bfloat16))
        spot = pl.ds(64 * CHUNK * c, 64 * CHUNK)
        total = total + dot_rows(values[spot], jnp.concatenate(parts, axis=0))
    rows[...] = jnp.zeros(rows.shape, jnp.float32)
    for t in range(TILES):
        rows[pl.ds(t, 1)] = sums[t]
    amount = joined(rows[...], flags, jnp.add, 0.0)
    out[g] = fold_lanes(total) / amount
    lse[g] = jnp.broadcast_to(top + jnp.log(amount), (8, LANES))


def attend_back_group(
    g, me, kv, own, queries, grads, lse, inner, flags, tall, dq, dkv,
    keys, values, scores, lse_rows, inner_rows,
):
    pack_all(g, kv, own, tall, keys, values)
    score_all(keys, queries[g], scores)
    lse_rows[...] = tile_rows(flags, lse[g][:1])
    inner_rows[...] = tile_rows(flags, inner[g][:1])
    total = jnp.zeros((256, LANES), jnp.float32)
    for c in range(TILES // CHUNK):
        spot = pl.ds(64 * CHUNK * c, 64 * CHUNK)
        grad_probs = dot_cols(values[spot], grads[g])
        probs, rest = [], []
        for i in range(CHUNK):
            t = c * CHUNK + i
            p = jnp.exp(scores[pl.ds(64 * t, 64)] - lse_rows[pl.ds(t, 1)])
            probs.append(p.astype(jnp.bfloat16))
            rest.append(
                (p * (grad_probs[64 * i : 64 * i + 64] - inner_rows[pl.ds(t, 1)])).astype(jnp.bfloat16)
            )
        probs = jnp.concatenate(probs, axis=0)
        rest = jnp.concatenate(rest, axis=0)
        total = total + dot_rows(keys[spot], rest)
        to_keys = jnp.dot(rest, queries[g], preferred_element_type=jnp.float32)
        to_values = jnp.dot(probs, grads[g], preferred_element_type=jnp.float32)
        left = lax.broadcasted_iota(jnp.int32, (64, 128), 1) < 64
        for i in range(CHUNK):
            t = c * CHUNK + i
            k0 = to_keys[64 * i : 64 * i + 64, :128]
            k1 = to_keys[64 * i : 64 * i + 64, 128:]
            v0 = to_values[64 * i : 64 * i + 64, :128]
            v1 = to_values[64 * i : 64 * i + 64, 128:]
            a = jnp.where(left, pltpu.roll(k0, 64, 1), v0)
            if t < TILES - 1:
                use_a = jnp.broadcast_to(tall[t][:1] > 0.5, (64, 128))
                lo = jnp.where(left, k0, pltpu.roll(v0, 64, 1)) + jnp.where(use_a, a, 0.0)
                hi = jnp.where(use_a, 0.0, jnp.where(left, k1, pltpu.roll(v1, 64, 1)))
                dkv[g, t // 8, (t // 2) % 4, t % 2, :64] = lo.astype(jnp.bfloat16)
                dkv[g, t // 8, (t // 2) % 4, t % 2, 64:] = hi.astype(jnp.bfloat16)
            else:
                spot = (g, me[1], me[2], me[3], pl.ds(0, 64))
                dkv[spot] = (dkv[spot].astype(jnp.float32) + a).astype(jnp.bfloat16)
    dq[g] = fold_lanes(total)


def weight_gather(me, source, whole, sends, recvs, swap_sends, swap_recvs, own_sem):
    def region(k, phase, at, core):
        index = [at[0], at[1], at[2]]
        for i in range(phase):
            index[(k + i) % 3] = slice(None)
        return whole.at[tuple(index) + (core, pl.ds(16 * k, 16))]

    def copy(src, dst, k, phase, s):
        return pltpu.make_async_remote_copy(
            src_ref=src, dst_ref=dst,
            send_sem=sends.at[k, phase, s - 1], recv_sem=recvs.at[k, phase, s - 1],
            device_id=device(*moved(me, (k + phase) % 3, s)), device_id_type=MESH)

    def send(k, phase, s):
        spot = region(k, phase, me, me[3])
        return copy(spot if phase else source.at[pl.ds(16 * k, 16)], spot, k, phase, s)

    def landed(k, phase, s):
        spot = region(k, phase, moved(me, (k + phase) % 3, -s), me[3])
        return copy(spot, spot, k, phase, s)

    def swap(k, s, core):
        spot = region(k, 2, moved(me, (k + 2) % 3, -s), core)
        return pltpu.make_async_remote_copy(
            src_ref=spot, dst_ref=spot,
            send_sem=swap_sends.at[k, s], recv_sem=swap_recvs.at[k, s],
            device_id=device(*sibling(me)), device_id_type=MESH)

    def begin():
        own = pltpu.make_async_copy(source, whole.at[me], own_sem)
        own.start()
        for k in range(3):
            for s in (2, 1, 3):
                send(k, 0, s).start()
        own.wait()

    def forward(phase):
        for k in range(3):
            for s in (1, 3, 2):
                landed(k, phase - 1, s).wait_recv()
            for s in (2, 1, 3):
                send(k, phase, s).start()
            if phase == 2:
                swap(k, 0, me[3]).start()

    def exchange():
        for s in (1, 3, 2):
            for k in range(3):
                landed(k, 2, s).wait_recv()
                swap(k, s, me[3]).start()

    def finish():
        for k in range(3):
            for phase in range(3):
                for s in (1, 2, 3):
                    send(k, phase, s).wait_send()
            for s in range(4):
                swap(k, s, me[3]).wait_send()
                swap(k, s, 1 - me[3]).wait_recv()

    return begin, forward, exchange, finish


WEIGHT_GATHER_SEMS = [
    pltpu.SemaphoreType.DMA((3, 3, 3)),
    pltpu.SemaphoreType.DMA((3, 3, 3)),
    pltpu.SemaphoreType.DMA((3, 4)),
    pltpu.SemaphoreType.DMA((3, 4)),
    pltpu.SemaphoreType.DMA,
]
WHOLE = jax.ShapeDtypeStruct((4, 4, 4, 2, 48, MODEL_WIDTH), jnp.bfloat16)
ALL_PEERS = tuple((a, s) for a in range(3) for s in (1, 2, 3))


def greet_all(me):
    greet([moved(me, a, s) for a, s in ALL_PEERS] + [sibling(me)])


def row_gather(me, own, kv, sends, recvs, swap_sends, swap_recvs, own_sems):
    def region(g, k, phase, at, core):
        index = [at[1], at[2]]
        if phase >= 1:
            index[1 - k] = slice(None)
        return kv.at[(g,) + tuple(index) + (core, pl.ds(64 * k, 64))]

    def axis_of(k, phase):
        return 1 + (1 - k + phase) % 2

    def copy(src, dst, g, k, phase, s):
        return pltpu.make_async_remote_copy(
            src_ref=src, dst_ref=dst,
            send_sem=sends.at[g, k, phase, s - 1], recv_sem=recvs.at[g, k, phase, s - 1],
            device_id=device(*moved(me, axis_of(k, phase), s)), device_id_type=MESH)

    def send(g, k, phase, s):
        spot = region(g, k, phase, me, me[3])
        return copy(spot if phase else own.at[g, pl.ds(64 * k, 64)], spot, g, k, phase, s)

    def landed(g, k, phase, s):
        spot = region(g, k, phase, moved(me, axis_of(k, phase), -s), me[3])
        return copy(spot, spot, g, k, phase, s)

    def swap(g, k, s, core):
        spot = region(g, k, 1, moved(me, axis_of(k, 1), -s), core)
        return pltpu.make_async_remote_copy(
            src_ref=spot, dst_ref=spot,
            send_sem=swap_sends.at[g, k, s], recv_sem=swap_recvs.at[g, k, s],
            device_id=device(*sibling(me)), device_id_type=MESH)

    def keep(g):
        return pltpu.make_async_copy(own.at[g], kv.at[g, me[1], me[2], me[3]], own_sems.at[g])

    def begin(g):
        for s in (2, 1, 3):
            for k in range(2):
                send(g, k, 0, s).start()
        keep(g).start()

    def forward(g):
        keep(g).wait()
        for k in range(2):
            for s in (1, 3, 2):
                landed(g, k, 0, s).wait_recv()
            for s in (2, 1, 3):
                send(g, k, 1, s).start()
            swap(g, k, 0, me[3]).start()

    def arrive(g):
        for s in (1, 3, 2):
            for k in range(2):
                landed(g, k, 1, s).wait_recv()
                swap(g, k, s, me[3]).start()
        for k in range(2):
            for s in range(4):
                swap(g, k, s, 1 - me[3]).wait_recv()

    def finish(g):
        for k in range(2):
            for phase in range(2):
                for s in (1, 2, 3):
                    send(g, k, phase, s).wait_send()
            for s in range(4):
                swap(g, k, s, me[3]).wait_send()

    return begin, forward, arrive, finish


def weight_reduce(
    me, out, grads, halves, landed_a, sum_a, landed_b, sum_b, landed_c,
    swap_sends, swap_recvs, sends, recvs,
):
    axes = ((2, 1, 0), (0, 2, 1), (1, 0, 2))

    def swap(y):
        return pltpu.make_async_remote_copy(
            src_ref=grads.at[y, :, :, 1 - me[3]], dst_ref=halves.at[y],
            send_sem=swap_sends.at[y], recv_sem=swap_recvs.at[y],
            device_id=device(*sibling(me)), device_id_type=MESH)

    def copy(stage, src, dst, k, s, peer):
        return pltpu.make_async_remote_copy(
            src_ref=src, dst_ref=dst,
            send_sem=sends.at[stage, k, s - 1], recv_sem=recvs.at[stage, k, s - 1],
            device_id=device(*peer), device_id_type=MESH)

    def send(stage, k, s):
        axis = axes[k][stage]
        peer = moved(me, axis, s)
        if stage == 0:
            index = [slice(None)] * 3
            index[axis] = peer[axis]
            return copy(0, halves.at[tuple(index) + (pl.ds(16 * k, 16),)], landed_a.at[k, s - 1], k, s, peer)
        if stage == 1:
            index = [slice(None)] * 2
            index[sorted(axes[k][1:]).index(axis)] = peer[axis]
            return copy(1, sum_a.at[(k,) + tuple(index)], landed_b.at[k, s - 1], k, s, peer)
        return copy(2, sum_b.at[k, peer[axis]], landed_c.at[k, s - 1], k, s, peer)

    def halve(y):
        swap(y).wait_recv()
        for x in range(4):
            for z in range(4):
                halves[y, x, z] = (
                    grads[y, x, z, me[3]].astype(jnp.float32) + halves[y, x, z].astype(jnp.float32)
                ).astype(jnp.bfloat16)

    def begin():
        for k in range(3):
            for s in (2, 1, 3):
                send(0, k, s).start()

    def second():
        for k in range(3):
            for s in (1, 3, 2):
                send(0, k, s).wait_recv()
            axis = axes[k][0]
            for i in range(4):
                for j in range(4):
                    at = [i, j]
                    at.insert(axis, me[axis])
                    total = halves[tuple(at) + (pl.ds(16 * k, 16),)].astype(jnp.float32)
                    for s in range(3):
                        total = total + landed_a[k, s, i, j].astype(jnp.float32)
                    sum_a[k, i, j] = total.astype(jnp.bfloat16)
            for s in (2, 1, 3):
                send(1, k, s).start()

    def third():
        for k in range(3):
            for s in (1, 3, 2):
                send(1, k, s).wait_recv()
            rest = sorted(axes[k][1:])
            for i in range(4):
                at = [i, i]
                at[rest.index(axes[k][1])] = me[axes[k][1]]
                total = sum_a[(k,) + tuple(at)].astype(jnp.float32)
                for s in range(3):
                    total = total + landed_b[k, s, i].astype(jnp.float32)
                sum_b[k, i] = total.astype(jnp.bfloat16)
            for s in (2, 1, 3):
                send(2, k, s).start()

    def finish(planes):
        for k in range(3):
            for s in (1, 3, 2):
                send(2, k, s).wait_recv()
            total = sum_b[k, me[axes[k][2]]].astype(jnp.float32)
            for s in range(3):
                total = total + landed_c[k, s].astype(jnp.float32)
            out[pl.ds(16 * k, 16)] = total
        for y in planes:
            swap(y).wait_send()
        for stage in range(3):
            for k in range(3):
                for s in (1, 2, 3):
                    send(stage, k, s).wait_send()

    return swap, halve, begin, second, third, finish


def weight_reduce_scratch():
    bf, w = jnp.bfloat16, MODEL_WIDTH
    return [
        pltpu.VMEM((4, 4, 4, 2, 48, w), bf),
        pltpu.VMEM((4, 4, 4, 48, w), bf),
        pltpu.VMEM((3, 3, 4, 4, 16, w), bf),
        pltpu.VMEM((3, 4, 4, 16, w), bf),
        pltpu.VMEM((3, 3, 4, 16, w), bf),
        pltpu.VMEM((3, 4, 16, w), bf),
        pltpu.VMEM((3, 3, 16, w), bf),
        pltpu.SemaphoreType.DMA((4,)),
        pltpu.SemaphoreType.DMA((4,)),
        pltpu.SemaphoreType.DMA((3, 3, 3)),
        pltpu.SemaphoreType.DMA((3, 3, 3)),
    ]


def row_reduce(
    me, terms, out, halves, landed_a, sum_a, landed_b, swap_sends, swap_recvs, sends, recvs
):
    axes = ((2, 1), (1, 2))

    def swap(g):
        return pltpu.make_async_remote_copy(
            src_ref=terms.at[g, :, :, 1 - me[3]], dst_ref=halves.at[g],
            send_sem=swap_sends.at[g], recv_sem=swap_recvs.at[g],
            device_id=device(*sibling(me)), device_id_type=MESH)

    def send(stage, g, k, s):
        axis = axes[k][stage]
        peer = moved(me, axis, s)
        if stage == 0:
            index = [slice(None)] * 2
            index[axis - 1] = peer[axis]
            src = halves.at[(g,) + tuple(index) + (pl.ds(64 * k, 64),)]
            dst = landed_a.at[g, k, s - 1]
        else:
            src = sum_a.at[g, k, peer[axis]]
            dst = landed_b.at[g, k, s - 1]
        return pltpu.make_async_remote_copy(
            src_ref=src, dst_ref=dst,
            send_sem=sends.at[stage, g, k, s - 1], recv_sem=recvs.at[stage, g, k, s - 1],
            device_id=device(*peer), device_id_type=MESH)

    def begin(g):
        swap(g).start()

    def second(g):
        swap(g).wait_recv()
        for x in range(4):
            for z in range(4):
                halves[g, x, z] = (
                    terms[g, x, z, me[3]].astype(jnp.float32) + halves[g, x, z].astype(jnp.float32)
                ).astype(jnp.bfloat16)
        for s in (2, 1, 3):
            for k in range(2):
                send(0, g, k, s).start()

    def third(g):
        for k in range(2):
            for s in (1, 3, 2):
                send(0, g, k, s).wait_recv()
            axis = axes[k][0]
            for i in range(4):
                at = [i]
                at.insert(axis - 1, me[axis])
                total = halves[(g,) + tuple(at) + (pl.ds(64 * k, 64),)].astype(jnp.float32)
                for s in range(3):
                    total = total + landed_a[g, k, s, i].astype(jnp.float32)
                sum_a[g, k, i] = total.astype(jnp.bfloat16)
            for s in (2, 1, 3):
                send(1, g, k, s).start()

    def finish(g):
        for k in range(2):
            for s in (1, 3, 2):
                send(1, g, k, s).wait_recv()
            total = sum_a[g, k, me[axes[k][1]]].astype(jnp.float32)
            for s in range(3):
                total = total + landed_b[g, k, s].astype(jnp.float32)
            out[g, pl.ds(64 * k, 64)] = total

    def drain(g):
        swap(g).wait_send()
        for stage in range(2):
            for k in range(2):
                for s in (1, 2, 3):
                    send(stage, g, k, s).wait_send()

    return begin, second, third, finish, drain


def row_reduce_scratch():
    bf = jnp.bfloat16
    return [
        pltpu.VMEM((3, 4, 4, 128, 128), bf),
        pltpu.VMEM((3, 2, 3, 4, 64, 128), bf),
        pltpu.VMEM((3, 2, 4, 64, 128), bf),
        pltpu.VMEM((3, 2, 3, 64, 128), bf),
        pltpu.SemaphoreType.DMA((3,)),
        pltpu.SemaphoreType.DMA((3,)),
        pltpu.SemaphoreType.DMA((2, 3, 2, 3)),
        pltpu.SemaphoreType.DMA((2, 3, 2, 3)),
    ]


def left_lanes():
    return lax.broadcasted_iota(jnp.int32, (128, 128), 1) < 64


def swapped(tile):
    low = lax.broadcasted_iota(jnp.int32, tile.shape, 1) % 64 < 32
    return jnp.where(low, pltpu.roll(tile, 96, 1), pltpu.roll(tile, 32, 1))


def spread_tile(spots, tile, j):
    other = pltpu.roll(tile, 64, 1)
    left = left_lanes()
    for i in range(2):
        head = 2 * j + i
        if head >= QUERY_HEADS:
            continue
        a = jnp.where(left, tile if i == 0 else other, 0.0).astype(jnp.bfloat16)
        b = jnp.where(left, 0.0, other if i == 0 else tile).astype(jnp.bfloat16)
        g, at = head // 3, 128 * (head % 3)
        spots[g, at : at + 64, :128] = b[:64]
        spots[g, at : at + 64, 128:] = a[64:]
        spots[g, at + 64 : at + 128, :128] = a[64:]
        spots[g, at + 64 : at + 128, 128:] = jnp.zeros((64, 128), jnp.bfloat16)


def group_weights(first, g):
    return jnp.concatenate(
        [first[0, 576 + 64 * g : 640 + 64 * g], first[0, 768 + 64 * g : 832 + 64 * g]], axis=0
    )


def inverse_root(values):
    return lax.rsqrt(jnp.mean(values * values, axis=-1, keepdims=True) + EPSILON)


def forward_kernel(
    hidden, planes, gains, cosine, sine, flags, tall, source,
    n1, queries, own, kv, turned, lse, mixed, middle, n2, gate, up, product, result, whole,
    keys, values, scores, rows, first, first_sem, *sems
):
    me = place()
    load = pltpu.make_async_copy(planes.at[pl.ds(0, 1)], first, first_sem)
    load.start()
    greet_all(me)
    load.wait()
    begin, forward, arrive, finish = row_gather(me, own, kv, *sems[:5])
    w_begin, w_forward, w_exchange, w_finish = weight_gather(me, source, whole, *sems[5:])
    left = left_lanes()
    x = hidden[...]
    normed = (x * inverse_root(x) * gains[:1]).astype(jnp.bfloat16)
    n1[...] = normed
    cos, sin = cosine[...], sine[...]
    for g in range(3):
        tile = dot_cols(normed, group_weights(first, g))
        tile = tile * jnp.where(left, cos, 1.0) + swapped(tile) * jnp.where(left, sin, 0.0)
        own[g] = tile.astype(jnp.bfloat16)
        begin(g)
    w_begin()
    for j in range(5):
        tile = dot_cols(normed, first[0, 128 * j : 128 * j + 128])
        tile = (tile * cos + swapped(tile) * sin) * HEAD_SIZE ** (-0.5)
        spread_tile(queries, tile, j)
    for g in range(3):
        forward(g)
    w_forward(1)

    def one(g, carry):
        arrive(g)

        def between():
            @pl.when(g == 0)
            def _():
                w_forward(2)

        attend_group(
            g, own, kv, queries, flags, tall, turned, lse, keys, values, scores, rows, between
        )
        return carry

    lax.fori_loop(0, 3, one, 0)
    for g in range(3):
        for h in range(3):
            mixed[64 * (3 * g + h) : 64 * (3 * g + h) + 64] = turned[
                g, :, 128 * h : 128 * h + 128
            ].astype(jnp.bfloat16)
    mid = x + dot_rows(mixed[...], first[0, 960:1536])
    middle[...] = mid
    normed = (mid * inverse_root(mid) * gains[1:2]).astype(jnp.bfloat16)
    n2[...] = normed
    w_exchange()
    for g in range(3):
        finish(g)
    w_finish()
    total = mid
    for i in range(4):
        part = pl.ds(384 * i, 384)
        gate_values = dot_cols(normed, whole[1, i].reshape(384, MODEL_WIDTH))
        up_values = dot_cols(normed, whole[2, i].reshape(384, MODEL_WIDTH))
        rounded = (gate_values * jax.nn.sigmoid(gate_values) * up_values).astype(jnp.bfloat16)
        gate[:, part] = gate_values
        up[:, part] = up_values
        product[:, part] = rounded
        total = total + jnp.dot(
            rounded, whole[3, i].reshape(384, MODEL_WIDTH), preferred_element_type=jnp.float32
        )
    result[...] = total


ROWS_F32 = jax.ShapeDtypeStruct((128, MODEL_WIDTH), jnp.float32)
ROWS_BF16 = jax.ShapeDtypeStruct((128, MODEL_WIDTH), jnp.bfloat16)
TURNED_BF16 = jax.ShapeDtypeStruct((MODEL_WIDTH, 128), jnp.bfloat16)
WIDE_F32 = jax.ShapeDtypeStruct((128, FEEDFORWARD_SIZE), jnp.float32)
WIDE_BF16 = jax.ShapeDtypeStruct((128, FEEDFORWARD_SIZE), jnp.bfloat16)
VMEM_SPEC = pl.BlockSpec(memory_space=pltpu.VMEM)
HBM_SPEC = pl.BlockSpec(memory_space=pl.ANY)


def layer_forward(hidden, planes, gains, turns, flags, source):
    outs = pl.pallas_call(
        forward_kernel,
        out_shape=(
            ROWS_BF16,
            jax.ShapeDtypeStruct((3, LANES, 256), jnp.bfloat16),
            jax.ShapeDtypeStruct((3, 128, 128), jnp.bfloat16),
            jax.ShapeDtypeStruct((3, 4, 4, 2, 128, 128), jnp.bfloat16),
            jax.ShapeDtypeStruct((3, 64, LANES), jnp.float32),
            jax.ShapeDtypeStruct((3, 8, LANES), jnp.float32),
            TURNED_BF16, ROWS_F32, ROWS_BF16, WIDE_F32, WIDE_F32, WIDE_BF16, ROWS_F32, WHOLE,
        ),
        in_specs=[VMEM_SPEC, HBM_SPEC] + [VMEM_SPEC] * 5 + [HBM_SPEC],
        out_specs=(VMEM_SPEC,) * 14,
        scratch_shapes=[
            pltpu.VMEM((64 * TILES, 256), jnp.bfloat16),
            pltpu.VMEM((64 * TILES, 256), jnp.bfloat16),
            pltpu.VMEM((64 * TILES, LANES), jnp.float32),
            pltpu.VMEM((40, LANES), jnp.float32),
            pltpu.VMEM((1, 1536, MODEL_WIDTH), jnp.bfloat16),
            pltpu.SemaphoreType.DMA,
            pltpu.SemaphoreType.DMA((3, 2, 2, 3)),
            pltpu.SemaphoreType.DMA((3, 2, 2, 3)),
            pltpu.SemaphoreType.DMA((3, 2, 4)),
            pltpu.SemaphoreType.DMA((3, 2, 4)),
            pltpu.SemaphoreType.DMA((3,)),
        ] + WEIGHT_GATHER_SEMS,
        compiler_params=pltpu.CompilerParams(
            collective_id=6 + planes.shape[0], has_side_effects=True, vmem_limit_bytes=48 * 2**20
        ),
        name="layer_forward",
    )(hidden, planes, gains, *turns[:2], *flags, source)
    return outs[:-2], outs[-2], outs[-1].reshape(4, 1536, MODEL_WIDTH)


def norm_back(grad_normed, values, gain):
    inverse = inverse_root(values)
    unit = values * inverse
    grad_gain = jnp.sum(grad_normed * unit, axis=0, keepdims=True)
    scaled = grad_normed * gain
    grad_values = inverse * (
        scaled - unit * jnp.mean(scaled * unit, axis=-1, keepdims=True)
    )
    return grad_values, grad_gain


def products_first(gq, gkv, mixed, n1, gb):
    parts = [jnp.dot(gq[...], n1[...], preferred_element_type=jnp.float32)]
    both = [dot_rows(gkv[g], n1[...]) for g in range(3)]
    parts.append(jnp.concatenate([m[:64] for m in both], axis=0))
    parts.append(jnp.concatenate([m[64:] for m in both], axis=0))
    parts.append(jnp.dot(mixed[...], gb[...], preferred_element_type=jnp.float32))
    return [
        p.astype(jnp.bfloat16).reshape(p.shape[0] // 48, 48, MODEL_WIDTH) for p in parts
    ]


def backward_kernel(extra_count, *refs):
    (
        grad_result, hidden, planes, rest, gains, cosine, sine, cosine_t, sine_t, flags, tall,
        n1, queries, own, kv, turned, lse, mixed, middle, n2, gate, up, product,
    ) = refs[:23]
    more = refs[23 : 23 + extra_count]
    grad_hidden, owned, gq, gkv, gb, gain_terms = refs[23 + extra_count : 29 + extra_count]
    (
        keys, values, scores, lse_rows, inner_rows, dkv, spots, inner, dq, sums, ggate, gup,
        first, whole, load_sems,
    ) = refs[29 + extra_count : 44 + extra_count]
    row_refs = refs[44 + extra_count : 52 + extra_count]
    weight_refs = refs[52 + extra_count :]
    me = place()
    loads = [
        pltpu.make_async_copy(rest.at[pl.ds(1, 3)], whole, load_sems.at[0]),
        pltpu.make_async_copy(planes.at[pl.ds(0, 1)], first, load_sems.at[1]),
    ]
    for load in loads:
        load.start()
    greet_all(me)
    for load in loads:
        load.wait()
    begin, second, third, finish, drain = row_reduce(me, dkv, sums, *row_refs)
    swap, halve, w_begin, w_second, w_third, w_finish = weight_reduce(
        me, owned, *weight_refs
    )
    grads, halves = weight_refs[0], weight_refs[1]
    order = (1, 2, 3, 0) if more else (1, 2, 3)

    gr = grad_result[...]
    gd = gr.astype(jnp.bfloat16)
    normed = n2[...]
    grad_normed = jnp.zeros((128, MODEL_WIDTH), jnp.float32)
    for i in range(4):
        part = pl.ds(384 * i, 384)
        grad_product = dot_cols(gd, whole[2, i])
        gate_values, up_values = gate[:, part], up[:, part]
        s = jax.nn.sigmoid(gate_values)
        gg = (grad_product * up_values * (s * (1.0 + gate_values * (1.0 - s)))).astype(jnp.bfloat16)
        gu = (grad_product * (gate_values * s)).astype(jnp.bfloat16)
        ggate[:, part] = gg
        gup[:, part] = gu
        grad_normed = grad_normed + jnp.dot(
            gg, whole[0, i], preferred_element_type=jnp.float32
        ) + jnp.dot(
            gu, whole[1, i], preferred_element_type=jnp.float32
        )
    for y, source, right in ((1, ggate, normed), (2, gup, normed), (3, product, gd)):
        for i in range(4):
            flat = dot_rows(source[:, 384 * i : 384 * i + 384], right).astype(jnp.bfloat16)
            grads[y, i] = flat.reshape(4, 2, 48, MODEL_WIDTH)
        swap(y).start()
    grad_middle, grad_gain = norm_back(grad_normed, middle[...], gains[1:2])
    gain_terms[...] = jnp.zeros(gain_terms.shape, jnp.float32)
    gain_terms[1:2] = grad_gain
    grad_middle = grad_middle + gr
    branch = grad_middle.astype(jnp.bfloat16)
    gb[...] = branch
    if more:
        at = 0
        for cut in products_first(*more):
            for i in range(cut.shape[0]):
                j = at + i
                grads[0, j // 8, (j // 2) % 4, j % 2] = cut[i]
            at += cut.shape[0]
        swap(0).start()
    for j in range(5):
        width = min(128, 576 - 128 * j)
        tile = dot_cols(branch, first[0, 960 + 128 * j : 960 + 128 * j + width])
        if width < 128:
            tile = jnp.concatenate([tile, jnp.zeros((128, 128 - width), jnp.float32)], axis=1)
        spread_tile(spots, tile, j)
    for g in range(3):
        for h in range(3):
            at = 64 * (3 * g + h)
            grad_turned = dot_cols(first[0, 960 + at : 1024 + at], branch)
            grad_turned = grad_turned.astype(jnp.bfloat16).astype(jnp.float32)
            row = jnp.sum(
                turned[g, :, 128 * h : 128 * h + 128] * grad_turned, axis=0, keepdims=True
            )
            inner[g, :, 128 * h : 128 * h + 128] = jnp.broadcast_to(row, (8, 128))

    def one(g, carry):
        attend_back_group(
            g, me, kv, own, queries, spots, lse, inner, flags, tall, dq, dkv,
            keys, values, scores, lse_rows, inner_rows,
        )
        begin(g)

        @pl.when(g == 0)
        def _():
            for y in order:
                halve(y)
            if not more:
                halves[0] = jnp.zeros(halves.shape[1:], jnp.bfloat16)
            w_begin()

        @pl.when(g == 1)
        def _():
            second(0)

        @pl.when(g == 2)
        def _():
            third(0)
            second(1)
            w_second()

        return carry

    lax.fori_loop(0, 3, one, 0)
    second(2)
    third(1)
    w_third()
    third(2)
    for g in range(3):
        for h in range(3):
            turn = dq[g, :, 128 * h : 128 * h + 128] * HEAD_SIZE ** (-0.5)
            a, b = turn[:32], turn[32:]
            at = 64 * (3 * g + h)
            gq[at : at + 32] = (a * cosine_t[...] + b * sine_t[...]).astype(jnp.bfloat16)
            gq[at + 32 : at + 64] = (b * cosine_t[...] - a * sine_t[...]).astype(jnp.bfloat16)
    grad_normed = dot_rows(gq[...], first[0, :576])
    left = left_lanes()
    cos, sin = jnp.where(left, cosine[...], 1.0), jnp.where(left, sine[...], 0.0)
    w_finish(order)
    for g in range(3):
        finish(g)
        tile = sums[g]
        tile = (tile * cos - swapped(tile) * sin).astype(jnp.bfloat16)
        gkv[g] = tile
        grad_normed = grad_normed + jnp.dot(
            tile, group_weights(first, g), preferred_element_type=jnp.float32
        )
    grad_values, grad_gain = norm_back(grad_normed, hidden[...], gains[:1])
    gain_terms[:1] = grad_gain
    grad_hidden[...] = grad_values + grad_middle
    for g in range(3):
        drain(g)


def layer_backward(collective_id, grad_result, hidden, first, whole, gains, turns, flags, kept, more):
    rest = whole.reshape(4, 4, 384, MODEL_WIDTH)
    return pl.pallas_call(
        functools.partial(backward_kernel, len(more)),
        out_shape=(
            ROWS_F32,
            jax.ShapeDtypeStruct((48, MODEL_WIDTH), jnp.float32),
            TURNED_BF16,
            jax.ShapeDtypeStruct((3, 128, 128), jnp.bfloat16),
            ROWS_BF16,
            jax.ShapeDtypeStruct((8, MODEL_WIDTH), jnp.float32),
        ),
        in_specs=[VMEM_SPEC] * 2 + [HBM_SPEC] * 2 + [VMEM_SPEC] * (19 + len(more)),
        out_specs=(VMEM_SPEC,) * 6,
        scratch_shapes=[
            pltpu.VMEM((64 * TILES, 256), jnp.bfloat16),
            pltpu.VMEM((64 * TILES, 256), jnp.bfloat16),
            pltpu.VMEM((64 * TILES, LANES), jnp.float32),
            pltpu.VMEM((40, LANES), jnp.float32),
            pltpu.VMEM((40, LANES), jnp.float32),
            pltpu.VMEM((3, 4, 4, 2, 128, 128), jnp.bfloat16),
            pltpu.VMEM((3, LANES, 256), jnp.bfloat16),
            pltpu.VMEM((3, 8, LANES), jnp.float32),
            pltpu.VMEM((3, 64, LANES), jnp.float32),
            pltpu.VMEM((3, 128, 128), jnp.float32),
            pltpu.VMEM((128, FEEDFORWARD_SIZE), jnp.bfloat16),
            pltpu.VMEM((128, FEEDFORWARD_SIZE), jnp.bfloat16),
            pltpu.VMEM((1, 1536, MODEL_WIDTH), jnp.bfloat16),
            pltpu.VMEM((3, 4, 384, MODEL_WIDTH), jnp.bfloat16),
            pltpu.SemaphoreType.DMA((2,)),
        ] + row_reduce_scratch() + weight_reduce_scratch(),
        compiler_params=pltpu.CompilerParams(
            collective_id=collective_id, has_side_effects=True, vmem_limit_bytes=60 * 2**20
        ),
        name="layer_backward",
    )(grad_result, hidden, first, rest, gains, *turns, *flags, *kept, *more)


HALF_ROWS = ((0, 32), (32, 16))


def gather_first_kernel(
    source, extra, whole, extras, stage, sends, recvs, swap_sends, swap_recvs,
    y_sends, y_recvs, extra_sends, extra_recvs, own_sems
):
    me = place()
    greet_all(me)

    def y_copy(src, dst, n, s):
        return pltpu.make_async_remote_copy(
            src_ref=src, dst_ref=dst,
            send_sem=y_sends.at[n, s - 1], recv_sem=y_recvs.at[n, s - 1],
            device_id=device(*moved(me, 0, s)), device_id_type=MESH)

    def rows_along_y(s, y):
        return y_copy(source, stage.at[y], 0, s)

    def extra_region(phase, at, core):
        index = [at[0], at[1], at[2]]
        for axis in (0, 2, 1)[:phase]:
            index[axis] = slice(None)
        return extras.at[tuple(index) + (core,)]

    def extra_copy(phase, s, spot, src, peer):
        return pltpu.make_async_remote_copy(
            src_ref=src, dst_ref=spot,
            send_sem=extra_sends.at[phase, s], recv_sem=extra_recvs.at[phase, s],
            device_id=device(*peer), device_id_type=MESH)

    def extra_send(phase, s):
        spot = extra_region(phase, me, me[3])
        return extra_copy(phase, s, spot, spot if phase else extra, moved(me, (0, 2, 1)[phase], s))

    def extra_landed(phase, s):
        axis = (0, 2, 1)[phase]
        spot = extra_region(phase, moved(me, axis, -s), me[3])
        return extra_copy(phase, s, spot, spot, moved(me, axis, s))

    def extra_swap(core):
        spot = extra_region(3, me, core)
        return extra_copy(3, 0, spot, spot, sibling(me))

    def region(k, phase, at, core):
        index = [at[1], at[2]]
        if phase:
            index[k] = slice(None)
        return whole.at[tuple(index) + (core, pl.ds(*HALF_ROWS[k]))]

    def copy(src, dst, k, phase, s):
        return pltpu.make_async_remote_copy(
            src_ref=src, dst_ref=dst,
            send_sem=sends.at[k, phase, s - 1], recv_sem=recvs.at[k, phase, s - 1],
            device_id=device(*moved(me, 1 + (k + phase) % 2, s)), device_id_type=MESH)

    def send(k, phase, s):
        spot = region(k, phase, me, me[3])
        return copy(spot if phase else stage.at[0, pl.ds(*HALF_ROWS[k])], spot, k, phase, s)

    def landed(k, phase, s):
        spot = region(k, phase, moved(me, 1 + (k + phase) % 2, -s), me[3])
        return copy(spot, spot, k, phase, s)

    def swap(k, s, core):
        spot = region(k, 1, moved(me, 1 + (k + 1) % 2, -s), core)
        return pltpu.make_async_remote_copy(
            src_ref=spot, dst_ref=spot,
            send_sem=swap_sends.at[k, s], recv_sem=swap_recvs.at[k, s],
            device_id=device(*sibling(me)), device_id_type=MESH)

    for s in (2, 1, 3):
        rows_along_y(s, me[0]).start()
        extra_send(0, s).start()
    own = pltpu.make_async_copy(source, stage.at[me[0]], own_sems.at[0])
    own_extra = pltpu.make_async_copy(extra, extras.at[me], own_sems.at[1])
    own.start()
    own_extra.start()
    own.wait()
    own_extra.wait()
    for s in (1, 3, 2):
        rows_along_y(s, (me[0] - s) % RING).wait_recv()
    keep = pltpu.make_async_copy(stage.at[0], whole.at[me[1], me[2], me[3]], own_sems.at[2])
    keep.start()
    for k in range(2):
        for s in (2, 1, 3):
            send(k, 0, s).start()
    for s in (1, 3, 2):
        extra_landed(0, s).wait_recv()
    for s in (2, 1, 3):
        extra_send(1, s).start()
    keep.wait()
    for k in range(2):
        for s in (1, 3, 2):
            landed(k, 0, s).wait_recv()
        for s in (2, 1, 3):
            send(k, 1, s).start()
        swap(k, 0, me[3]).start()
    for s in (1, 3, 2):
        extra_landed(1, s).wait_recv()
    for s in (2, 1, 3):
        extra_send(2, s).start()
    for s in (1, 3, 2):
        for k in (1, 0):
            landed(k, 1, s).wait_recv()
            swap(k, s, me[3]).start()
    for s in (1, 3, 2):
        extra_landed(2, s).wait_recv()
    extra_swap(me[3]).start()
    for s in (1, 2, 3):
        rows_along_y(s, me[0]).wait_send()
        for phase in range(3):
            extra_send(phase, s).wait_send()
    for k in range(2):
        for phase in range(2):
            for s in (1, 2, 3):
                send(k, phase, s).wait_send()
        for s in range(4):
            swap(k, s, me[3]).wait_send()
            swap(k, s, 1 - me[3]).wait_recv()
    extra_swap(me[3]).wait_send()
    extra_swap(1 - me[3]).wait_recv()


def gather_first(source, extra):
    hbm = pl.BlockSpec(memory_space=pl.ANY)
    vmem = pl.BlockSpec(memory_space=pltpu.VMEM)
    return pl.pallas_call(
        gather_first_kernel,
        out_shape=(
            jax.ShapeDtypeStruct((4, 4, 2, 48, MODEL_WIDTH), jnp.bfloat16),
            jax.ShapeDtypeStruct((4, 4, 4, 2, 16, 128), jnp.bfloat16),
        ),
        in_specs=[hbm, hbm],
        out_specs=(hbm, hbm),
        scratch_shapes=[
            pltpu.VMEM((4, 48, MODEL_WIDTH), jnp.bfloat16),
            pltpu.SemaphoreType.DMA((2, 2, 3)),
            pltpu.SemaphoreType.DMA((2, 2, 3)),
            pltpu.SemaphoreType.DMA((2, 4)),
            pltpu.SemaphoreType.DMA((2, 4)),
            pltpu.SemaphoreType.DMA((1, 3)),
            pltpu.SemaphoreType.DMA((1, 3)),
            pltpu.SemaphoreType.DMA((4, 4)),
            pltpu.SemaphoreType.DMA((4, 4)),
            pltpu.SemaphoreType.DMA((3,)),
        ],
        compiler_params=pltpu.CompilerParams(collective_id=1, has_side_effects=True),
        name="gather_first",
    )(source, extra)


def reduce_last_kernel(
    gq, gkv, mixed, n1, gb, gains, out, gains_out,
    grads, halves, first, landed_a, sum_a, landed_b, sum_b, landed_y, gain_in, gain_sum,
    swap_sends, swap_recvs, sends, recvs, y_sends, y_recvs, gain_sends, gain_recvs
):
    me = place()
    greet_all(me)

    def gain_copy(stage, s, peer):
        return pltpu.make_async_remote_copy(
            src_ref=gain_sum.at[stage], dst_ref=gain_in.at[stage, s - 1],
            send_sem=gain_sends.at[stage, s - 1], recv_sem=gain_recvs.at[stage, s - 1],
            device_id=device(*peer), device_id_type=MESH)

    def gain_stage(stage, axis):
        total = gain_sum[stage]
        for s in (1,) if stage == 0 else (1, 2, 3):
            gain_copy(stage, s, me if stage else sibling(me)).wait_recv()
            total = total + gain_in[stage, s - 1]
        if axis is None:
            gains_out[...] = total
            return
        gain_sum[stage + 1] = total
        for s in (1, 2, 3):
            gain_copy(stage + 1, s, moved(me, axis, s)).start()

    def swap(x):
        return pltpu.make_async_remote_copy(
            src_ref=grads.at[x, :, 1 - me[3]], dst_ref=halves.at[x],
            send_sem=swap_sends.at[x], recv_sem=swap_recvs.at[x],
            device_id=device(*sibling(me)), device_id_type=MESH)

    def copy(stage, src, dst, k, s):
        return pltpu.make_async_remote_copy(
            src_ref=src, dst_ref=dst,
            send_sem=sends.at[stage, k, s - 1], recv_sem=recvs.at[stage, k, s - 1],
            device_id=device(*moved(me, 1 + (k + 1 + stage) % 2, s)), device_id_type=MESH)

    def send(stage, k, s):
        axis = 1 + (k + 1 + stage) % 2
        to = moved(me, axis, s)[axis]
        rows = pl.ds(*HALF_ROWS[k])
        if stage == 0:
            index = [slice(None)] * 2
            index[axis - 1] = to
            return copy(0, first.at[tuple(index) + (rows,)], landed_a.at[s - 1, :, rows], k, s)
        return copy(1, sum_a.at[to, rows], landed_b.at[s - 1, rows], k, s)

    def y_copy(s):
        return pltpu.make_async_remote_copy(
            src_ref=sum_b, dst_ref=landed_y.at[s - 1],
            send_sem=y_sends.at[s - 1], recv_sem=y_recvs.at[s - 1],
            device_id=device(*moved(me, 0, s)), device_id_type=MESH)

    gain_sum[0] = gains[...]
    gain_copy(0, 1, sibling(me)).start()
    at = 0
    for cut in products_first(gq, gkv, mixed, n1, gb):
        amount = cut.shape[0]
        for i in range(amount):
            j = at + i
            grads[j // 8, (j // 2) % 4, j % 2] = cut[i]
            if j % 8 == 7:
                swap(j // 8).start()
        at += amount
    gain_stage(0, 2)
    for x in range(4):
        swap(x).wait_recv()
        for z in range(4):
            first[x, z] = (
                grads[x, z, me[3]].astype(jnp.float32) + halves[x, z].astype(jnp.float32)
            ).astype(jnp.bfloat16)
    for k in range(2):
        for s in (2, 1, 3):
            send(0, k, s).start()
    gain_stage(1, 1)
    for k in (1, 0):
        rows = pl.ds(*HALF_ROWS[k])
        for s in (1, 3, 2):
            send(0, k, s).wait_recv()
        axis = 1 + (k + 1) % 2
        for i in range(4):
            spot = [i]
            spot.insert(axis - 1, me[axis])
            total = first[tuple(spot) + (rows,)].astype(jnp.float32)
            for s in range(3):
                total = total + landed_a[s, i, rows].astype(jnp.float32)
            sum_a[i, rows] = total.astype(jnp.bfloat16)
        for s in (2, 1, 3):
            send(1, k, s).start()
    gain_stage(2, 0)
    for k in (1, 0):
        rows = pl.ds(*HALF_ROWS[k])
        for s in (1, 3, 2):
            send(1, k, s).wait_recv()
        total = sum_a[me[1 + k % 2], rows].astype(jnp.float32)
        for s in range(3):
            total = total + landed_b[s, rows].astype(jnp.float32)
        sum_b[rows] = total.astype(jnp.bfloat16)
    for s in (2, 1, 3):
        y_copy(s).start()
    gain_stage(3, None)
    total = sum_b[...].astype(jnp.float32)
    for s in (1, 3, 2):
        y_copy(s).wait_recv()
        total = total + landed_y[s - 1].astype(jnp.float32)
    out[...] = total
    for x in range(4):
        swap(x).wait_send()
    for stage in range(2):
        for k in range(2):
            for s in (1, 2, 3):
                send(stage, k, s).wait_send()
    gain_copy(0, 1, sibling(me)).wait_send()
    for s in (1, 2, 3):
        y_copy(s).wait_send()
        for stage, axis in ((1, 2), (2, 1), (3, 0)):
            gain_copy(stage, s, moved(me, axis, s)).wait_send()


def reduce_last(arrays, gains):
    bf, w = jnp.bfloat16, MODEL_WIDTH
    vmem = pl.BlockSpec(memory_space=pltpu.VMEM)
    rows = gains.shape[0]
    return pl.pallas_call(
        reduce_last_kernel,
        out_shape=(
            jax.ShapeDtypeStruct((48, w), jnp.float32),
            jax.ShapeDtypeStruct(gains.shape, jnp.float32),
        ),
        in_specs=[vmem] * 6,
        out_specs=(vmem, vmem),
        scratch_shapes=[
            pltpu.VMEM((4, 4, 2, 48, w), bf),
            pltpu.VMEM((4, 4, 48, w), bf),
            pltpu.VMEM((4, 4, 48, w), bf),
            pltpu.VMEM((3, 4, 48, w), bf),
            pltpu.VMEM((4, 48, w), bf),
            pltpu.VMEM((3, 48, w), bf),
            pltpu.VMEM((48, w), bf),
            pltpu.VMEM((3, 48, w), bf),
            pltpu.VMEM((4, 3, rows, w), jnp.float32),
            pltpu.VMEM((4, rows, w), jnp.float32),
            pltpu.SemaphoreType.DMA((4,)),
            pltpu.SemaphoreType.DMA((4,)),
            pltpu.SemaphoreType.DMA((2, 2, 3)),
            pltpu.SemaphoreType.DMA((2, 2, 3)),
            pltpu.SemaphoreType.DMA((3,)),
            pltpu.SemaphoreType.DMA((3,)),
            pltpu.SemaphoreType.DMA((4, 3)),
            pltpu.SemaphoreType.DMA((4, 3)),
        ],
        compiler_params=pltpu.CompilerParams(
            collective_id=5, has_side_effects=True, vmem_limit_bytes=32 * 2**20
        ),
        name="reduce_last",
    )(*arrays, gains)


def turn_tables(places):
    half = HEAD_SIZE // 2
    frequency = 1.0 / THETA ** (2 * jnp.arange(half).astype(jnp.float32) / HEAD_SIZE)
    phases = places.astype(jnp.float32)[:, None] * frequency[None, :]
    cos, sin = jnp.cos(phases), jnp.sin(phases)
    return (
        jnp.concatenate([cos] * 4, 1), jnp.concatenate([-sin, sin] * 2, 1), cos.T, sin.T,
    )


def on_device(hidden_in, positions, params, gains, cotangent):
    places = positions[0]
    block = places[0] // 64
    turn = block >= 32
    block = jnp.minimum(block, 63 - block)

    def lo_first(rows):
        return jnp.where(turn, jnp.concatenate([rows[64:], rows[:64]], 0), rows)

    extra = jnp.concatenate(
        [jnp.pad(gains, ((0, 0), (0, 119))), jnp.full((14, 128), block, jnp.bfloat16)], 0
    )
    at_front = lax.axis_index("fsdp") == 0
    sources = (jnp.where(at_front, params[1], params[0]), params[1])
    first, extras = gather_first(params[0], extra)
    turns = turn_tables(lo_first(places))
    firsts = [first.reshape(1, 1536, MODEL_WIDTH)]
    extras = extras.reshape(128, 16, 128)
    gain_rows = extras[:, :2, :9].astype(jnp.float32).transpose(1, 0, 2)
    gain_rows = jnp.pad(gain_rows.reshape(LAYERS, 2, MODEL_WIDTH), ((0, 0), (0, 6), (0, 0)))
    blocks = lax.dynamic_slice(
        extras[:, 2, 0], (lax.axis_index("fsdp") * 32,), (32,)
    ).astype(jnp.int32)
    flags = jnp.concatenate([blocks < block, jnp.full((8,), True)]).astype(jnp.float32)
    flags = (
        jnp.broadcast_to(flags[:, None], (40, LANES)),
        jnp.broadcast_to(flags[:, None, None], (40, 8, 128)),
    )
    hidden = lo_first(hidden_in[0]).astype(jnp.float32)
    inputs, kept, wholes = [], [], []
    for layer in range(LAYERS):
        inputs.append(hidden)
        state, hidden, whole = layer_forward(
            hidden, firsts[layer], gain_rows[layer], turns, flags, sources[layer]
        )
        kept.append(state)
        wholes.append(whole)
        firsts.append(whole)
    output_rows = lo_first(hidden.astype(jnp.bfloat16))
    grad_hidden = lo_first(cotangent[0]).astype(jnp.float32)
    owned = [None] * LAYERS
    gain_terms = [None] * LAYERS
    left = ()
    for layer in reversed(range(LAYERS)):
        grad_hidden, owned[layer], gq, gkv, gb, gain_terms[layer] = layer_backward(
            3 + layer, grad_hidden, inputs[layer], firsts[layer], wholes[layer],
            gain_rows[layer], turns, flags, kept[layer], left,
        )
        left = (gq, gkv, kept[layer][6], kept[layer][0], gb)
    last, gain_sums = reduce_last(left, jnp.concatenate(gain_terms, 0))
    owned = [jnp.where(at_front, last, owned[0]), jnp.where(at_front, owned[0], owned[1])]
    index = lax.axis_index("fsdp") * 32 + lax.axis_index("ctx")
    gain_sums = gain_sums.reshape(LAYERS, 8, MODEL_WIDTH)[:, :2].reshape(LAYERS, 2 * MODEL_WIDTH)
    owned_gains = lax.dynamic_slice(gain_sums, (0, index * 9), (LAYERS, 9))
    return (
        output_rows[None],
        lo_first(grad_hidden)[None],
        jnp.stack(owned),
        owned_gains,
    )


def solution(mesh):
    return jax.shard_map(
        on_device,
        mesh=mesh,
        in_specs=(
            P("fsdp", "ctx", None),
            P("fsdp", "ctx"),
            P(None, ("fsdp", "ctx"), None),
            P(None, ("fsdp", "ctx")),
            P("fsdp", "ctx", None),
        ),
        out_specs=(
            P("fsdp", "ctx", None),
            P("fsdp", "ctx", None),
            P(None, ("fsdp", "ctx"), None),
            P(None, ("fsdp", "ctx")),
        ),
        check_vma=False,
    )
```

```python
import functools

import jax
import jax.numpy as jnp
from jax import lax
from jax.experimental import pallas as pl
from jax.experimental.pallas import tpu as pltpu
from jax.sharding import PartitionSpec as P

MODEL_WIDTH = 576
FEEDFORWARD_SIZE = 1536
QUERY_HEADS = 9
KEY_VALUE_HEADS = 3
HEAD_SIZE = 64
LAYERS = 2

EPSILON = 1e-05
THETA = 100000.0
MASKED = -1e30
MESH = pl.DeviceIdType.MESH
RING = 4


def place():
    t = lax.axis_index("ctx")
    return (lax.axis_index("fsdp"), t // 8, (t // 2) % 4, t % 2)


def device(y, x, z, c):
    return (y, x * 8 + z * 2 + c)


def moved(me, axis, step):
    other = list(me)
    other[axis] = (me[axis] + step) % RING
    return tuple(other)


def sibling(me):
    return (me[0], me[1], me[2], 1 - me[3])


def greet(peers):
    barrier = pltpu.get_barrier_semaphore()
    for peer in peers:
        pl.semaphore_signal(barrier, inc=1, device_id=device(*peer), device_id_type=MESH)
    pl.semaphore_wait(barrier, len(peers))


TILES = 33
CHUNK = 11
LANES = 384


def head_lanes():
    return lax.broadcasted_iota(jnp.int32, (1, LANES), 1) % 128 >= 64


def roll_heads(rows):
    return jnp.concatenate(
        [pltpu.roll(rows[:, 128 * h : 128 * h + 128], 64, 1) for h in range(3)], axis=1
    )


def pack_tile(lo, hi, keep_lo, use_a, use_b):
    lo = lo.astype(jnp.float32)
    hi = hi.astype(jnp.float32)
    zero = jnp.zeros_like(lo)
    a = jnp.where(use_a, lo, zero)
    b = jnp.where(use_b, hi, zero)
    if not keep_lo:
        lo = zero
    left = lax.broadcasted_iota(jnp.int32, (64, 128), 1) < 64
    keys = [jnp.where(left, lo, pltpu.roll(a, 64, 1)), jnp.where(left, b, zero)]
    values = [jnp.where(left, pltpu.roll(lo, 64, 1), a), jnp.where(left, pltpu.roll(b, 64, 1), zero)]
    return (
        jnp.concatenate(keys, axis=1).astype(jnp.bfloat16),
        jnp.concatenate(values, axis=1).astype(jnp.bfloat16),
    )


def pack_all(g, me, kv, tall, keys, values):
    def one(t, carry):
        at = kv[g, t // 8, (t // 2) % 4, t % 2]
        use_a = jnp.broadcast_to(tall[t][:1] > 0.5, (64, 128))
        k, v = pack_tile(at[:64], at[64:], True, use_a, jnp.logical_not(use_a))
        spot = pl.ds(pl.multiple_of(t * 64, 64), 64)
        keys[spot] = k
        values[spot] = v
        return carry

    lax.fori_loop(0, TILES - 1, one, 0, unroll=4)
    yes = jnp.full((64, 128), True)
    at = kv[g, me[1], me[2], me[3]]
    k, v = pack_tile(at[:64], at[64:], False, yes, jnp.logical_not(yes))
    keys[pl.ds(64 * (TILES - 1), 64)] = k
    values[pl.ds(64 * (TILES - 1), 64)] = v


def dot_cols(left, right):
    return lax.dot_general(
        left, right, (((1,), (1,)), ((), ())), preferred_element_type=jnp.float32
    )


def dot_rows(left, right):
    return lax.dot_general(
        left, right, (((0,), (0,)), ((), ())), preferred_element_type=jnp.float32
    )


def score_all(keys, queries, scores):
    for c in range(TILES // CHUNK):
        rows = pl.ds(64 * CHUNK * c, 64 * CHUNK)
        scores[rows] = dot_cols(keys[rows], queries)
    at = lax.broadcasted_iota(jnp.int32, (64, LANES), 0)
    lane = lax.broadcasted_iota(jnp.int32, (64, LANES), 1) % 128
    causal = jnp.logical_and(lane < 64, at <= lane)
    mine = pl.ds(pl.multiple_of(lax.axis_index("ctx") * 64, 64), 64)
    scores[mine] = jnp.where(jnp.logical_or(lane >= 64, causal), scores[mine], MASKED)
    last = pl.ds(64 * (TILES - 1), 64)
    scores[last] = jnp.where(causal, scores[last], MASKED)


def tile_rows(flags, row):
    crossed = jnp.where(head_lanes(), row, roll_heads(row))
    return jnp.where(flags[...] > 0.5, row, crossed)


def joined(rows, flags, merge, empty):
    straight = jnp.where(jnp.logical_or(head_lanes(), flags[...] > 0.5), rows, empty)
    crossed = jnp.where(jnp.logical_or(head_lanes(), flags[...] > 0.5), empty, rows)
    down = jnp.max if merge is jnp.maximum else jnp.sum
    one = down(straight, axis=0, keepdims=True)
    other = roll_heads(down(crossed, axis=0, keepdims=True))
    return merge(one, other)


def fold_lanes(product):
    return jnp.where(
        head_lanes(), product[:64] + roll_heads(product[128:192]), product[64:128]
    )


def attend_group(
    g, me, kv, queries, flags, tall, out, lse, keys, values, scores, rows, between
):
    pack_all(g, me, kv, tall, keys, values)
    score_all(keys, queries[g], scores)
    between()
    rows[...] = jnp.full(rows.shape, MASKED, jnp.float32)

    for t in range(TILES):
        rows[pl.ds(t, 1)] = jnp.max(scores[pl.ds(64 * t, 64)], axis=0, keepdims=True)
    top = joined(rows[...], flags, jnp.maximum, MASKED)
    rows[...] = tile_rows(flags, top)
    total = jnp.zeros((256, LANES), jnp.float32)
    sums = []
    for c in range(TILES // CHUNK):
        parts = []
        for i in range(CHUNK):
            t = c * CHUNK + i
            raised = jnp.exp(scores[pl.ds(64 * t, 64)] - rows[pl.ds(t, 1)])
            sums.append(jnp.sum(raised, axis=0, keepdims=True))
            parts.append(raised.astype(jnp.bfloat16))
        spot = pl.ds(64 * CHUNK * c, 64 * CHUNK)
        total = total + dot_rows(values[spot], jnp.concatenate(parts, axis=0))
    rows[...] = jnp.zeros(rows.shape, jnp.float32)
    for t in range(TILES):
        rows[pl.ds(t, 1)] = sums[t]
    amount = joined(rows[...], flags, jnp.add, 0.0)
    out[g] = fold_lanes(total) / amount
    lse[g] = jnp.broadcast_to(top + jnp.log(amount), (8, LANES))


def attend_back_group(
    g, me, kv, queries, grads, lse, inner, flags, tall, dq, dkv,
    keys, values, scores, lse_rows, inner_rows,
):
    pack_all(g, me, kv, tall, keys, values)
    score_all(keys, queries[g], scores)
    lse_rows[...] = tile_rows(flags, lse[g][:1])
    inner_rows[...] = tile_rows(flags, inner[g][:1])
    total = jnp.zeros((256, LANES), jnp.float32)
    for c in range(TILES // CHUNK):
        spot = pl.ds(64 * CHUNK * c, 64 * CHUNK)
        grad_probs = dot_cols(values[spot], grads[g])
        probs, rest = [], []
        for i in range(CHUNK):
            t = c * CHUNK + i
            p = jnp.exp(scores[pl.ds(64 * t, 64)] - lse_rows[pl.ds(t, 1)])
            probs.append(p.astype(jnp.bfloat16))
            rest.append(
                (p * (grad_probs[64 * i : 64 * i + 64] - inner_rows[pl.ds(t, 1)])).astype(jnp.bfloat16)
            )
        probs = jnp.concatenate(probs, axis=0)
        rest = jnp.concatenate(rest, axis=0)
        total = total + dot_rows(keys[spot], rest)
        to_keys = jnp.dot(rest, queries[g], preferred_element_type=jnp.float32)
        to_values = jnp.dot(probs, grads[g], preferred_element_type=jnp.float32)
        left = lax.broadcasted_iota(jnp.int32, (64, 128), 1) < 64
        for i in range(CHUNK):
            t = c * CHUNK + i
            k0 = to_keys[64 * i : 64 * i + 64, :128]
            k1 = to_keys[64 * i : 64 * i + 64, 128:]
            v0 = to_values[64 * i : 64 * i + 64, :128]
            v1 = to_values[64 * i : 64 * i + 64, 128:]
            a = jnp.where(left, pltpu.roll(k0, 64, 1), v0)
            if t < TILES - 1:
                use_a = jnp.broadcast_to(tall[t][:1] > 0.5, (64, 128))
                lo = jnp.where(left, k0, pltpu.roll(v0, 64, 1)) + jnp.where(use_a, a, 0.0)
                hi = jnp.where(use_a, 0.0, jnp.where(left, k1, pltpu.roll(v1, 64, 1)))
                dkv[g, t // 8, (t // 2) % 4, t % 2, :64] = lo.astype(jnp.bfloat16)
                dkv[g, t // 8, (t // 2) % 4, t % 2, 64:] = hi.astype(jnp.bfloat16)
            else:
                spot = (g, me[1], me[2], me[3], pl.ds(0, 64))
                dkv[spot] = (dkv[spot].astype(jnp.float32) + a).astype(jnp.bfloat16)
    dq[g] = fold_lanes(total)


def weight_gather(
    me, source, whole, sends, recvs, swap_sends, swap_recvs, own_sem, skip=False
):
    def region(k, phase, at, core):
        index = [at[0], at[1], at[2]]
        for i in range(phase):
            axis = (k + i) % 3
            index[axis] = pl.ds(1, 3) if skip and axis == 0 else slice(None)
        return whole.at[tuple(index) + (core, pl.ds(16 * k, 16))]

    def has(k, phase, y):
        return None if not skip or phase > -k % 3 else y != 0

    def copy(src, dst, k, phase, s):
        return pltpu.make_async_remote_copy(
            src_ref=src, dst_ref=dst,
            send_sem=sends.at[k, phase, s - 1], recv_sem=recvs.at[k, phase, s - 1],
            device_id=device(*moved(me, (k + phase) % 3, s)), device_id_type=MESH)

    def send(k, phase, s, what):
        spot = region(k, phase, me, me[3])
        made = copy(spot if phase else source.at[pl.ds(16 * k, 16)], spot, k, phase, s)
        only(has(k, phase, me[0]), made.start if what == "start" else made.wait_send)

    def land(k, phase, s):
        there = moved(me, (k + phase) % 3, -s)
        spot = region(k, phase, there, me[3])
        only(has(k, phase, there[0]), copy(spot, spot, k, phase, s).wait_recv)

    def swap(k, s, core, what):
        there = moved(me, (k + 2) % 3, -s)
        spot = region(k, 2, there, core)
        made = pltpu.make_async_remote_copy(
            src_ref=spot, dst_ref=spot,
            send_sem=swap_sends.at[k, s], recv_sem=swap_recvs.at[k, s],
            device_id=device(*sibling(me)), device_id_type=MESH)
        act = {"start": made.start, "sent": made.wait_send, "landed": made.wait_recv}
        only(has(k, 2, there[0]), act[what])

    def begin():
        own = pltpu.make_async_copy(source, whole.at[me], own_sem)
        own.start()
        for k in range(3):
            for s in (2, 1, 3):
                send(k, 0, s, "start")
        own.wait()

    def forward(phase):
        for k in range(3):
            for s in (1, 3, 2):
                land(k, phase - 1, s)
            for s in (2, 1, 3):
                send(k, phase, s, "start")
            if phase == 2:
                swap(k, 0, me[3], "start")

    def exchange():
        for s in (1, 3, 2):
            for k in range(3):
                land(k, 2, s)
                swap(k, s, me[3], "start")

    def arrive():
        for k in range(3):
            for s in range(4):
                swap(k, s, 1 - me[3], "landed")

    def finish():
        for k in range(3):
            for phase in range(3):
                for s in (1, 2, 3):
                    send(k, phase, s, "sent")
            for s in range(4):
                swap(k, s, me[3], "sent")

    return begin, forward, exchange, arrive, finish


def only(condition, act):
    if condition is None:
        act()
    else:
        pl.when(condition)(act)


WEIGHT_GATHER_SEMS = [
    pltpu.SemaphoreType.DMA((3, 3, 3)),
    pltpu.SemaphoreType.DMA((3, 3, 3)),
    pltpu.SemaphoreType.DMA((3, 4)),
    pltpu.SemaphoreType.DMA((3, 4)),
    pltpu.SemaphoreType.DMA,
]
WHOLE = jax.ShapeDtypeStruct((4, 4, 4, 2, 48, MODEL_WIDTH), jnp.bfloat16)
ALL_PEERS = tuple((a, s) for a in range(3) for s in (1, 2, 3))


def greet_all(me):
    greet([moved(me, a, s) for a, s in ALL_PEERS] + [sibling(me)])


def row_gather(me, own, kv, sends, recvs, swap_sends, swap_recvs, own_sems):
    def region(g, k, phase, at, core):
        index = [at[1], at[2]]
        if phase >= 1:
            index[1 - k] = slice(None)
        return kv.at[(g,) + tuple(index) + (core, pl.ds(64 * k, 64))]

    def axis_of(k, phase):
        return 1 + (1 - k + phase) % 2

    def copy(src, dst, g, k, phase, s):
        return pltpu.make_async_remote_copy(
            src_ref=src, dst_ref=dst,
            send_sem=sends.at[g, k, phase, s - 1], recv_sem=recvs.at[g, k, phase, s - 1],
            device_id=device(*moved(me, axis_of(k, phase), s)), device_id_type=MESH)

    def send(g, k, phase, s):
        spot = region(g, k, phase, me, me[3])
        return copy(spot if phase else own.at[g, pl.ds(64 * k, 64)], spot, g, k, phase, s)

    def landed(g, k, phase, s):
        spot = region(g, k, phase, moved(me, axis_of(k, phase), -s), me[3])
        return copy(spot, spot, g, k, phase, s)

    def swap(g, k, s, core):
        spot = region(g, k, 1, moved(me, axis_of(k, 1), -s), core)
        return pltpu.make_async_remote_copy(
            src_ref=spot, dst_ref=spot,
            send_sem=swap_sends.at[g, k, s], recv_sem=swap_recvs.at[g, k, s],
            device_id=device(*sibling(me)), device_id_type=MESH)

    def keep(g):
        return pltpu.make_async_copy(own.at[g], kv.at[g, me[1], me[2], me[3]], own_sems.at[g])

    def begin(g):
        for s in (2, 1, 3):
            for k in range(2):
                send(g, k, 0, s).start()
        keep(g).start()

    def forward(g):
        keep(g).wait()
        for k in range(2):
            for s in (1, 3, 2):
                landed(g, k, 0, s).wait_recv()
            for s in (2, 1, 3):
                send(g, k, 1, s).start()
            swap(g, k, 0, me[3]).start()

    def arrive(g):
        for s in (1, 3, 2):
            for k in range(2):
                landed(g, k, 1, s).wait_recv()
                swap(g, k, s, me[3]).start()
        for k in range(2):
            for s in range(4):
                swap(g, k, s, 1 - me[3]).wait_recv()

    def finish(g):
        for k in range(2):
            for phase in range(2):
                for s in (1, 2, 3):
                    send(g, k, phase, s).wait_send()
            for s in range(4):
                swap(g, k, s, me[3]).wait_send()

    return begin, forward, arrive, finish


def weight_reduce(
    me, grads, halves, landed_a, sum_a, landed_b, sum_b, landed_c,
    swap_sends, swap_recvs, sends, recvs,
):
    axes = ((2, 1, 0), (0, 2, 1), (1, 0, 2))

    def swap(y):
        return pltpu.make_async_remote_copy(
            src_ref=grads.at[y, :, :, 1 - me[3]], dst_ref=halves.at[y],
            send_sem=swap_sends.at[y], recv_sem=swap_recvs.at[y],
            device_id=device(*sibling(me)), device_id_type=MESH)

    def copy(stage, src, dst, k, s, peer):
        return pltpu.make_async_remote_copy(
            src_ref=src, dst_ref=dst,
            send_sem=sends.at[stage, k, s - 1], recv_sem=recvs.at[stage, k, s - 1],
            device_id=device(*peer), device_id_type=MESH)

    def send(stage, k, s):
        axis = axes[k][stage]
        peer = moved(me, axis, s)
        if stage == 0:
            index = [slice(None)] * 3
            index[axis] = peer[axis]
            return copy(0, halves.at[tuple(index) + (pl.ds(16 * k, 16),)], landed_a.at[k, s - 1], k, s, peer)
        if stage == 1:
            index = [slice(None)] * 2
            index[sorted(axes[k][1:]).index(axis)] = peer[axis]
            return copy(1, sum_a.at[(k,) + tuple(index)], landed_b.at[k, s - 1], k, s, peer)
        return copy(2, sum_b.at[k, peer[axis]], landed_c.at[k, s - 1], k, s, peer)

    def halve(y):
        swap(y).wait_recv()
        for x in range(4):
            for z in range(4):
                halves[y, x, z] = (
                    grads[y, x, z, me[3]].astype(jnp.float32) + halves[y, x, z].astype(jnp.float32)
                ).astype(jnp.bfloat16)

    def begin():
        for k in range(3):
            for s in (2, 1, 3):
                send(0, k, s).start()

    def second():
        for k in range(3):
            for s in (1, 3, 2):
                send(0, k, s).wait_recv()
            axis = axes[k][0]
            for i in range(4):
                for j in range(4):
                    at = [i, j]
                    at.insert(axis, me[axis])
                    total = halves[tuple(at) + (pl.ds(16 * k, 16),)].astype(jnp.float32)
                    for s in range(3):
                        total = total + landed_a[k, s, i, j].astype(jnp.float32)
                    sum_a[k, i, j] = total.astype(jnp.bfloat16)
            for s in (2, 1, 3):
                send(1, k, s).start()

    def third():
        for k in range(3):
            for s in (1, 3, 2):
                send(1, k, s).wait_recv()
            rest = sorted(axes[k][1:])
            for i in range(4):
                at = [i, i]
                at[rest.index(axes[k][1])] = me[axes[k][1]]
                total = sum_a[(k,) + tuple(at)].astype(jnp.float32)
                for s in range(3):
                    total = total + landed_b[k, s, i].astype(jnp.float32)
                sum_b[k, i] = total.astype(jnp.bfloat16)
            for s in (2, 1, 3):
                send(2, k, s).start()

    def finish(planes, out):
        for k in range(3):
            for s in (1, 3, 2):
                send(2, k, s).wait_recv()
            total = sum_b[k, me[axes[k][2]]].astype(jnp.float32)
            for s in range(3):
                total = total + landed_c[k, s].astype(jnp.float32)
            out[pl.ds(16 * k, 16)] = total
        for y in planes:
            swap(y).wait_send()
        for stage in range(3):
            for k in range(3):
                for s in (1, 2, 3):
                    send(stage, k, s).wait_send()

    return swap, halve, begin, second, third, finish


def weight_reduce_scratch():
    bf, w = jnp.bfloat16, MODEL_WIDTH
    return [
        pltpu.VMEM((4, 4, 4, 2, 48, w), bf),
        pltpu.VMEM((4, 4, 4, 48, w), bf),
        pltpu.VMEM((3, 3, 4, 4, 16, w), bf),
        pltpu.VMEM((3, 4, 4, 16, w), bf),
        pltpu.VMEM((3, 3, 4, 16, w), bf),
        pltpu.VMEM((3, 4, 16, w), bf),
        pltpu.VMEM((3, 3, 16, w), bf),
        pltpu.SemaphoreType.DMA((4,)),
        pltpu.SemaphoreType.DMA((4,)),
        pltpu.SemaphoreType.DMA((3, 3, 3)),
        pltpu.SemaphoreType.DMA((3, 3, 3)),
    ]


def row_reduce(
    me, terms, out, halves, landed_a, sum_a, landed_b, swap_sends, swap_recvs, sends, recvs
):
    axes = ((2, 1), (1, 2))

    def swap(g):
        return pltpu.make_async_remote_copy(
            src_ref=terms.at[g, :, :, 1 - me[3]], dst_ref=halves.at[g],
            send_sem=swap_sends.at[g], recv_sem=swap_recvs.at[g],
            device_id=device(*sibling(me)), device_id_type=MESH)

    def send(stage, g, k, s):
        axis = axes[k][stage]
        peer = moved(me, axis, s)
        if stage == 0:
            index = [slice(None)] * 2
            index[axis - 1] = peer[axis]
            src = halves.at[(g,) + tuple(index) + (pl.ds(64 * k, 64),)]
            dst = landed_a.at[g, k, s - 1]
        else:
            src = sum_a.at[g, k, peer[axis]]
            dst = landed_b.at[g, k, s - 1]
        return pltpu.make_async_remote_copy(
            src_ref=src, dst_ref=dst,
            send_sem=sends.at[stage, g, k, s - 1], recv_sem=recvs.at[stage, g, k, s - 1],
            device_id=device(*peer), device_id_type=MESH)

    def begin(g):
        swap(g).start()

    def second(g):
        swap(g).wait_recv()
        for x in range(4):
            for z in range(4):
                halves[g, x, z] = (
                    terms[g, x, z, me[3]].astype(jnp.float32) + halves[g, x, z].astype(jnp.float32)
                ).astype(jnp.bfloat16)
        for s in (2, 1, 3):
            for k in range(2):
                send(0, g, k, s).start()

    def third(g):
        for k in range(2):
            for s in (1, 3, 2):
                send(0, g, k, s).wait_recv()
            axis = axes[k][0]
            for i in range(4):
                at = [i]
                at.insert(axis - 1, me[axis])
                total = halves[(g,) + tuple(at) + (pl.ds(64 * k, 64),)].astype(jnp.float32)
                for s in range(3):
                    total = total + landed_a[g, k, s, i].astype(jnp.float32)
                sum_a[g, k, i] = total.astype(jnp.bfloat16)
            for s in (2, 1, 3):
                send(1, g, k, s).start()

    def finish(g):
        for k in range(2):
            for s in (1, 3, 2):
                send(1, g, k, s).wait_recv()
            total = sum_a[g, k, me[axes[k][1]]].astype(jnp.float32)
            for s in range(3):
                total = total + landed_b[g, k, s].astype(jnp.float32)
            out[g, pl.ds(64 * k, 64)] = total

    def drain(g):
        swap(g).wait_send()
        for stage in range(2):
            for k in range(2):
                for s in (1, 2, 3):
                    send(stage, g, k, s).wait_send()

    return begin, second, third, finish, drain


def row_reduce_scratch():
    bf = jnp.bfloat16
    return [
        pltpu.VMEM((3, 4, 4, 128, 128), bf),
        pltpu.VMEM((3, 2, 3, 4, 64, 128), bf),
        pltpu.VMEM((3, 2, 4, 64, 128), bf),
        pltpu.VMEM((3, 2, 3, 64, 128), bf),
        pltpu.SemaphoreType.DMA((3,)),
        pltpu.SemaphoreType.DMA((3,)),
        pltpu.SemaphoreType.DMA((2, 3, 2, 3)),
        pltpu.SemaphoreType.DMA((2, 3, 2, 3)),
    ]


def left_lanes():
    return lax.broadcasted_iota(jnp.int32, (128, 128), 1) < 64


def swapped(tile):
    low = lax.broadcasted_iota(jnp.int32, tile.shape, 1) % 64 < 32
    return jnp.where(low, pltpu.roll(tile, 96, 1), pltpu.roll(tile, 32, 1))


def spread_tile(spots, tile, j):
    other = pltpu.roll(tile, 64, 1)
    left = left_lanes()
    for i in range(2):
        head = 2 * j + i
        if head >= QUERY_HEADS:
            continue
        a = jnp.where(left, tile if i == 0 else other, 0.0).astype(jnp.bfloat16)
        b = jnp.where(left, 0.0, other if i == 0 else tile).astype(jnp.bfloat16)
        g, at = head // 3, 128 * (head % 3)
        spots[g, at : at + 64, :128] = b[:64]
        spots[g, at : at + 64, 128:] = a[64:]
        spots[g, at + 64 : at + 128, :128] = a[64:]
        spots[g, at + 64 : at + 128, 128:] = jnp.zeros((64, 128), jnp.bfloat16)


def group_weights(first, g):
    return jnp.concatenate(
        [first[0, 576 + 64 * g : 640 + 64 * g], first[0, 768 + 64 * g : 832 + 64 * g]], axis=0
    )


def inverse_root(values):
    return lax.rsqrt(jnp.mean(values * values, axis=-1, keepdims=True) + EPSILON)


HALF_ROWS = ((0, 32), (32, 16))


SAVED = (
    ((128, MODEL_WIDTH), jnp.bfloat16),
    ((3, LANES, 256), jnp.bfloat16),
    ((3, 4, 4, 2, 128, 128), jnp.bfloat16),
    ((3, 64, LANES), jnp.float32),
    ((3, 8, LANES), jnp.float32),
    ((MODEL_WIDTH, 128), jnp.bfloat16),
    ((128, MODEL_WIDTH), jnp.float32),
    ((128, MODEL_WIDTH), jnp.bfloat16),
    ((128, FEEDFORWARD_SIZE), jnp.float32),
    ((128, FEEDFORWARD_SIZE), jnp.float32),
    ((128, FEEDFORWARD_SIZE), jnp.bfloat16),
)


def sum_everywhere(me, parts, landed, sends, recvs):
    axes = (None, 2, 1, 0)

    def copy(stage, s):
        peer = sibling(me) if stage == 0 else moved(me, axes[stage], s)
        return pltpu.make_async_remote_copy(
            src_ref=parts.at[stage], dst_ref=landed.at[stage, s - 1],
            send_sem=sends.at[stage, s - 1], recv_sem=recvs.at[stage, s - 1],
            device_id=device(*peer), device_id_type=MESH)

    def steps(stage):
        return (1,) if stage == 0 else (2, 1, 3)

    def begin(value):
        parts[0] = value
        copy(0, 1).start()

    def step(stage):
        total = parts[stage]
        for s in steps(stage):
            copy(stage, s).wait_recv()
            total = total + landed[stage, s - 1]
        if stage < 3:
            parts[stage + 1] = total
            for s in steps(stage + 1):
                copy(stage + 1, s).start()
        return total

    def finish():
        for stage in range(4):
            for s in steps(stage):
                copy(stage, s).wait_send()

    return begin, step, finish


def first_gather(me, source, whole, stage, sends, recvs, swap_sends, swap_recvs, y_sends, y_recvs, own_sems):
    def along_y(s, y):
        return pltpu.make_async_remote_copy(
            src_ref=source, dst_ref=stage.at[y],
            send_sem=y_sends.at[s - 1], recv_sem=y_recvs.at[s - 1],
            device_id=device(*moved(me, 0, s)), device_id_type=MESH)

    def region(k, phase, at, core):
        index = [at[1], at[2]]
        if phase:
            index[k] = slice(None)
        return whole.at[tuple(index) + (core, pl.ds(*HALF_ROWS[k]))]

    def copy(src, dst, k, phase, s):
        return pltpu.make_async_remote_copy(
            src_ref=src, dst_ref=dst,
            send_sem=sends.at[k, phase, s - 1], recv_sem=recvs.at[k, phase, s - 1],
            device_id=device(*moved(me, 1 + (k + phase) % 2, s)), device_id_type=MESH)

    def send(k, phase, s):
        spot = region(k, phase, me, me[3])
        return copy(spot if phase else stage.at[0, pl.ds(*HALF_ROWS[k])], spot, k, phase, s)

    def landed(k, phase, s):
        spot = region(k, phase, moved(me, 1 + (k + phase) % 2, -s), me[3])
        return copy(spot, spot, k, phase, s)

    def swap(k, s, core):
        spot = region(k, 1, moved(me, 1 + (k + 1) % 2, -s), core)
        return pltpu.make_async_remote_copy(
            src_ref=spot, dst_ref=spot,
            send_sem=swap_sends.at[k, s], recv_sem=swap_recvs.at[k, s],
            device_id=device(*sibling(me)), device_id_type=MESH)

    own = pltpu.make_async_copy(source, stage.at[me[0]], own_sems.at[0])
    keep = pltpu.make_async_copy(stage.at[0], whole.at[me[1], me[2], me[3]], own_sems.at[1])

    def begin():
        for s in (2, 1, 3):
            along_y(s, me[0]).start()
        own.start()

    def spread():
        own.wait()
        for s in (1, 3, 2):
            along_y(s, (me[0] - s) % RING).wait_recv()
        for k in range(2):
            for s in (2, 1, 3):
                send(k, 0, s).start()
        keep.start()

    def forward():
        keep.wait()
        for k in range(2):
            for s in (1, 3, 2):
                landed(k, 0, s).wait_recv()
            for s in (2, 1, 3):
                send(k, 1, s).start()
            swap(k, 0, me[3]).start()

    def exchange():
        for s in (1, 3, 2):
            for k in (1, 0):
                landed(k, 1, s).wait_recv()
                swap(k, s, me[3]).start()

    def arrive():
        for k in range(2):
            for s in range(4):
                swap(k, s, 1 - me[3]).wait_recv()

    def finish():
        for s in (1, 2, 3):
            along_y(s, me[0]).wait_send()
        for k in range(2):
            for phase in range(2):
                for s in (1, 2, 3):
                    send(k, phase, s).wait_send()
            for s in range(4):
                swap(k, s, me[3]).wait_send()

    return begin, spread, forward, exchange, arrive, finish


def find_flags(blocks, mine, flags, tall):
    column = jnp.broadcast_to(blocks, (128, 128)).T[:40]
    place_of = lax.broadcasted_iota(jnp.int32, (40, 128), 0)
    before = jnp.logical_or(place_of >= TILES - 1, column < mine[:1])
    before = jnp.where(before, 1.0, 0.0)
    flags[...] = jnp.concatenate([before] * 3, axis=1)
    for t in range(40):
        tall[t] = jnp.broadcast_to(before[t : t + 1], (8, 128))


def flatten(first, planes):
    for j in range(32):
        first[0, 48 * j : 48 * j + 48] = planes[j // 8, (j // 2) % 4, j % 2]


def forward_kernel(
    hidden, params, extra, mine, cosine, sine,
    result, hidden_one, gains, flags, tall, first_out, whole0_out, whole1_out, *refs
):
    count = len(SAVED)
    saved_out, saved = refs[:count], refs[count : 2 * count]
    (
        keys, values, scores, rows, first, planes, stage, mix, whole0, whole1, parts, landed, owns,
    ) = refs[2 * count : 2 * count + 13]
    sems = refs[2 * count + 13 :]
    save_sems, row_sems, first_sems = sems[0], sems[1:6], sems[6:13]
    sum_sems, mix_sem = sems[13:15], sems[15]
    weight_sems = (sems[16:21], sems[21:26])
    me = place()
    for y in range(2):
        @pl.when((me[0] == 0) == (y == 0))
        def _():
            pltpu.make_async_copy(params.at[1 - y], mix, mix_sem).start()
    x = hidden[...]
    scaled = x * inverse_root(x)
    greet_all(me)
    g_begin, g_step, g_finish = sum_everywhere(me, parts, landed, *sum_sems)
    f_begin, f_spread, f_forward, f_exchange, f_arrive, f_finish = first_gather(
        me, params.at[0], planes, stage, *first_sems
    )
    weights = (
        weight_gather(me, mix, whole0, *weight_sems[0]),
        weight_gather(me, params.at[1], whole1, *weight_sems[1], skip=True),
    )
    saves = []

    def save(layer, i):
        copy = pltpu.make_async_copy(
            saved[i].at[layer], saved_out[i].at[layer], save_sems.at[layer, i]
        )
        copy.start()
        saves.append(copy)

    def save_as(i, src, dst):
        copy = pltpu.make_async_copy(src, dst, save_sems.at[2, i])
        copy.start()
        saves.append(copy)

    f_begin()
    g_begin(extra[...])
    pltpu.make_async_copy(params.at[0], mix, mix_sem).wait()
    f_spread()
    g_step(0)
    weights[0][0]()
    g_step(1)
    f_forward()
    blocks = g_step(2)
    find_flags(blocks[4:5, :128], mine, flags, tall)
    weights[0][1](1)
    gains[...] = g_step(3)
    f_exchange()
    f_arrive()
    flatten(first, planes)
    save_as(0, first, first_out)

    left = left_lanes()
    cos, sin = cosine[...], sine[...]
    for layer in range(LAYERS):
        whole = (whole0, whole1)[layer]
        w_begin, w_forward, w_exchange, w_arrive, w_finish = weights[layer]
        n1, queries, kv, turned, lse, mixed, middle, n2, gate, up, product = [
            r.at[layer] for r in saved
        ]
        own = owns.at[layer]
        begin, forward, arrive, finish = row_gather(
            me, own, kv, *[s.at[layer] for s in row_sems]
        )
        normed = (scaled * gains[2 * layer : 2 * layer + 1]).astype(jnp.bfloat16)
        n1[...] = normed
        for g in range(3):
            tile = dot_cols(normed, group_weights(first, g))
            tile = tile * jnp.where(left, cos, 1.0) + swapped(tile) * jnp.where(left, sin, 0.0)
            own[g] = tile.astype(jnp.bfloat16)
            begin(g)
        for j in range(5):
            tile = dot_cols(normed, first[0, 128 * j : 128 * j + 128])
            tile = (tile * cos + swapped(tile) * sin) * HEAD_SIZE ** (-0.5)
            spread_tile(queries, tile, j)
        save(layer, 0)
        save(layer, 1)
        for g in range(3):
            forward(g)
        if layer == 1:
            w_forward(1)

        def one(g, carry):
            arrive(g)

            def between():
                @pl.when(g == 0)
                def _():
                    w_forward(2)

            attend_group(
                g, me, kv, queries, flags, tall, turned, lse, keys, values, scores, rows, between
            )
            return carry

        lax.fori_loop(0, 3, one, 0)
        w_exchange()
        if layer == 0:
            weights[1][0]()
        for i in (2, 3, 4):
            save(layer, i)
        for g in range(3):
            for h in range(3):
                mixed[64 * (3 * g + h) : 64 * (3 * g + h) + 64] = turned[
                    g, :, 128 * h : 128 * h + 128
                ].astype(jnp.bfloat16)
        mid = x + dot_rows(mixed[...], first[0, 960:1536])
        middle[...] = mid
        normed = (mid * inverse_root(mid) * gains[2 * layer + 1 : 2 * layer + 2]).astype(jnp.bfloat16)
        n2[...] = normed
        for i in (5, 6, 7):
            save(layer, i)
        w_arrive()
        save_as(1 + layer, whole, (whole0_out, whole1_out)[layer])
        total = mid
        for i in range(4):
            part = pl.ds(384 * i, 384)
            gate_values = dot_cols(normed, whole[1, i].reshape(384, MODEL_WIDTH))
            up_values = dot_cols(normed, whole[2, i].reshape(384, MODEL_WIDTH))
            rounded = (gate_values * jax.nn.sigmoid(gate_values) * up_values).astype(jnp.bfloat16)
            gate[:, part] = gate_values
            up[:, part] = up_values
            product[:, part] = rounded
            total = total + jnp.dot(
                rounded, whole[3, i].reshape(384, MODEL_WIDTH), preferred_element_type=jnp.float32
            )
        for i in (8, 9, 10):
            save(layer, i)
        if layer == 0:
            hidden_one[...] = total
            x = total
            scaled = x * inverse_root(x)
            saves[0].wait()
            saves.pop(0)
            flatten(first, whole0.at[0])
        else:
            result[...] = total
        for g in range(3):
            finish(g)
    g_finish()
    f_finish()
    for w in weights:
        w[4]()
    for copy in saves:
        copy.wait()


ROWS_F32 = jax.ShapeDtypeStruct((128, MODEL_WIDTH), jnp.float32)
ROWS_BF16 = jax.ShapeDtypeStruct((128, MODEL_WIDTH), jnp.bfloat16)
TURNED_BF16 = jax.ShapeDtypeStruct((MODEL_WIDTH, 128), jnp.bfloat16)
VMEM_SPEC = pl.BlockSpec(memory_space=pltpu.VMEM)
HBM_SPEC = pl.BlockSpec(memory_space=pl.ANY)


def forward_pass(hidden, params, extra, mine, turns):
    bf, w = jnp.bfloat16, MODEL_WIDTH
    dma = pltpu.SemaphoreType.DMA
    outs = pl.pallas_call(
        forward_kernel,
        out_shape=(
            ROWS_F32,
            ROWS_F32,
            jax.ShapeDtypeStruct((8, w), jnp.float32),
            jax.ShapeDtypeStruct((40, LANES), jnp.float32),
            jax.ShapeDtypeStruct((40, 8, 128), jnp.float32),
            jax.ShapeDtypeStruct((1, 1536, w), bf),
            WHOLE,
            WHOLE,
        ) + tuple(jax.ShapeDtypeStruct((LAYERS,) + shape, dtype) for shape, dtype in SAVED),
        in_specs=[VMEM_SPEC, HBM_SPEC] + [VMEM_SPEC] * 4,
        out_specs=(VMEM_SPEC,) * 5 + (HBM_SPEC,) * (3 + len(SAVED)),
        scratch_shapes=[pltpu.VMEM((LAYERS,) + shape, dtype) for shape, dtype in SAVED] + [
            pltpu.VMEM((64 * TILES, 256), bf),
            pltpu.VMEM((64 * TILES, 256), bf),
            pltpu.VMEM((64 * TILES, LANES), jnp.float32),
            pltpu.VMEM((40, LANES), jnp.float32),
            pltpu.VMEM((1, 1536, w), bf),
            pltpu.VMEM((4, 4, 2, 48, w), bf),
            pltpu.VMEM((4, 48, w), bf),
            pltpu.VMEM((48, w), bf),
            pltpu.VMEM(WHOLE.shape, bf),
            pltpu.VMEM(WHOLE.shape, bf),
            pltpu.VMEM((4, 8, w), jnp.float32),
            pltpu.VMEM((4, 3, 8, w), jnp.float32),
            pltpu.VMEM((LAYERS, 3, 128, 128), bf),
            dma((3, len(SAVED))),
            dma((LAYERS, 3, 2, 2, 3)),
            dma((LAYERS, 3, 2, 2, 3)),
            dma((LAYERS, 3, 2, 4)),
            dma((LAYERS, 3, 2, 4)),
            dma((LAYERS, 3)),
            dma((2, 2, 3)),
            dma((2, 2, 3)),
            dma((2, 4)),
            dma((2, 4)),
            dma((3,)),
            dma((3,)),
            dma((2,)),
            dma((4, 3)),
            dma((4, 3)),
            dma,
        ] + WEIGHT_GATHER_SEMS * 2,
        compiler_params=pltpu.CompilerParams(
            collective_id=1, has_side_effects=True, vmem_limit_bytes=58 * 2**20
        ),
        name="forward_pass",
    )(hidden, params, extra, mine, *turns[:2])
    return outs[:8], outs[8:]


def norm_back(grad_normed, values, gain):
    inverse = inverse_root(values)
    unit = values * inverse
    grad_gain = jnp.sum(grad_normed * unit, axis=0, keepdims=True)
    scaled = grad_normed * gain
    grad_values = inverse * (
        scaled - unit * jnp.mean(scaled * unit, axis=-1, keepdims=True)
    )
    return grad_values, grad_gain


def products_first(gq, gkv, mixed, n1, gb):
    parts = [jnp.dot(gq[...], n1[...], preferred_element_type=jnp.float32)]
    both = [dot_rows(gkv[g], n1[...]) for g in range(3)]
    parts.append(jnp.concatenate([m[:64] for m in both], axis=0))
    parts.append(jnp.concatenate([m[64:] for m in both], axis=0))
    parts.append(jnp.dot(mixed[...], gb[...], preferred_element_type=jnp.float32))
    return [
        p.astype(jnp.bfloat16).reshape(p.shape[0] // 48, 48, MODEL_WIDTH) for p in parts
    ]


BIG = (2, 8, 9, 10)


def last_reduce(me, grads, halves, landed_a, sum_a, landed_b, sum_b, landed_y, swap_sends, swap_recvs, sends, recvs, y_sends, y_recvs):
    def swap(x):
        return pltpu.make_async_remote_copy(
            src_ref=grads.at[x, :, 1 - me[3]], dst_ref=halves.at[x],
            send_sem=swap_sends.at[x], recv_sem=swap_recvs.at[x],
            device_id=device(*sibling(me)), device_id_type=MESH)

    def copy(stage, src, dst, k, s):
        return pltpu.make_async_remote_copy(
            src_ref=src, dst_ref=dst,
            send_sem=sends.at[stage, k, s - 1], recv_sem=recvs.at[stage, k, s - 1],
            device_id=device(*moved(me, 1 + (k + 1 + stage) % 2, s)), device_id_type=MESH)

    def send(stage, k, s):
        axis = 1 + (k + 1 + stage) % 2
        to = moved(me, axis, s)[axis]
        rows = pl.ds(*HALF_ROWS[k])
        if stage == 0:
            index = [slice(None)] * 2
            index[axis - 1] = to
            return copy(0, halves.at[tuple(index) + (rows,)], landed_a.at[s - 1, :, rows], k, s)
        return copy(1, sum_a.at[to, rows], landed_b.at[s - 1, rows], k, s)

    def along_y(s):
        return pltpu.make_async_remote_copy(
            src_ref=sum_b, dst_ref=landed_y.at[s - 1],
            send_sem=y_sends.at[s - 1], recv_sem=y_recvs.at[s - 1],
            device_id=device(*moved(me, 0, s)), device_id_type=MESH)

    def begin():
        for x in range(4):
            swap(x).wait_recv()
            for z in range(4):
                halves[x, z] = (
                    grads[x, z, me[3]].astype(jnp.float32) + halves[x, z].astype(jnp.float32)
                ).astype(jnp.bfloat16)
        for s in (2, 1, 3):
            for k in range(2):
                send(0, k, s).start()

    def second():
        for k in (1, 0):
            rows = pl.ds(*HALF_ROWS[k])
            for s in (1, 3, 2):
                send(0, k, s).wait_recv()
            axis = 1 + (k + 1) % 2
            for i in range(4):
                spot = [i]
                spot.insert(axis - 1, me[axis])
                total = halves[tuple(spot) + (rows,)].astype(jnp.float32)
                for s in range(3):
                    total = total + landed_a[s, i, rows].astype(jnp.float32)
                sum_a[i, rows] = total.astype(jnp.bfloat16)
            for s in (2, 1, 3):
                send(1, k, s).start()

    def third():
        for k in (1, 0):
            rows = pl.ds(*HALF_ROWS[k])
            for s in (1, 3, 2):
                send(1, k, s).wait_recv()
            total = sum_a[me[1 + k % 2], rows].astype(jnp.float32)
            for s in range(3):
                total = total + landed_b[s, rows].astype(jnp.float32)
            sum_b[rows] = total.astype(jnp.bfloat16)
        for s in (2, 1, 3):
            along_y(s).start()

    def finish(out):
        total = sum_b[...].astype(jnp.float32)
        for s in (1, 3, 2):
            along_y(s).wait_recv()
            total = total + landed_y[s - 1].astype(jnp.float32)
        out[...] = total
        for x in range(4):
            swap(x).wait_send()
        for s in (1, 2, 3):
            along_y(s).wait_send()
            for stage in range(2):
                for k in range(2):
                    send(stage, k, s).wait_send()

    return swap, begin, second, third, finish


def backward_kernel(
    cotangent, hidden0, hidden1, first0, first1, rest0, rest1,
    gains, cosine, sine, cosine_t, sine_t, flags, tall, *refs
):
    count = len(SAVED)
    kept, refs = refs[:count], refs[count:]
    grad_hidden, owned, gain_sums = refs[:3]
    (
        keys, values, scores, lse_rows, inner_rows, dkv, spots, inner, dq, sums, ggate, gup,
        firsts, whole, gq, gkv, gb, gain_terms, reduced, load_sems, free_sem,
    ) = refs[3:24]
    row_refs = refs[24:32]
    weight_refs = refs[32:43]
    last_refs = refs[43:55]
    sum_refs = refs[55:59]
    saved = refs[59:]
    me = place()
    peers = [moved(me, a, s) for a, s in ALL_PEERS] + [sibling(me)]

    def view(layer, i):
        return saved[i] if i in BIG else saved[i].at[layer]

    def load(layer, i):
        return pltpu.make_async_copy(kept[i].at[layer], view(layer, i), load_sems.at[layer, i])

    def load_rest(layer):
        return pltpu.make_async_copy(
            (rest0, rest1)[layer].at[pl.ds(1, 3)], whole, load_sems.at[layer, count]
        )

    def load_first(layer):
        return pltpu.make_async_copy(
            (first0, first1)[layer].at[0], firsts.at[layer], load_sems.at[layer, count + 1]
        )

    load_rest(1).start()
    for i in (8, 9, 10, 7, 6, 3, 0, 1, 4, 5, 2):
        load(1, i).start()
    load_first(1).start()
    load_first(0).start()
    for i in range(count):
        if i not in BIG:
            load(0, i).start()
    greet(peers)
    begin, second, third, finish, drain = row_reduce(me, dkv, sums, *row_refs)
    swap, halve, w_begin, w_second, w_third, w_finish = weight_reduce(me, *weight_refs)
    grads, halves = weight_refs[0], weight_refs[1]
    l_swap, l_begin, l_second, l_third, l_finish = last_reduce(me, grads.at[0], *last_refs)
    g_begin, g_step, g_finish = sum_everywhere(me, *sum_refs)
    left = left_lanes()
    cos, sin = jnp.where(left, cosine[...], 1.0), jnp.where(left, sine[...], 0.0)
    gain_terms[...] = jnp.zeros(gain_terms.shape, jnp.float32)
    gr = cotangent[...]

    def first_products(layer, done):
        at = 0
        for cut in products_first(gq, gkv, view(layer, 5), view(layer, 0), gb):
            for i in range(cut.shape[0]):
                j = at + i
                grads[0, j // 8, (j // 2) % 4, j % 2] = cut[i]
                done(j)
            at += cut.shape[0]

    for layer in (1, 0):
        n1, queries, kv, turned, lse, mixed, middle, n2, gate, up, product = [
            view(layer, i) for i in range(count)
        ]
        first = firsts.at[layer]
        order = (1, 2, 3) if layer == 1 else (1, 2, 3, 0)
        load_rest(layer).wait()
        for i in (8, 9, 10, 7, 6):
            load(layer, i).wait()
        if layer == 0:
            first_products(1, lambda j: None)
        gd = gr.astype(jnp.bfloat16)
        normed = n2[...]
        grad_normed = jnp.zeros((128, MODEL_WIDTH), jnp.float32)
        for i in range(4):
            part = pl.ds(384 * i, 384)
            grad_product = dot_cols(gd, whole[2, i])
            gate_values, up_values = gate[:, part], up[:, part]
            s = jax.nn.sigmoid(gate_values)
            gg = (
                grad_product * up_values * (s * (1.0 + gate_values * (1.0 - s)))
            ).astype(jnp.bfloat16)
            gu = (grad_product * (gate_values * s)).astype(jnp.bfloat16)
            ggate[:, part] = gg
            gup[:, part] = gu
            grad_normed = grad_normed + jnp.dot(
                gg, whole[0, i], preferred_element_type=jnp.float32
            ) + jnp.dot(gu, whole[1, i], preferred_element_type=jnp.float32)
        for y, source, right in ((1, ggate, normed), (2, gup, normed), (3, product, gd)):
            for i in range(4):
                flat = dot_rows(source[:, 384 * i : 384 * i + 384], right).astype(jnp.bfloat16)
                grads[y, i] = flat.reshape(4, 2, 48, MODEL_WIDTH)
            if y == 1 and layer == 0:
                pl.semaphore_wait(free_sem, len(peers))
                swap(0).start()
            swap(y).start()
        if layer == 1:
            load_rest(0).start()
            for i in (8, 9, 10):
                load(0, i).start()
        grad_middle, grad_gain = norm_back(
            grad_normed, middle[...], gains[2 * layer + 1 : 2 * layer + 2]
        )
        gain_terms[2 * layer + 1 : 2 * layer + 2] = grad_gain
        grad_middle = grad_middle + gr
        branch = grad_middle.astype(jnp.bfloat16)
        gb[...] = branch
        load_first(layer).wait()
        for i in (3, 0, 1, 4, 5):
            load(layer, i).wait()
        for j in range(5):
            width = min(128, 576 - 128 * j)
            tile = dot_cols(branch, first[960 + 128 * j : 960 + 128 * j + width])
            if width < 128:
                tile = jnp.concatenate([tile, jnp.zeros((128, 128 - width), jnp.float32)], axis=1)
            spread_tile(spots, tile, j)
        for g in range(3):
            for h in range(3):
                at = 64 * (3 * g + h)
                grad_turned = dot_cols(first[960 + at : 1024 + at], branch)
                grad_turned = grad_turned.astype(jnp.bfloat16).astype(jnp.float32)
                row = jnp.sum(
                    turned[g, :, 128 * h : 128 * h + 128] * grad_turned, axis=0, keepdims=True
                )
                inner[g, :, 128 * h : 128 * h + 128] = jnp.broadcast_to(row, (8, 128))
        load(layer, 2).wait()

        def one(g, carry):
            attend_back_group(
                g, me, kv, queries, spots, lse, inner, flags, tall, dq, dkv,
                keys, values, scores, lse_rows, inner_rows,
            )
            begin(g)

            @pl.when(g == 0)
            def _():
                for y in order:
                    halve(y)
                if layer == 1:
                    halves[0] = jnp.zeros(halves.shape[1:], jnp.bfloat16)
                w_begin()

            @pl.when(g == 1)
            def _():
                second(0)

            @pl.when(g == 2)
            def _():
                third(0)
                second(1)

            return carry

        lax.fori_loop(0, 3, one, 0)
        if layer == 1:
            load(0, 2).start()
        second(2)
        third(1)
        for g in range(3):
            for h in range(3):
                turn = dq[g, :, 128 * h : 128 * h + 128] * HEAD_SIZE ** (-0.5)
                a, b = turn[:32], turn[32:]
                at = 64 * (3 * g + h)
                gq[at : at + 32] = (a * cosine_t[...] + b * sine_t[...]).astype(jnp.bfloat16)
                gq[at + 32 : at + 64] = (b * cosine_t[...] - a * sine_t[...]).astype(jnp.bfloat16)
        third(2)
        w_second()
        grad_normed = dot_rows(gq[...], first[:576])
        for g in range(3):
            finish(g)
            tile = sums[g]
            tile = (tile * cos - swapped(tile) * sin).astype(jnp.bfloat16)
            gkv[g] = tile
            weights = jnp.concatenate(
                [first[576 + 64 * g : 640 + 64 * g], first[768 + 64 * g : 832 + 64 * g]], axis=0
            )
            grad_normed = grad_normed + jnp.dot(tile, weights, preferred_element_type=jnp.float32)
        if layer == 0:
            swap(0).wait_send()
            first_products(0, lambda j: l_swap(j // 8).start() if j % 8 == 7 else None)
        w_third()
        x = (hidden0, hidden1)[layer][...]
        grad_values, grad_gain = norm_back(grad_normed, x, gains[2 * layer : 2 * layer + 1])
        gain_terms[2 * layer : 2 * layer + 1] = grad_gain
        gr = grad_values + grad_middle
        for g in range(3):
            drain(g)
        if layer == 1:
            w_finish(order, reduced.at[1])
            for peer in peers:
                pl.semaphore_signal(
                    free_sem, inc=1, device_id=device(*peer), device_id_type=MESH
                )
    grad_hidden[...] = gr
    g_begin(gain_terms[...])
    l_begin()
    g_step(0)
    w_finish((1, 2, 3), reduced.at[0])
    g_step(1)
    l_second()
    g_step(2)
    l_third()
    gain_sums[...] = g_step(3)
    l_finish(reduced.at[2])
    g_finish()
    at_front = jnp.broadcast_to(me[0], (48, MODEL_WIDTH)) == 0
    owned[0] = jnp.where(at_front, reduced[2], reduced[0])
    owned[1] = jnp.where(at_front, reduced[0], reduced[1])


def backward_pass(cotangent, hidden0, hidden1, first, whole0, whole1, gains, turns, flags, kept):
    planes, rows = (4, 1536, MODEL_WIDTH), (4, 4, 384, MODEL_WIDTH)
    bf, w = jnp.bfloat16, MODEL_WIDTH
    dma = pltpu.SemaphoreType.DMA
    return pl.pallas_call(
        backward_kernel,
        out_shape=(
            ROWS_F32,
            jax.ShapeDtypeStruct((LAYERS, 48, w), jnp.float32),
            jax.ShapeDtypeStruct((8, w), jnp.float32),
        ),
        in_specs=[VMEM_SPEC] * 3 + [HBM_SPEC] * 4 + [VMEM_SPEC] * 7 + [HBM_SPEC] * len(SAVED),
        out_specs=(VMEM_SPEC,) * 3,
        scratch_shapes=[
            pltpu.VMEM((64 * TILES, 256), bf),
            pltpu.VMEM((64 * TILES, 256), bf),
            pltpu.VMEM((64 * TILES, LANES), jnp.float32),
            pltpu.VMEM((40, LANES), jnp.float32),
            pltpu.VMEM((40, LANES), jnp.float32),
            pltpu.VMEM((3, 4, 4, 2, 128, 128), bf),
            pltpu.VMEM((3, LANES, 256), bf),
            pltpu.VMEM((3, 8, LANES), jnp.float32),
            pltpu.VMEM((3, 64, LANES), jnp.float32),
            pltpu.VMEM((3, 128, 128), jnp.float32),
            pltpu.VMEM((128, FEEDFORWARD_SIZE), bf),
            pltpu.VMEM((128, FEEDFORWARD_SIZE), bf),
            pltpu.VMEM((LAYERS, 1536, w), bf),
            pltpu.VMEM((3, 4, 384, w), bf),
            pltpu.VMEM((w, 128), bf),
            pltpu.VMEM((3, 128, 128), bf),
            pltpu.VMEM((128, w), bf),
            pltpu.VMEM((8, w), jnp.float32),
            pltpu.VMEM((3, 48, w), jnp.float32),
            dma((LAYERS, len(SAVED) + 2)),
            pltpu.SemaphoreType.REGULAR,
        ] + row_reduce_scratch() + weight_reduce_scratch() + [
            pltpu.VMEM((4, 4, 48, w), bf),
            pltpu.VMEM((3, 4, 48, w), bf),
            pltpu.VMEM((4, 48, w), bf),
            pltpu.VMEM((3, 48, w), bf),
            pltpu.VMEM((48, w), bf),
            pltpu.VMEM((3, 48, w), bf),
            dma((4,)),
            dma((4,)),
            dma((2, 2, 3)),
            dma((2, 2, 3)),
            dma((3,)),
            dma((3,)),
            pltpu.VMEM((4, 8, w), jnp.float32),
            pltpu.VMEM((4, 3, 8, w), jnp.float32),
            dma((4, 3)),
            dma((4, 3)),
        ] + [
            pltpu.VMEM(shape if i in BIG else (LAYERS,) + shape, dtype)
            for i, (shape, dtype) in enumerate(SAVED)
        ],
        compiler_params=pltpu.CompilerParams(
            collective_id=2, has_side_effects=True, vmem_limit_bytes=62 * 2**20
        ),
        name="backward_pass",
    )(
        cotangent, hidden0, hidden1, first, whole0.reshape(planes), whole0.reshape(rows),
        whole1.reshape(rows), gains, *turns, *flags, *kept
    )


def turn_tables(places):
    half = HEAD_SIZE // 2
    frequency = 1.0 / THETA ** (2 * jnp.arange(half).astype(jnp.float32) / HEAD_SIZE)
    phases = places.astype(jnp.float32)[:, None] * frequency[None, :]
    cos, sin = jnp.cos(phases), jnp.sin(phases)
    return (
        jnp.concatenate([cos] * 4, 1), jnp.concatenate([-sin, sin] * 2, 1), cos.T, sin.T,
    )


def on_device(hidden_in, positions, params, gains, cotangent):
    places = positions[0]
    block = places[0] // 64
    turn = block >= 32
    block = jnp.minimum(block, 63 - block)

    def lo_first(rows):
        return jnp.where(turn, jnp.concatenate([rows[64:], rows[:64]], 0), rows)

    index = lax.axis_index("fsdp") * 32 + lax.axis_index("ctx")
    spaced = jnp.zeros((LAYERS, 2 * MODEL_WIDTH), jnp.float32)
    spaced = lax.dynamic_update_slice(spaced, gains.astype(jnp.float32), (0, index * 9))
    spaced = spaced.reshape(2 * LAYERS, MODEL_WIDTH)
    number = block.astype(jnp.float32)
    lane = jnp.arange(MODEL_WIDTH)[None]
    numbers = jnp.where(lane == lax.axis_index("ctx"), number, 0.0)
    extra = jnp.concatenate([spaced, numbers, jnp.zeros((3, MODEL_WIDTH), jnp.float32)], 0)
    turns = turn_tables(lo_first(places))
    hidden = lo_first(hidden_in[0]).astype(jnp.float32)
    main, kept = forward_pass(hidden, params, extra, jnp.full((8, 128), number), turns)
    hidden_in, hidden = hidden, main[0]
    gain_rows, flags = main[2], main[3:5]
    output_rows = lo_first(hidden.astype(jnp.bfloat16))
    grad_hidden = lo_first(cotangent[0]).astype(jnp.float32)
    grad_hidden, owned, gain_sums = backward_pass(
        grad_hidden, hidden_in, main[1], main[5], *main[6:8], gain_rows, turns, flags, kept
    )
    gain_sums = gain_sums[:4].reshape(LAYERS, 2 * MODEL_WIDTH)
    owned_gains = lax.dynamic_slice(gain_sums, (0, index * 9), (LAYERS, 9))
    return (
        output_rows[None],
        lo_first(grad_hidden)[None],
        owned,
        owned_gains,
    )


def solution(mesh):
    return jax.shard_map(
        on_device,
        mesh=mesh,
        in_specs=(
            P("fsdp", "ctx", None),
            P("fsdp", "ctx"),
            P(None, ("fsdp", "ctx"), None),
            P(None, ("fsdp", "ctx")),
            P("fsdp", "ctx", None),
        ),
        out_specs=(
            P("fsdp", "ctx", None),
            P("fsdp", "ctx", None),
            P(None, ("fsdp", "ctx"), None),
            P(None, ("fsdp", "ctx")),
        ),
        check_vma=False,
    )
```

```python
import functools

import jax
import jax.numpy as jnp
from jax import lax
from jax.experimental import pallas as pl
from jax.experimental.pallas import tpu as pltpu
from jax.sharding import PartitionSpec as P

MODEL_WIDTH = 576
FEEDFORWARD_SIZE = 1536
QUERY_HEADS = 9
KEY_VALUE_HEADS = 3
HEAD_SIZE = 64
LAYERS = 2
SEQ_LEN = 4096

EPSILON = 1e-05
THETA = 100000.0
MASKED = -1e30
MESH = pl.DeviceIdType.MESH
RING = 4


def place():
    t = lax.axis_index("ctx")
    return (lax.axis_index("fsdp"), t // 8, (t // 2) % 4, t % 2)


def device(y, x, z, c):
    return (y, x * 8 + z * 2 + c)


def moved(me, axis, step):
    other = list(me)
    other[axis] = (me[axis] + step) % RING
    return tuple(other)


def sibling(me):
    return (me[0], me[1], me[2], 1 - me[3])


def greet(peers):
    barrier = pltpu.get_barrier_semaphore()
    for peer in peers:
        pl.semaphore_signal(barrier, inc=1, device_id=device(*peer), device_id_type=MESH)
    pl.semaphore_wait(barrier, len(peers))


TILES = 33
CHUNK = 11
LANES = 384


def head_lanes():
    return lax.broadcasted_iota(jnp.int32, (1, LANES), 1) % 128 >= 64


def roll_heads(rows):
    return jnp.concatenate(
        [pltpu.roll(rows[:, 128 * h : 128 * h + 128], 64, 1) for h in range(3)], axis=1
    )


def pack_tile(lo, hi, keep_lo, use_a, use_b):
    lo = lo.astype(jnp.float32)
    hi = hi.astype(jnp.float32)
    zero = jnp.zeros_like(lo)
    a = jnp.where(use_a, lo, zero)
    b = jnp.where(use_b, hi, zero)
    if not keep_lo:
        lo = zero
    left = lax.broadcasted_iota(jnp.int32, (64, 128), 1) < 64
    keys = [jnp.where(left, lo, pltpu.roll(a, 64, 1)), jnp.where(left, b, zero)]
    values = [jnp.where(left, pltpu.roll(lo, 64, 1), a), jnp.where(left, pltpu.roll(b, 64, 1), zero)]
    return (
        jnp.concatenate(keys, axis=1).astype(jnp.bfloat16),
        jnp.concatenate(values, axis=1).astype(jnp.bfloat16),
    )


def pack_all(g, me, kv, tall, keys, values):
    def one(t, carry):
        at = kv[g, t // 8, (t // 2) % 4, t % 2]
        use_a = jnp.broadcast_to(tall[t][:1] > 0.5, (64, 128))
        k, v = pack_tile(at[:64], at[64:], True, use_a, jnp.logical_not(use_a))
        spot = pl.ds(pl.multiple_of(t * 64, 64), 64)
        keys[spot] = k
        values[spot] = v
        return carry

    lax.fori_loop(0, TILES - 1, one, 0, unroll=4)
    yes = jnp.full((64, 128), True)
    at = kv[g, me[1], me[2], me[3]]
    k, v = pack_tile(at[:64], at[64:], False, yes, jnp.logical_not(yes))
    keys[pl.ds(64 * (TILES - 1), 64)] = k
    values[pl.ds(64 * (TILES - 1), 64)] = v


def dot_cols(left, right):
    return lax.dot_general(
        left, right, (((1,), (1,)), ((), ())), preferred_element_type=jnp.float32
    )


def dot_rows(left, right):
    return lax.dot_general(
        left, right, (((0,), (0,)), ((), ())), preferred_element_type=jnp.float32
    )


def score_all(keys, queries, scores):
    for c in range(TILES // CHUNK):
        rows = pl.ds(64 * CHUNK * c, 64 * CHUNK)
        scores[rows] = dot_cols(keys[rows], queries)
    at = lax.broadcasted_iota(jnp.int32, (64, LANES), 0)
    lane = lax.broadcasted_iota(jnp.int32, (64, LANES), 1) % 128
    causal = jnp.logical_and(lane < 64, at <= lane)
    mine = pl.ds(pl.multiple_of(lax.axis_index("ctx") * 64, 64), 64)
    scores[mine] = jnp.where(jnp.logical_or(lane >= 64, causal), scores[mine], MASKED)
    last = pl.ds(64 * (TILES - 1), 64)
    scores[last] = jnp.where(causal, scores[last], MASKED)


def tile_rows(flags, row):
    crossed = jnp.where(head_lanes(), row, roll_heads(row))
    return jnp.where(flags[...] > 0.5, row, crossed)


def joined(rows, flags, merge, empty):
    straight = jnp.where(jnp.logical_or(head_lanes(), flags[...] > 0.5), rows, empty)
    crossed = jnp.where(jnp.logical_or(head_lanes(), flags[...] > 0.5), empty, rows)
    down = jnp.max if merge is jnp.maximum else jnp.sum
    one = down(straight, axis=0, keepdims=True)
    other = roll_heads(down(crossed, axis=0, keepdims=True))
    return merge(one, other)


def fold_lanes(product):
    return jnp.where(
        head_lanes(), product[:64] + roll_heads(product[128:192]), product[64:128]
    )


def attend_group(
    g, me, kv, queries, flags, tall, out, lse, keys, values, scores, rows, between
):
    pack_all(g, me, kv, tall, keys, values)
    score_all(keys, queries[g], scores)
    between()
    rows[...] = jnp.full(rows.shape, MASKED, jnp.float32)

    for t in range(TILES):
        rows[pl.ds(t, 1)] = jnp.max(scores[pl.ds(64 * t, 64)], axis=0, keepdims=True)
    top = joined(rows[...], flags, jnp.maximum, MASKED)
    rows[...] = tile_rows(flags, top)
    total = jnp.zeros((256, LANES), jnp.float32)
    sums = []
    for c in range(TILES // CHUNK):
        parts = []
        for i in range(CHUNK):
            t = c * CHUNK + i
            raised = jnp.exp(scores[pl.ds(64 * t, 64)] - rows[pl.ds(t, 1)])
            sums.append(jnp.sum(raised, axis=0, keepdims=True))
            parts.append(raised.astype(jnp.bfloat16))
        spot = pl.ds(64 * CHUNK * c, 64 * CHUNK)
        total = total + dot_rows(values[spot], jnp.concatenate(parts, axis=0))
    rows[...] = jnp.zeros(rows.shape, jnp.float32)
    for t in range(TILES):
        rows[pl.ds(t, 1)] = sums[t]
    amount = joined(rows[...], flags, jnp.add, 0.0)
    out[g] = fold_lanes(total) / amount
    lse[g] = jnp.broadcast_to(top + jnp.log(amount), (8, LANES))


def attend_back_group(
    g, me, kv, queries, grads, lse, inner, flags, tall, dq, dkv,
    keys, values, scores, lse_rows, inner_rows,
):
    pack_all(g, me, kv, tall, keys, values)
    score_all(keys, queries[g], scores)
    lse_rows[...] = tile_rows(flags, lse[g][:1])
    inner_rows[...] = tile_rows(flags, inner[g][:1])
    total = jnp.zeros((256, LANES), jnp.float32)
    for c in range(TILES // CHUNK):
        spot = pl.ds(64 * CHUNK * c, 64 * CHUNK)
        grad_probs = dot_cols(values[spot], grads[g])
        probs, rest = [], []
        for i in range(CHUNK):
            t = c * CHUNK + i
            p = jnp.exp(scores[pl.ds(64 * t, 64)] - lse_rows[pl.ds(t, 1)])
            probs.append(p.astype(jnp.bfloat16))
            rest.append(
                (p * (grad_probs[64 * i : 64 * i + 64] - inner_rows[pl.ds(t, 1)])).astype(jnp.bfloat16)
            )
        probs = jnp.concatenate(probs, axis=0)
        rest = jnp.concatenate(rest, axis=0)
        total = total + dot_rows(keys[spot], rest)
        to_keys = jnp.dot(rest, queries[g], preferred_element_type=jnp.float32)
        to_values = jnp.dot(probs, grads[g], preferred_element_type=jnp.float32)
        left = lax.broadcasted_iota(jnp.int32, (64, 128), 1) < 64
        for i in range(CHUNK):
            t = c * CHUNK + i
            k0 = to_keys[64 * i : 64 * i + 64, :128]
            k1 = to_keys[64 * i : 64 * i + 64, 128:]
            v0 = to_values[64 * i : 64 * i + 64, :128]
            v1 = to_values[64 * i : 64 * i + 64, 128:]
            a = jnp.where(left, pltpu.roll(k0, 64, 1), v0)
            if t < TILES - 1:
                use_a = jnp.broadcast_to(tall[t][:1] > 0.5, (64, 128))
                lo = jnp.where(left, k0, pltpu.roll(v0, 64, 1)) + jnp.where(use_a, a, 0.0)
                hi = jnp.where(use_a, 0.0, jnp.where(left, k1, pltpu.roll(v1, 64, 1)))
                dkv[g, t // 8, (t // 2) % 4, t % 2, :64] = lo.astype(jnp.bfloat16)
                dkv[g, t // 8, (t // 2) % 4, t % 2, 64:] = hi.astype(jnp.bfloat16)
            else:
                spot = (g, me[1], me[2], me[3], pl.ds(0, 64))
                dkv[spot] = (dkv[spot].astype(jnp.float32) + a).astype(jnp.bfloat16)
    dq[g] = fold_lanes(total)


def weight_gather(
    me, source, whole, sends, recvs, swap_sends, swap_recvs, own_sem, skip=False
):
    def region(k, phase, at, core):
        index = [at[0], at[1], at[2]]
        for i in range(phase):
            axis = (k + i) % 3
            index[axis] = pl.ds(1, 3) if skip and axis == 0 else slice(None)
        return whole.at[tuple(index) + (core, pl.ds(16 * k, 16))]

    def has(k, phase, y):
        return None if not skip or phase > -k % 3 else y != 0

    def copy(src, dst, k, phase, s):
        return pltpu.make_async_remote_copy(
            src_ref=src, dst_ref=dst,
            send_sem=sends.at[k, phase, s - 1], recv_sem=recvs.at[k, phase, s - 1],
            device_id=device(*moved(me, (k + phase) % 3, s)), device_id_type=MESH)

    def send(k, phase, s, what):
        spot = region(k, phase, me, me[3])
        made = copy(spot if phase else source.at[pl.ds(16 * k, 16)], spot, k, phase, s)
        only(has(k, phase, me[0]), made.start if what == "start" else made.wait_send)

    def land(k, phase, s):
        there = moved(me, (k + phase) % 3, -s)
        spot = region(k, phase, there, me[3])
        only(has(k, phase, there[0]), copy(spot, spot, k, phase, s).wait_recv)

    def relay_copy(k, i, at, what):
        axis = (k + 2) % 3
        index = [at[0], at[1], at[2]]
        for j in (k, (k + 1) % 3):
            index[j] = pl.ds(1, 3) if skip and j == 0 else slice(None)
        index[1 if k < 2 else 2] = pl.ds(2 * i, 2)
        spot = whole.at[tuple(index) + (me[3], pl.ds(16 * k, 16))]
        made = pltpu.make_async_remote_copy(
            src_ref=spot, dst_ref=spot,
            send_sem=sends.at[k, 2, 1 + 2 * i], recv_sem=recvs.at[k, 2, 1 + 2 * i],
            device_id=device(*moved(me, axis, 3 if i else 1)), device_id_type=MESH)
        act = {"start": made.start, "sent": made.wait_send, "landed": made.wait_recv}
        only(has(k, 2, at[0]), act[what])

    def relayed(k, i):
        return moved(me, (k + 2) % 3, 1 if i else 3)

    def swap(k, s, core, what):
        there = moved(me, (k + 2) % 3, -s)
        spot = region(k, 2, there, core)
        made = pltpu.make_async_remote_copy(
            src_ref=spot, dst_ref=spot,
            send_sem=swap_sends.at[k, s], recv_sem=swap_recvs.at[k, s],
            device_id=device(*sibling(me)), device_id_type=MESH)
        act = {"start": made.start, "sent": made.wait_send, "landed": made.wait_recv}
        only(has(k, 2, there[0]), act[what])

    def begin():
        own = pltpu.make_async_copy(source, whole.at[me], own_sem)
        own.start()
        for k in range(3):
            for s in (2, 1, 3):
                send(k, 0, s, "start")
        own.wait()

    def forward(phase):
        for k in range(3):
            for s in (1, 3, 2):
                land(k, phase - 1, s)
            for s in (1, 3) if phase == 2 else (2, 1, 3):
                send(k, phase, s, "start")
            if phase == 2:
                swap(k, 0, me[3], "start")

    def relay():
        for i, s in enumerate((1, 3)):
            for k in range(3):
                land(k, 2, s)
                relay_copy(k, i, relayed(k, i), "start")
                swap(k, s, me[3], "start")

    def exchange():
        for k in range(3):
            for i in range(2):
                relay_copy(k, i, moved(me, (k + 2) % 3, 2), "landed")
            swap(k, 2, me[3], "start")

    def arrive():
        for k in range(3):
            for s in range(4):
                swap(k, s, 1 - me[3], "landed")

    def finish():
        for k in range(3):
            for phase in range(3):
                for s in (1, 3) if phase == 2 else (1, 2, 3):
                    send(k, phase, s, "sent")
            for i in range(2):
                relay_copy(k, i, relayed(k, i), "sent")
            for s in range(4):
                swap(k, s, me[3], "sent")

    return begin, forward, relay, exchange, arrive, finish


def only(condition, act):
    if condition is None:
        act()
    else:
        pl.when(condition)(act)


WEIGHT_GATHER_SEMS = [
    pltpu.SemaphoreType.DMA((3, 3, 4)),
    pltpu.SemaphoreType.DMA((3, 3, 4)),
    pltpu.SemaphoreType.DMA((3, 4)),
    pltpu.SemaphoreType.DMA((3, 4)),
    pltpu.SemaphoreType.DMA,
]
WHOLE = jax.ShapeDtypeStruct((4, 4, 4, 2, 48, MODEL_WIDTH), jnp.bfloat16)
ALL_PEERS = tuple((a, s) for a in range(3) for s in (1, 2, 3))


def greet_all(me):
    greet([moved(me, a, s) for a, s in ALL_PEERS] + [sibling(me)])


def row_gather(me, own, kv, sends, recvs, swap_sends, swap_recvs, own_sems):
    def region(g, k, phase, at, core):
        index = [at[1], at[2]]
        if phase >= 1:
            index[1 - k] = slice(None)
        return kv.at[(g,) + tuple(index) + (core, pl.ds(64 * k, 64))]

    def axis_of(k, phase):
        return 1 + (1 - k + phase) % 2

    def copy(src, dst, g, k, phase, s):
        return pltpu.make_async_remote_copy(
            src_ref=src, dst_ref=dst,
            send_sem=sends.at[g, k, phase, s - 1], recv_sem=recvs.at[g, k, phase, s - 1],
            device_id=device(*moved(me, axis_of(k, phase), s)), device_id_type=MESH)

    def send(g, k, phase, s):
        spot = region(g, k, phase, me, me[3])
        return copy(spot if phase else own.at[g, pl.ds(64 * k, 64)], spot, g, k, phase, s)

    def landed(g, k, phase, s):
        spot = region(g, k, phase, moved(me, axis_of(k, phase), -s), me[3])
        return copy(spot, spot, g, k, phase, s)

    def relay_copy(g, k, i, at):
        index = [at[1], at[2]]
        index[1 - k] = pl.ds(2 * i, 2)
        spot = kv.at[(g,) + tuple(index) + (me[3], pl.ds(64 * k, 64))]
        return pltpu.make_async_remote_copy(
            src_ref=spot, dst_ref=spot,
            send_sem=sends.at[g, k, 1, 1 + 2 * i], recv_sem=recvs.at[g, k, 1, 1 + 2 * i],
            device_id=device(*moved(me, axis_of(k, 1), 3 if i else 1)), device_id_type=MESH)

    def relayed(k, i):
        return moved(me, axis_of(k, 1), 1 if i else 3)

    def swap(g, k, s, core):
        spot = region(g, k, 1, moved(me, axis_of(k, 1), -s), core)
        return pltpu.make_async_remote_copy(
            src_ref=spot, dst_ref=spot,
            send_sem=swap_sends.at[g, k, s], recv_sem=swap_recvs.at[g, k, s],
            device_id=device(*sibling(me)), device_id_type=MESH)

    def keep(g):
        return pltpu.make_async_copy(own.at[g], kv.at[g, me[1], me[2], me[3]], own_sems.at[g])

    def begin(g):
        for s in (2, 1, 3):
            for k in range(2):
                send(g, k, 0, s).start()
        keep(g).start()

    def forward(g):
        keep(g).wait()
        for k in range(2):
            for s in (1, 3, 2):
                landed(g, k, 0, s).wait_recv()
            for s in (1, 3):
                send(g, k, 1, s).start()
            swap(g, k, 0, me[3]).start()

    def relay(g):
        for i, s in enumerate((1, 3)):
            for k in range(2):
                landed(g, k, 1, s).wait_recv()
                relay_copy(g, k, i, relayed(k, i)).start()
                swap(g, k, s, me[3]).start()

    def arrive(g):
        for k in range(2):
            for i in range(2):
                relay_copy(g, k, i, moved(me, axis_of(k, 1), 2)).wait_recv()
            swap(g, k, 2, me[3]).start()
        for k in range(2):
            for s in range(4):
                swap(g, k, s, 1 - me[3]).wait_recv()

    def finish(g):
        for k in range(2):
            for phase in range(2):
                for s in (1, 3) if phase else (1, 2, 3):
                    send(g, k, phase, s).wait_send()
            for i in range(2):
                relay_copy(g, k, i, relayed(k, i)).wait_send()
            for s in range(4):
                swap(g, k, s, me[3]).wait_send()

    return begin, forward, relay, arrive, finish


def weight_reduce(
    me, grads, halves, landed_a, sum_a, landed_b, sum_b, landed_c,
    swap_sends, swap_recvs, sends, recvs,
):
    axes = ((2, 1, 0), (0, 2, 1), (1, 0, 2))

    def swap(y):
        return pltpu.make_async_remote_copy(
            src_ref=grads.at[y, :, :, 1 - me[3]], dst_ref=halves.at[y],
            send_sem=swap_sends.at[y], recv_sem=swap_recvs.at[y],
            device_id=device(*sibling(me)), device_id_type=MESH)

    def copy(stage, src, dst, k, s, peer):
        return pltpu.make_async_remote_copy(
            src_ref=src, dst_ref=dst,
            send_sem=sends.at[stage, k, s - 1], recv_sem=recvs.at[stage, k, s - 1],
            device_id=device(*peer), device_id_type=MESH)

    def send(stage, k, s):
        axis = axes[k][stage]
        peer = moved(me, axis, s)
        if stage == 0:
            index = [slice(None)] * 3
            index[axis] = peer[axis]
            return copy(0, halves.at[tuple(index) + (pl.ds(16 * k, 16),)], landed_a.at[k, s - 1], k, s, peer)
        if stage == 1:
            index = [slice(None)] * 2
            index[sorted(axes[k][1:]).index(axis)] = peer[axis]
            return copy(1, sum_a.at[(k,) + tuple(index)], landed_b.at[k, s - 1], k, s, peer)
        return copy(2, sum_b.at[k, peer[axis]], landed_c.at[k, s - 1], k, s, peer)

    def halve(y):
        swap(y).wait_recv()
        for x in range(4):
            for z in range(4):
                halves[y, x, z] = (
                    grads[y, x, z, me[3]].astype(jnp.float32) + halves[y, x, z].astype(jnp.float32)
                ).astype(jnp.bfloat16)

    def begin():
        for k in range(3):
            for s in (2, 1, 3):
                send(0, k, s).start()

    def second():
        for k in range(3):
            for s in (1, 3, 2):
                send(0, k, s).wait_recv()
            axis = axes[k][0]
            for i in range(4):
                for j in range(4):
                    at = [i, j]
                    at.insert(axis, me[axis])
                    total = halves[tuple(at) + (pl.ds(16 * k, 16),)].astype(jnp.float32)
                    for s in range(3):
                        total = total + landed_a[k, s, i, j].astype(jnp.float32)
                    sum_a[k, i, j] = total.astype(jnp.bfloat16)
            for s in (2, 1, 3):
                send(1, k, s).start()

    def third():
        for k in range(3):
            for s in (1, 3, 2):
                send(1, k, s).wait_recv()
            rest = sorted(axes[k][1:])
            for i in range(4):
                at = [i, i]
                at[rest.index(axes[k][1])] = me[axes[k][1]]
                total = sum_a[(k,) + tuple(at)].astype(jnp.float32)
                for s in range(3):
                    total = total + landed_b[k, s, i].astype(jnp.float32)
                sum_b[k, i] = total.astype(jnp.bfloat16)
            for s in (2, 1, 3):
                send(2, k, s).start()

    def finish(planes, out):
        for k in range(3):
            for s in (1, 3, 2):
                send(2, k, s).wait_recv()
            total = sum_b[k, me[axes[k][2]]].astype(jnp.float32)
            for s in range(3):
                total = total + landed_c[k, s].astype(jnp.float32)
            out[pl.ds(16 * k, 16)] = total
        for y in planes:
            swap(y).wait_send()
        for stage in range(3):
            for k in range(3):
                for s in (1, 2, 3):
                    send(stage, k, s).wait_send()

    return swap, halve, begin, second, third, finish


def weight_reduce_scratch():
    bf, w = jnp.bfloat16, MODEL_WIDTH
    return [
        pltpu.VMEM((4, 4, 4, 2, 48, w), bf),
        pltpu.VMEM((4, 4, 4, 48, w), bf),
        pltpu.VMEM((3, 3, 4, 4, 16, w), bf),
        pltpu.VMEM((3, 4, 4, 16, w), bf),
        pltpu.VMEM((3, 3, 4, 16, w), bf),
        pltpu.VMEM((3, 4, 16, w), bf),
        pltpu.VMEM((3, 3, 16, w), bf),
        pltpu.SemaphoreType.DMA((4,)),
        pltpu.SemaphoreType.DMA((4,)),
        pltpu.SemaphoreType.DMA((3, 3, 3)),
        pltpu.SemaphoreType.DMA((3, 3, 3)),
    ]


def row_reduce(
    me, terms, out, halves, landed_a, sum_a, landed_b, swap_sends, swap_recvs, sends, recvs
):
    axes = ((2, 1), (1, 2))

    def swap(g):
        return pltpu.make_async_remote_copy(
            src_ref=terms.at[g, :, :, 1 - me[3]], dst_ref=halves.at[g],
            send_sem=swap_sends.at[g], recv_sem=swap_recvs.at[g],
            device_id=device(*sibling(me)), device_id_type=MESH)

    def send(stage, g, k, s):
        axis = axes[k][stage]
        peer = moved(me, axis, s)
        if stage == 0:
            index = [slice(None)] * 2
            index[axis - 1] = peer[axis]
            src = halves.at[(g,) + tuple(index) + (pl.ds(64 * k, 64),)]
            dst = landed_a.at[g, k, s - 1]
        else:
            src = sum_a.at[g, k, peer[axis]]
            dst = landed_b.at[g, k, s - 1]
        return pltpu.make_async_remote_copy(
            src_ref=src, dst_ref=dst,
            send_sem=sends.at[stage, g, k, s - 1], recv_sem=recvs.at[stage, g, k, s - 1],
            device_id=device(*peer), device_id_type=MESH)

    def begin(g):
        swap(g).start()

    def second(g):
        swap(g).wait_recv()
        for x in range(4):
            for z in range(4):
                halves[g, x, z] = (
                    terms[g, x, z, me[3]].astype(jnp.float32) + halves[g, x, z].astype(jnp.float32)
                ).astype(jnp.bfloat16)
        for s in (2, 1, 3):
            for k in range(2):
                send(0, g, k, s).start()

    def third(g):
        for k in range(2):
            for s in (1, 3, 2):
                send(0, g, k, s).wait_recv()
            axis = axes[k][0]
            for i in range(4):
                at = [i]
                at.insert(axis - 1, me[axis])
                total = halves[(g,) + tuple(at) + (pl.ds(64 * k, 64),)].astype(jnp.float32)
                for s in range(3):
                    total = total + landed_a[g, k, s, i].astype(jnp.float32)
                sum_a[g, k, i] = total.astype(jnp.bfloat16)
            for s in (2, 1, 3):
                send(1, g, k, s).start()

    def finish(g):
        for k in range(2):
            for s in (1, 3, 2):
                send(1, g, k, s).wait_recv()
            total = sum_a[g, k, me[axes[k][1]]].astype(jnp.float32)
            for s in range(3):
                total = total + landed_b[g, k, s].astype(jnp.float32)
            out[g, pl.ds(64 * k, 64)] = total

    def drain(g):
        swap(g).wait_send()
        for stage in range(2):
            for k in range(2):
                for s in (1, 2, 3):
                    send(stage, g, k, s).wait_send()

    return begin, second, third, finish, drain


def row_reduce_scratch():
    bf = jnp.bfloat16
    return [
        pltpu.VMEM((3, 4, 4, 128, 128), bf),
        pltpu.VMEM((3, 2, 3, 4, 64, 128), bf),
        pltpu.VMEM((3, 2, 4, 64, 128), bf),
        pltpu.VMEM((3, 2, 3, 64, 128), bf),
        pltpu.SemaphoreType.DMA((3,)),
        pltpu.SemaphoreType.DMA((3,)),
        pltpu.SemaphoreType.DMA((2, 3, 2, 3)),
        pltpu.SemaphoreType.DMA((2, 3, 2, 3)),
    ]


def left_lanes():
    return lax.broadcasted_iota(jnp.int32, (128, 128), 1) < 64


def swapped(tile):
    low = lax.broadcasted_iota(jnp.int32, tile.shape, 1) % 64 < 32
    return jnp.where(low, pltpu.roll(tile, 96, 1), pltpu.roll(tile, 32, 1))


def spread_tile(spots, tile, j):
    other = pltpu.roll(tile, 64, 1)
    left = left_lanes()
    for i in range(2):
        head = 2 * j + i
        if head >= QUERY_HEADS:
            continue
        a = jnp.where(left, tile if i == 0 else other, 0.0).astype(jnp.bfloat16)
        b = jnp.where(left, 0.0, other if i == 0 else tile).astype(jnp.bfloat16)
        g, at = head // 3, 128 * (head % 3)
        spots[g, at : at + 64, :128] = b[:64]
        spots[g, at : at + 64, 128:] = a[64:]
        spots[g, at + 64 : at + 128, :128] = a[64:]
        spots[g, at + 64 : at + 128, 128:] = jnp.zeros((64, 128), jnp.bfloat16)


def group_weights(first, g):
    return jnp.concatenate(
        [first[0, 576 + 64 * g : 640 + 64 * g], first[0, 768 + 64 * g : 832 + 64 * g]], axis=0
    )


def inverse_root(values):
    return lax.rsqrt(jnp.mean(values * values, axis=-1, keepdims=True) + EPSILON)


HALF_ROWS = ((0, 32), (32, 16))


SAVED = (
    ((128, MODEL_WIDTH), jnp.bfloat16),
    ((3, LANES, 256), jnp.bfloat16),
    ((3, 4, 4, 2, 128, 128), jnp.bfloat16),
    ((3, 64, LANES), jnp.float32),
    ((3, 8, LANES), jnp.float32),
    ((MODEL_WIDTH, 128), jnp.bfloat16),
    ((128, MODEL_WIDTH), jnp.float32),
    ((128, MODEL_WIDTH), jnp.bfloat16),
    ((128, FEEDFORWARD_SIZE), jnp.float32),
    ((128, FEEDFORWARD_SIZE), jnp.float32),
    ((128, FEEDFORWARD_SIZE), jnp.bfloat16),
    ((128, MODEL_WIDTH), jnp.float32),
)


def sum_everywhere(me, parts, landed, sends, recvs):
    axes = (None, 2, 1, 0)

    def copy(stage, s):
        peer = sibling(me) if stage == 0 else moved(me, axes[stage], s)
        return pltpu.make_async_remote_copy(
            src_ref=parts.at[stage], dst_ref=landed.at[stage, s - 1],
            send_sem=sends.at[stage, s - 1], recv_sem=recvs.at[stage, s - 1],
            device_id=device(*peer), device_id_type=MESH)

    def steps(stage):
        return (1,) if stage == 0 else (2, 1, 3)

    def begin(value):
        parts[0] = value
        copy(0, 1).start()

    def step(stage):
        total = parts[stage]
        for s in steps(stage):
            copy(stage, s).wait_recv()
            total = total + landed[stage, s - 1]
        if stage < 3:
            parts[stage + 1] = total
            for s in steps(stage + 1):
                copy(stage + 1, s).start()
        return total

    def finish():
        for stage in range(4):
            for s in steps(stage):
                copy(stage, s).wait_send()

    return begin, step, finish


def first_gather(me, source, whole, stage, sends, recvs, swap_sends, swap_recvs, y_sends, y_recvs, own_sems):
    def along_y(s, y):
        return pltpu.make_async_remote_copy(
            src_ref=source, dst_ref=stage.at[y],
            send_sem=y_sends.at[s - 1], recv_sem=y_recvs.at[s - 1],
            device_id=device(*moved(me, 0, s)), device_id_type=MESH)

    def region(k, phase, at, core):
        index = [at[1], at[2]]
        if phase:
            index[k] = slice(None)
        return whole.at[tuple(index) + (core, pl.ds(*HALF_ROWS[k]))]

    def copy(src, dst, k, phase, s):
        return pltpu.make_async_remote_copy(
            src_ref=src, dst_ref=dst,
            send_sem=sends.at[k, phase, s - 1], recv_sem=recvs.at[k, phase, s - 1],
            device_id=device(*moved(me, 1 + (k + phase) % 2, s)), device_id_type=MESH)

    def send(k, phase, s):
        spot = region(k, phase, me, me[3])
        return copy(spot if phase else stage.at[0, pl.ds(*HALF_ROWS[k])], spot, k, phase, s)

    def landed(k, phase, s):
        spot = region(k, phase, moved(me, 1 + (k + phase) % 2, -s), me[3])
        return copy(spot, spot, k, phase, s)

    def swap(k, s, core):
        spot = region(k, 1, moved(me, 1 + (k + 1) % 2, -s), core)
        return pltpu.make_async_remote_copy(
            src_ref=spot, dst_ref=spot,
            send_sem=swap_sends.at[k, s], recv_sem=swap_recvs.at[k, s],
            device_id=device(*sibling(me)), device_id_type=MESH)

    own = pltpu.make_async_copy(source, stage.at[me[0]], own_sems.at[0])
    keep = pltpu.make_async_copy(stage.at[0], whole.at[me[1], me[2], me[3]], own_sems.at[1])

    def begin():
        for s in (2, 1, 3):
            along_y(s, me[0]).start()
        own.start()

    def spread():
        own.wait()
        for s in (1, 3, 2):
            along_y(s, (me[0] - s) % RING).wait_recv()
        for k in range(2):
            for s in (2, 1, 3):
                send(k, 0, s).start()
        keep.start()

    def forward():
        keep.wait()
        for k in range(2):
            for s in (1, 3, 2):
                landed(k, 0, s).wait_recv()
            for s in (2, 1, 3):
                send(k, 1, s).start()
            swap(k, 0, me[3]).start()

    def exchange():
        for s in (1, 3, 2):
            for k in (1, 0):
                landed(k, 1, s).wait_recv()
                swap(k, s, me[3]).start()

    def arrive():
        for k in range(2):
            for s in range(4):
                swap(k, s, 1 - me[3]).wait_recv()

    def finish():
        for s in (1, 2, 3):
            along_y(s, me[0]).wait_send()
        for k in range(2):
            for phase in range(2):
                for s in (1, 2, 3):
                    send(k, phase, s).wait_send()
            for s in range(4):
                swap(k, s, me[3]).wait_send()

    return begin, spread, forward, exchange, arrive, finish


def find_flags(blocks, number, flags, tall):
    column = jnp.broadcast_to(blocks, (128, 128)).T[:40]
    place_of = lax.broadcasted_iota(jnp.int32, (40, 128), 0)
    before = jnp.logical_or(place_of >= TILES - 1, column < number[:, :128])
    before = jnp.where(before, 1.0, 0.0)
    flags[...] = jnp.concatenate([before] * 3, axis=1)
    for t in range(40):
        tall[t] = jnp.broadcast_to(before[t : t + 1], (8, 128))


def own_block(positions):
    start = jnp.broadcast_to(positions[:, :1], (1, MODEL_WIDTH))
    block = lax.shift_right_logical(start, jnp.full(start.shape, 6, jnp.int32))
    return jnp.minimum(block, 63 - block).astype(jnp.float32), jnp.where(block >= 32, 1.0, 0.0)


def wide_turns(cosine_t, sine_t):
    cos, sin = cosine_t[...], sine_t[...]
    return jnp.concatenate([cos] * 4, axis=0).T, jnp.concatenate([-sin, sin] * 2, axis=0).T


def in_turn(rows, turn):
    other = jnp.concatenate([rows[64:], rows[:64]], axis=0)
    return jnp.where(jnp.broadcast_to(turn, rows.shape) > 0.5, other, rows)


def flatten(first, planes):
    for j in range(32):
        first[0, 48 * j : 48 * j + 48] = planes[j // 8, (j // 2) % 4, j % 2]


def forward_kernel(
    hidden, params, gain_part, positions, cosine_t, sine_t,
    result, gains, flags, tall, first_out, whole0_out, whole1_out, *refs
):
    count = len(SAVED)
    saved_out, saved = refs[:count], refs[count : 2 * count]
    (
        keys, values, scores, rows, first, planes, stage, mix, whole0, whole1, parts, landed, owns,
        spaced,
    ) = refs[2 * count : 2 * count + 14]
    sems = refs[2 * count + 14 :]
    save_sems, row_sems, first_sems = sems[0], sems[1:6], sems[6:13]
    sum_sems, mix_sem = sems[13:15], sems[15]
    weight_sems = (sems[16:21], sems[21:26])
    me = place()
    for y in range(2):
        @pl.when((me[0] == 0) == (y == 0))
        def _():
            pltpu.make_async_copy(params.at[1 - y], mix, mix_sem).start()
    number, turn = own_block(positions)
    x = in_turn(hidden[...].astype(jnp.float32).T, turn)
    scaled = x * inverse_root(x)
    greet_all(me)
    g_begin, g_step, g_finish = sum_everywhere(me, parts, landed, *sum_sems)
    f_begin, f_spread, f_forward, f_exchange, f_arrive, f_finish = first_gather(
        me, params.at[0], planes, stage, *first_sems
    )
    weights = (
        weight_gather(me, mix, whole0, *weight_sems[0]),
        weight_gather(me, params.at[1], whole1, *weight_sems[1], skip=True),
    )
    saves = []

    def save(layer, i):
        copy = pltpu.make_async_copy(
            saved[i].at[layer], saved_out[i].at[layer], save_sems.at[layer, i]
        )
        copy.start()
        saves.append(copy)

    def save_as(i, src, dst):
        copy = pltpu.make_async_copy(src, dst, save_sems.at[2, i])
        copy.start()
        saves.append(copy)

    f_begin()
    spaced[...] = jnp.zeros(spaced.shape, jnp.float32)
    lane = lax.broadcasted_iota(jnp.int32, (1, MODEL_WIDTH), 1)
    at = 9 * (32 * lax.axis_index("fsdp") + lax.axis_index("ctx"))
    own_gains = gain_part[...].astype(jnp.float32)
    for r in range(2 * LAYERS):
        row = jnp.zeros((1, MODEL_WIDTH), jnp.float32)
        for j in range(9):
            value = jnp.broadcast_to(own_gains[r // 2 : r // 2 + 1, j : j + 1], row.shape)
            row = jnp.where(lane + MODEL_WIDTH * (r % 2) == at + j, value, row)
        spaced[r : r + 1] = row
    spaced[4:5] = jnp.where(lane == lax.axis_index("ctx"), number, 0.0)
    g_begin(spaced[...])
    pltpu.make_async_copy(params.at[0], mix, mix_sem).wait()
    weights[0][0]()
    f_spread()
    g_step(0)
    g_step(1)
    f_forward()
    weights[0][1](1)
    blocks = g_step(2)
    find_flags(blocks[4:5, :128], number, flags, tall)
    gains[...] = g_step(3)
    f_exchange()
    f_arrive()
    flatten(first, planes)
    save_as(0, first, first_out)

    left = left_lanes()
    cos, sin = wide_turns(cosine_t, sine_t)
    for layer in range(LAYERS):
        whole = (whole0, whole1)[layer]
        w_begin, w_forward, w_relay, w_exchange, w_arrive, w_finish = weights[layer]
        n1, queries, kv, turned, lse, mixed, middle, n2, gate, up, product, start = [
            r.at[layer] for r in saved
        ]
        own = owns.at[layer]
        begin, forward, relay, arrive, finish = row_gather(
            me, own, kv, *[s.at[layer] for s in row_sems]
        )
        normed = (scaled * gains[2 * layer : 2 * layer + 1]).astype(jnp.bfloat16)
        n1[...] = normed
        start[...] = x
        for g in range(3):
            tile = dot_cols(normed, group_weights(first, g))
            tile = tile * jnp.where(left, cos, 1.0) + swapped(tile) * jnp.where(left, sin, 0.0)
            own[g] = tile.astype(jnp.bfloat16)
            begin(g)
        for j in range(5):
            tile = dot_cols(normed, first[0, 128 * j : 128 * j + 128])
            tile = (tile * cos + swapped(tile) * sin) * HEAD_SIZE ** (-0.5)
            spread_tile(queries, tile, j)
        for i in (0, 1, 11):
            save(layer, i)
        forward(0)
        forward(1)
        relay(0)
        forward(2)
        relay(1)

        def one(g, carry):
            arrive(g)

            def between():
                @pl.when(g == 0)
                def _():
                    relay(2)
                    w_forward(2)

                @pl.when(g == 2)
                def _():
                    w_relay()

            attend_group(
                g, me, kv, queries, flags, tall, turned, lse, keys, values, scores, rows, between
            )
            return carry

        lax.fori_loop(0, 3, one, 0)
        w_exchange()
        for i in (2, 3, 4):
            save(layer, i)
        for g in range(3):
            for h in range(3):
                mixed[64 * (3 * g + h) : 64 * (3 * g + h) + 64] = turned[
                    g, :, 128 * h : 128 * h + 128
                ].astype(jnp.bfloat16)
        mid = x + dot_rows(mixed[...], first[0, 960:1536])
        middle[...] = mid
        normed = (mid * inverse_root(mid) * gains[2 * layer + 1 : 2 * layer + 2]).astype(jnp.bfloat16)
        n2[...] = normed
        for i in (5, 6, 7):
            save(layer, i)
        w_arrive()
        if layer == 0:
            weights[1][0]()
        save_as(1 + layer, whole, (whole0_out, whole1_out)[layer])
        total = mid
        for i in range(4):
            part = pl.ds(384 * i, 384)
            gate_values = dot_cols(normed, whole[1, i].reshape(384, MODEL_WIDTH))
            up_values = dot_cols(normed, whole[2, i].reshape(384, MODEL_WIDTH))
            rounded = (gate_values * jax.nn.sigmoid(gate_values) * up_values).astype(jnp.bfloat16)
            gate[:, part] = gate_values
            up[:, part] = up_values
            product[:, part] = rounded
            total = total + jnp.dot(
                rounded, whole[3, i].reshape(384, MODEL_WIDTH), preferred_element_type=jnp.float32
            )
        for i in (8, 9, 10):
            save(layer, i)
        if layer == 0:
            weights[1][1](1)
            x = total
            scaled = x * inverse_root(x)
            saves[0].wait()
            saves.pop(0)
            flatten(first, whole0.at[0])
        else:
            result[...] = in_turn(total, turn).T.astype(jnp.bfloat16)
        for g in range(3):
            finish(g)
    g_finish()
    f_finish()
    for w in weights:
        w[5]()
    for copy in saves:
        copy.wait()


TURNED_BF16 = jax.ShapeDtypeStruct((MODEL_WIDTH, 128), jnp.bfloat16)
VMEM_SPEC = pl.BlockSpec(memory_space=pltpu.VMEM)
HBM_SPEC = pl.BlockSpec(memory_space=pl.ANY)


def forward_pass(hidden, params, gains, positions, turns):
    bf, w = jnp.bfloat16, MODEL_WIDTH
    dma = pltpu.SemaphoreType.DMA
    outs = pl.pallas_call(
        forward_kernel,
        out_shape=(
            TURNED_BF16,
            jax.ShapeDtypeStruct((8, w), jnp.float32),
            jax.ShapeDtypeStruct((40, LANES), jnp.float32),
            jax.ShapeDtypeStruct((40, 8, 128), jnp.float32),
            jax.ShapeDtypeStruct((1, 1536, w), bf),
            WHOLE,
            WHOLE,
        ) + tuple(jax.ShapeDtypeStruct((LAYERS,) + shape, dtype) for shape, dtype in SAVED),
        in_specs=[VMEM_SPEC, HBM_SPEC] + [VMEM_SPEC] * 4,
        out_specs=(VMEM_SPEC,) * 4 + (HBM_SPEC,) * (3 + len(SAVED)),
        scratch_shapes=[pltpu.VMEM((LAYERS,) + shape, dtype) for shape, dtype in SAVED] + [
            pltpu.VMEM((64 * TILES, 256), bf),
            pltpu.VMEM((64 * TILES, 256), bf),
            pltpu.VMEM((64 * TILES, LANES), jnp.float32),
            pltpu.VMEM((40, LANES), jnp.float32),
            pltpu.VMEM((1, 1536, w), bf),
            pltpu.VMEM((4, 4, 2, 48, w), bf),
            pltpu.VMEM((4, 48, w), bf),
            pltpu.VMEM((48, w), bf),
            pltpu.VMEM(WHOLE.shape, bf),
            pltpu.VMEM(WHOLE.shape, bf),
            pltpu.VMEM((4, 8, w), jnp.float32),
            pltpu.VMEM((4, 3, 8, w), jnp.float32),
            pltpu.VMEM((LAYERS, 3, 128, 128), bf),
            pltpu.VMEM((8, w), jnp.float32),
            dma((3, len(SAVED))),
            dma((LAYERS, 3, 2, 2, 4)),
            dma((LAYERS, 3, 2, 2, 4)),
            dma((LAYERS, 3, 2, 4)),
            dma((LAYERS, 3, 2, 4)),
            dma((LAYERS, 3)),
            dma((2, 2, 3)),
            dma((2, 2, 3)),
            dma((2, 4)),
            dma((2, 4)),
            dma((3,)),
            dma((3,)),
            dma((2,)),
            dma((4, 3)),
            dma((4, 3)),
            dma,
        ] + WEIGHT_GATHER_SEMS * 2,
        compiler_params=pltpu.CompilerParams(
            collective_id=1, has_side_effects=True, vmem_limit_bytes=58 * 2**20
        ),
        name="forward_pass",
    )(hidden, params, gains, positions, *turns)
    return outs[:7], outs[7:]


def norm_back(grad_normed, values, gain):
    inverse = inverse_root(values)
    unit = values * inverse
    grad_gain = jnp.sum(grad_normed * unit, axis=0, keepdims=True)
    scaled = grad_normed * gain
    grad_values = inverse * (
        scaled - unit * jnp.mean(scaled * unit, axis=-1, keepdims=True)
    )
    return grad_values, grad_gain


def products_first(gq, gkv, mixed, n1, gb):
    parts = [jnp.dot(gq[...], n1[...], preferred_element_type=jnp.float32)]
    both = [dot_rows(gkv[g], n1[...]) for g in range(3)]
    parts.append(jnp.concatenate([m[:64] for m in both], axis=0))
    parts.append(jnp.concatenate([m[64:] for m in both], axis=0))
    parts.append(jnp.dot(mixed[...], gb[...], preferred_element_type=jnp.float32))
    return [
        p.astype(jnp.bfloat16).reshape(p.shape[0] // 48, 48, MODEL_WIDTH) for p in parts
    ]


BIG = (2, 8, 9, 10)


def last_reduce(me, grads, halves, landed_a, sum_a, landed_b, sum_b, landed_y, swap_sends, swap_recvs, sends, recvs, y_sends, y_recvs):
    def swap(x):
        return pltpu.make_async_remote_copy(
            src_ref=grads.at[x, :, 1 - me[3]], dst_ref=halves.at[x],
            send_sem=swap_sends.at[x], recv_sem=swap_recvs.at[x],
            device_id=device(*sibling(me)), device_id_type=MESH)

    def copy(stage, src, dst, k, s):
        return pltpu.make_async_remote_copy(
            src_ref=src, dst_ref=dst,
            send_sem=sends.at[stage, k, s - 1], recv_sem=recvs.at[stage, k, s - 1],
            device_id=device(*moved(me, 1 + (k + 1 + stage) % 2, s)), device_id_type=MESH)

    def send(stage, k, s):
        axis = 1 + (k + 1 + stage) % 2
        to = moved(me, axis, s)[axis]
        rows = pl.ds(*HALF_ROWS[k])
        if stage == 0:
            index = [slice(None)] * 2
            index[axis - 1] = to
            return copy(0, halves.at[tuple(index) + (rows,)], landed_a.at[s - 1, :, rows], k, s)
        return copy(1, sum_a.at[to, rows], landed_b.at[s - 1, rows], k, s)

    def along_y(s):
        return pltpu.make_async_remote_copy(
            src_ref=sum_b, dst_ref=landed_y.at[s - 1],
            send_sem=y_sends.at[s - 1], recv_sem=y_recvs.at[s - 1],
            device_id=device(*moved(me, 0, s)), device_id_type=MESH)

    def begin():
        for x in range(4):
            swap(x).wait_recv()
            for z in range(4):
                halves[x, z] = (
                    grads[x, z, me[3]].astype(jnp.float32) + halves[x, z].astype(jnp.float32)
                ).astype(jnp.bfloat16)
        for s in (2, 1, 3):
            for k in range(2):
                send(0, k, s).start()

    def second():
        for k in (1, 0):
            rows = pl.ds(*HALF_ROWS[k])
            for s in (1, 3, 2):
                send(0, k, s).wait_recv()
            axis = 1 + (k + 1) % 2
            for i in range(4):
                spot = [i]
                spot.insert(axis - 1, me[axis])
                total = halves[tuple(spot) + (rows,)].astype(jnp.float32)
                for s in range(3):
                    total = total + landed_a[s, i, rows].astype(jnp.float32)
                sum_a[i, rows] = total.astype(jnp.bfloat16)
            for s in (2, 1, 3):
                send(1, k, s).start()

    def third():
        for k in (1, 0):
            rows = pl.ds(*HALF_ROWS[k])
            for s in (1, 3, 2):
                send(1, k, s).wait_recv()
            total = sum_a[me[1 + k % 2], rows].astype(jnp.float32)
            for s in range(3):
                total = total + landed_b[s, rows].astype(jnp.float32)
            sum_b[rows] = total.astype(jnp.bfloat16)
        for s in (2, 1, 3):
            along_y(s).start()

    def finish(out):
        total = sum_b[...].astype(jnp.float32)
        for s in (1, 3, 2):
            along_y(s).wait_recv()
            total = total + landed_y[s - 1].astype(jnp.float32)
        out[...] = total
        for x in range(4):
            swap(x).wait_send()
        for s in (1, 2, 3):
            along_y(s).wait_send()
            for stage in range(2):
                for k in range(2):
                    send(stage, k, s).wait_send()

    return swap, begin, second, third, finish


def backward_kernel(
    cotangent, positions, first0, first1, rest0, rest1,
    gains, cosine_t, sine_t, flags, tall, *refs
):
    count = len(SAVED)
    kept, refs = refs[:count], refs[count:]
    grad_hidden, owned, gain_sums = refs[:3]
    (
        keys, values, scores, lse_rows, inner_rows, dkv, spots, inner, dq, sums, ggate, gup,
        firsts, whole, gq, gkv, gb, gain_terms, reduced, load_sems, free_sem,
    ) = refs[3:24]
    row_refs = refs[24:32]
    weight_refs = refs[32:43]
    last_refs = refs[43:55]
    sum_refs = refs[55:59]
    saved = refs[59:]
    me = place()
    peers = [moved(me, a, s) for a, s in ALL_PEERS] + [sibling(me)]

    def view(layer, i):
        return saved[i] if i in BIG else saved[i].at[layer]

    def load(layer, i):
        return pltpu.make_async_copy(kept[i].at[layer], view(layer, i), load_sems.at[layer, i])

    def load_rest(layer):
        return pltpu.make_async_copy(
            (rest0, rest1)[layer].at[pl.ds(1, 3)], whole, load_sems.at[layer, count]
        )

    def load_first(layer):
        return pltpu.make_async_copy(
            (first0, first1)[layer].at[0], firsts.at[layer], load_sems.at[layer, count + 1]
        )

    load_rest(1).start()
    for i in (8, 9, 10, 7, 6, 3, 0, 1, 4, 5, 2, 11):
        load(1, i).start()
    load_first(1).start()
    load_first(0).start()
    for i in range(count):
        if i not in BIG:
            load(0, i).start()
    greet(peers)
    begin, second, third, finish, drain = row_reduce(me, dkv, sums, *row_refs)
    swap, halve, w_begin, w_second, w_third, w_finish = weight_reduce(me, *weight_refs)
    grads, halves = weight_refs[0], weight_refs[1]
    l_swap, l_begin, l_second, l_third, l_finish = last_reduce(me, grads.at[0], *last_refs)
    g_begin, g_step, g_finish = sum_everywhere(me, *sum_refs)
    left = left_lanes()
    cos, sin = wide_turns(cosine_t, sine_t)
    cos, sin = jnp.where(left, cos, 1.0), jnp.where(left, sin, 0.0)
    gain_terms[...] = jnp.zeros(gain_terms.shape, jnp.float32)
    turn = own_block(positions)[1]
    gr = in_turn(cotangent[...].astype(jnp.float32).T, turn)

    def first_products(layer, done):
        at = 0
        for cut in products_first(gq, gkv, view(layer, 5), view(layer, 0), gb):
            for i in range(cut.shape[0]):
                j = at + i
                grads[0, j // 8, (j // 2) % 4, j % 2] = cut[i]
                done(j)
            at += cut.shape[0]

    for layer in (1, 0):
        n1, queries, kv, turned, lse, mixed, middle, n2, gate, up, product, start = [
            view(layer, i) for i in range(count)
        ]
        first = firsts.at[layer]
        order = (1, 2, 3) if layer == 1 else (1, 2, 3, 0)
        load_rest(layer).wait()
        for i in (8, 9, 10, 7, 6):
            load(layer, i).wait()
        gd = gr.astype(jnp.bfloat16)
        normed = n2[...]
        grad_normed = jnp.zeros((128, MODEL_WIDTH), jnp.float32)
        for i in range(4):
            part = pl.ds(384 * i, 384)
            grad_product = dot_cols(gd, whole[2, i])
            gate_values, up_values = gate[:, part], up[:, part]
            s = jax.nn.sigmoid(gate_values)
            gg = (
                grad_product * up_values * (s * (1.0 + gate_values * (1.0 - s)))
            ).astype(jnp.bfloat16)
            gu = (grad_product * (gate_values * s)).astype(jnp.bfloat16)
            ggate[:, part] = gg
            gup[:, part] = gu
            grad_normed = grad_normed + jnp.dot(
                gg, whole[0, i], preferred_element_type=jnp.float32
            ) + jnp.dot(gu, whole[1, i], preferred_element_type=jnp.float32)
        if layer == 0:
            w_finish((1, 2, 3), reduced.at[1])
            for peer in peers:
                pl.semaphore_signal(
                    free_sem, inc=1, device_id=device(*peer), device_id_type=MESH
                )
            first_products(1, lambda j: None)
        for y, source, right in ((1, ggate, normed), (2, gup, normed), (3, product, gd)):
            for i in range(4):
                flat = dot_rows(source[:, 384 * i : 384 * i + 384], right).astype(jnp.bfloat16)
                grads[y, i] = flat.reshape(4, 2, 48, MODEL_WIDTH)
            if layer == 1:
                swap(y).start()
        if layer == 1:
            load_rest(0).start()
            for i in (8, 9, 10):
                load(0, i).start()
        grad_middle, grad_gain = norm_back(
            grad_normed, middle[...], gains[2 * layer + 1 : 2 * layer + 2]
        )
        gain_terms[2 * layer + 1 : 2 * layer + 2] = grad_gain
        grad_middle = grad_middle + gr
        branch = grad_middle.astype(jnp.bfloat16)
        gb[...] = branch
        load_first(layer).wait()
        for i in (3, 0, 1, 4, 5, 11):
            load(layer, i).wait()
        for j in range(5):
            width = min(128, 576 - 128 * j)
            tile = dot_cols(branch, first[960 + 128 * j : 960 + 128 * j + width])
            if width < 128:
                tile = jnp.concatenate([tile, jnp.zeros((128, 128 - width), jnp.float32)], axis=1)
            spread_tile(spots, tile, j)
        for g in range(3):
            for h in range(3):
                at = 64 * (3 * g + h)
                grad_turned = dot_cols(first[960 + at : 1024 + at], branch)
                grad_turned = grad_turned.astype(jnp.bfloat16).astype(jnp.float32)
                row = jnp.sum(
                    turned[g, :, 128 * h : 128 * h + 128] * grad_turned, axis=0, keepdims=True
                )
                inner[g, :, 128 * h : 128 * h + 128] = jnp.broadcast_to(row, (8, 128))
        load(layer, 2).wait()
        if layer == 0:
            pl.semaphore_wait(free_sem, len(peers))
            for y in order:
                swap(y).start()

        def one(g, carry):
            attend_back_group(
                g, me, kv, queries, spots, lse, inner, flags, tall, dq, dkv,
                keys, values, scores, lse_rows, inner_rows,
            )
            begin(g)

            @pl.when(g == 0)
            def _():
                for y in order:
                    halve(y)
                if layer == 1:
                    halves[0] = jnp.zeros(halves.shape[1:], jnp.bfloat16)
                w_begin()

            @pl.when(g == 1)
            def _():
                second(0)

            @pl.when(g == 2)
            def _():
                third(0)
                second(1)

            return carry

        lax.fori_loop(0, 3, one, 0)
        if layer == 1:
            load(0, 2).start()
        second(2)
        third(1)
        for g in range(3):
            for h in range(3):
                rows = dq[g, :, 128 * h : 128 * h + 128] * HEAD_SIZE ** (-0.5)
                a, b = rows[:32], rows[32:]
                at = 64 * (3 * g + h)
                gq[at : at + 32] = (a * cosine_t[...] + b * sine_t[...]).astype(jnp.bfloat16)
                gq[at + 32 : at + 64] = (b * cosine_t[...] - a * sine_t[...]).astype(jnp.bfloat16)
        third(2)
        w_second()
        grad_normed = dot_rows(gq[...], first[:576])
        for g in range(3):
            finish(g)
            tile = sums[g]
            tile = (tile * cos - swapped(tile) * sin).astype(jnp.bfloat16)
            gkv[g] = tile
            weights = jnp.concatenate(
                [first[576 + 64 * g : 640 + 64 * g], first[768 + 64 * g : 832 + 64 * g]], axis=0
            )
            grad_normed = grad_normed + jnp.dot(tile, weights, preferred_element_type=jnp.float32)
        if layer == 0:
            swap(0).wait_send()
            first_products(0, lambda j: l_swap(j // 8).start() if j % 8 == 7 else None)
        w_third()
        grad_values, grad_gain = norm_back(
            grad_normed, start[...], gains[2 * layer : 2 * layer + 1]
        )
        gain_terms[2 * layer : 2 * layer + 1] = grad_gain
        gr = grad_values + grad_middle
        for g in range(3):
            drain(g)
    grad_hidden[...] = in_turn(gr, turn).T
    g_begin(gain_terms[...])
    l_begin()
    g_step(0)
    w_finish((1, 2, 3), reduced.at[0])
    g_step(1)
    l_second()
    g_step(2)
    l_third()
    gain_sums[...] = g_step(3)
    l_finish(reduced.at[2])
    g_finish()
    at_front = jnp.broadcast_to(me[0], (48, MODEL_WIDTH)) == 0
    owned[0] = jnp.where(at_front, reduced[2], reduced[0])
    owned[1] = jnp.where(at_front, reduced[0], reduced[1])


def backward_pass(cotangent, positions, first, whole0, whole1, gains, turns, flags, kept):
    planes, rows = (4, 1536, MODEL_WIDTH), (4, 4, 384, MODEL_WIDTH)
    bf, w = jnp.bfloat16, MODEL_WIDTH
    dma = pltpu.SemaphoreType.DMA
    return pl.pallas_call(
        backward_kernel,
        out_shape=(
            jax.ShapeDtypeStruct((w, 128), jnp.float32),
            jax.ShapeDtypeStruct((LAYERS, 48, w), jnp.float32),
            jax.ShapeDtypeStruct((8, w), jnp.float32),
        ),
        in_specs=[VMEM_SPEC] * 2 + [HBM_SPEC] * 4 + [VMEM_SPEC] * 5 + [HBM_SPEC] * len(SAVED),
        out_specs=(VMEM_SPEC,) * 3,
        scratch_shapes=[
            pltpu.VMEM((64 * TILES, 256), bf),
            pltpu.VMEM((64 * TILES, 256), bf),
            pltpu.VMEM((64 * TILES, LANES), jnp.float32),
            pltpu.VMEM((40, LANES), jnp.float32),
            pltpu.VMEM((40, LANES), jnp.float32),
            pltpu.VMEM((3, 4, 4, 2, 128, 128), bf),
            pltpu.VMEM((3, LANES, 256), bf),
            pltpu.VMEM((3, 8, LANES), jnp.float32),
            pltpu.VMEM((3, 64, LANES), jnp.float32),
            pltpu.VMEM((3, 128, 128), jnp.float32),
            pltpu.VMEM((128, FEEDFORWARD_SIZE), bf),
            pltpu.VMEM((128, FEEDFORWARD_SIZE), bf),
            pltpu.VMEM((LAYERS, 1536, w), bf),
            pltpu.VMEM((3, 4, 384, w), bf),
            pltpu.VMEM((w, 128), bf),
            pltpu.VMEM((3, 128, 128), bf),
            pltpu.VMEM((128, w), bf),
            pltpu.VMEM((8, w), jnp.float32),
            pltpu.VMEM((3, 48, w), jnp.float32),
            dma((LAYERS, len(SAVED) + 2)),
            pltpu.SemaphoreType.REGULAR,
        ] + row_reduce_scratch() + weight_reduce_scratch() + [
            pltpu.VMEM((4, 4, 48, w), bf),
            pltpu.VMEM((3, 4, 48, w), bf),
            pltpu.VMEM((4, 48, w), bf),
            pltpu.VMEM((3, 48, w), bf),
            pltpu.VMEM((48, w), bf),
            pltpu.VMEM((3, 48, w), bf),
            dma((4,)),
            dma((4,)),
            dma((2, 2, 3)),
            dma((2, 2, 3)),
            dma((3,)),
            dma((3,)),
            pltpu.VMEM((4, 8, w), jnp.float32),
            pltpu.VMEM((4, 3, 8, w), jnp.float32),
            dma((4, 3)),
            dma((4, 3)),
        ] + [
            pltpu.VMEM(shape if i in BIG else (LAYERS,) + shape, dtype)
            for i, (shape, dtype) in enumerate(SAVED)
        ],
        compiler_params=pltpu.CompilerParams(
            collective_id=2, has_side_effects=True, vmem_limit_bytes=62 * 2**20
        ),
        name="backward_pass",
    )(
        cotangent, positions, first, whole0.reshape(planes), whole0.reshape(rows),
        whole1.reshape(rows), gains, *turns, *flags, *kept
    )


def turn_tables(places):
    half = HEAD_SIZE // 2
    frequency = 1.0 / THETA ** (2 * jnp.arange(half).astype(jnp.float32) / HEAD_SIZE)
    phases = frequency[:, None] * places.astype(jnp.float32)[None, :]
    return jnp.cos(phases), jnp.sin(phases)


def on_device(hidden_in, positions, params, gains, cotangent):
    places = positions[0]
    turn = places[0] >= SEQ_LEN // 2
    turns = turn_tables(jnp.where(turn, jnp.concatenate([places[64:], places[:64]]), places))
    main, kept = forward_pass(hidden_in[0].T, params, gains, positions, turns)
    hidden_out, gain_rows, flags = main[0], main[1], main[2:4]
    grad_in, owned, gain_sums = backward_pass(
        cotangent[0].T, positions, *main[4:7], gain_rows, turns, flags, kept
    )
    index = lax.axis_index("fsdp") * 32 + lax.axis_index("ctx")
    gain_sums = gain_sums[:4].reshape(LAYERS, 2 * MODEL_WIDTH)
    owned_gains = lax.dynamic_slice(gain_sums, (0, index * 9), (LAYERS, 9))
    return (hidden_out.T[None], grad_in.T[None], owned, owned_gains)


def solution(mesh):
    return jax.shard_map(
        on_device,
        mesh=mesh,
        in_specs=(
            P("fsdp", "ctx", None),
            P("fsdp", "ctx"),
            P(None, ("fsdp", "ctx"), None),
            P(None, ("fsdp", "ctx")),
            P("fsdp", "ctx", None),
        ),
        out_specs=(
            P("fsdp", "ctx", None),
            P("fsdp", "ctx", None),
            P(None, ("fsdp", "ctx"), None),
            P(None, ("fsdp", "ctx")),
        ),
        check_vma=False,
    )
```

```python
import functools

import jax
import jax.numpy as jnp
from jax import lax
from jax.experimental import pallas as pl
from jax.experimental.pallas import tpu as pltpu
from jax.sharding import PartitionSpec as P

MODEL_WIDTH = 576
FEEDFORWARD_SIZE = 1536
QUERY_HEADS = 9
KEY_VALUE_HEADS = 3
HEAD_SIZE = 64
LAYERS = 2
SEQ_LEN = 4096

EPSILON = 1e-05
THETA = 100000.0
MASKED = -1e30
MESH = pl.DeviceIdType.MESH
RING = 4


def place():
    t = lax.axis_index("ctx")
    return (lax.axis_index("fsdp"), t // 8, (t // 2) % 4, t % 2)


def device(y, x, z, c):
    return (y, x * 8 + z * 2 + c)


def moved(me, axis, step):
    other = list(me)
    other[axis] = (me[axis] + step) % RING
    return tuple(other)


def sibling(me):
    return (me[0], me[1], me[2], 1 - me[3])


def greet(peers):
    barrier = pltpu.get_barrier_semaphore()
    for peer in peers:
        pl.semaphore_signal(barrier, inc=1, device_id=device(*peer), device_id_type=MESH)
    pl.semaphore_wait(barrier, len(peers))


TILES = 33
CHUNK = 11
LANES = 384


def head_lanes():
    return lax.broadcasted_iota(jnp.int32, (1, LANES), 1) % 128 >= 64


def roll_heads(rows):
    return jnp.concatenate(
        [pltpu.roll(rows[:, 128 * h : 128 * h + 128], 64, 1) for h in range(3)], axis=1
    )


def pack_tile(lo, hi, keep_lo, use_a, use_b):
    lo = lo.astype(jnp.float32)
    hi = hi.astype(jnp.float32)
    zero = jnp.zeros_like(lo)
    a = jnp.where(use_a, lo, zero)
    b = jnp.where(use_b, hi, zero)
    if not keep_lo:
        lo = zero
    left = lax.broadcasted_iota(jnp.int32, (64, 128), 1) < 64
    keys = [jnp.where(left, lo, pltpu.roll(a, 64, 1)), jnp.where(left, b, zero)]
    values = [jnp.where(left, pltpu.roll(lo, 64, 1), a), jnp.where(left, pltpu.roll(b, 64, 1), zero)]
    return (
        jnp.concatenate(keys, axis=1).astype(jnp.bfloat16),
        jnp.concatenate(values, axis=1).astype(jnp.bfloat16),
    )


def pack_all(g, me, kv, tall, keys, values):
    def one(t, carry):
        at = kv[g, t // 8, (t // 2) % 4, t % 2]
        use_a = jnp.broadcast_to(tall[t][:1] > 0.5, (64, 128))
        k, v = pack_tile(at[:64], at[64:], True, use_a, jnp.logical_not(use_a))
        spot = pl.ds(pl.multiple_of(t * 64, 64), 64)
        keys[spot] = k
        values[spot] = v
        return carry

    lax.fori_loop(0, TILES - 1, one, 0, unroll=4)
    yes = jnp.full((64, 128), True)
    at = kv[g, me[1], me[2], me[3]]
    k, v = pack_tile(at[:64], at[64:], False, yes, jnp.logical_not(yes))
    keys[pl.ds(64 * (TILES - 1), 64)] = k
    values[pl.ds(64 * (TILES - 1), 64)] = v


def dot_cols(left, right):
    return lax.dot_general(
        left, right, (((1,), (1,)), ((), ())), preferred_element_type=jnp.float32
    )


def dot_rows(left, right):
    return lax.dot_general(
        left, right, (((0,), (0,)), ((), ())), preferred_element_type=jnp.float32
    )


def score_all(keys, queries, scores):
    for c in range(TILES // CHUNK):
        rows = pl.ds(64 * CHUNK * c, 64 * CHUNK)
        scores[rows] = dot_cols(keys[rows], queries)
    at = lax.broadcasted_iota(jnp.int32, (64, LANES), 0)
    lane = lax.broadcasted_iota(jnp.int32, (64, LANES), 1) % 128
    causal = jnp.logical_and(lane < 64, at <= lane)
    mine = pl.ds(pl.multiple_of(lax.axis_index("ctx") * 64, 64), 64)
    scores[mine] = jnp.where(jnp.logical_or(lane >= 64, causal), scores[mine], MASKED)
    last = pl.ds(64 * (TILES - 1), 64)
    scores[last] = jnp.where(causal, scores[last], MASKED)


def tile_rows(flags, row):
    crossed = jnp.where(head_lanes(), row, roll_heads(row))
    return jnp.where(flags[...] > 0.5, row, crossed)


def joined(rows, flags, merge, empty):
    straight = jnp.where(jnp.logical_or(head_lanes(), flags[...] > 0.5), rows, empty)
    crossed = jnp.where(jnp.logical_or(head_lanes(), flags[...] > 0.5), empty, rows)
    down = jnp.max if merge is jnp.maximum else jnp.sum
    one = down(straight, axis=0, keepdims=True)
    other = roll_heads(down(crossed, axis=0, keepdims=True))
    return merge(one, other)


def fold_lanes(product):
    return jnp.where(
        head_lanes(), product[:64] + roll_heads(product[128:192]), product[64:128]
    )


def attend_group(
    g, me, kv, queries, flags, tall, out, lse, keys, values, scores, rows, between
):
    pack_all(g, me, kv, tall, keys, values)
    score_all(keys, queries[g], scores)
    between()
    rows[...] = jnp.full(rows.shape, MASKED, jnp.float32)

    for t in range(TILES):
        rows[pl.ds(t, 1)] = jnp.max(scores[pl.ds(64 * t, 64)], axis=0, keepdims=True)
    top = joined(rows[...], flags, jnp.maximum, MASKED)
    rows[...] = tile_rows(flags, top)
    total = jnp.zeros((256, LANES), jnp.float32)
    sums = []
    for c in range(TILES // CHUNK):
        parts = []
        for i in range(CHUNK):
            t = c * CHUNK + i
            raised = jnp.exp(scores[pl.ds(64 * t, 64)] - rows[pl.ds(t, 1)])
            sums.append(jnp.sum(raised, axis=0, keepdims=True))
            parts.append(raised.astype(jnp.bfloat16))
        spot = pl.ds(64 * CHUNK * c, 64 * CHUNK)
        total = total + dot_rows(values[spot], jnp.concatenate(parts, axis=0))
    rows[...] = jnp.zeros(rows.shape, jnp.float32)
    for t in range(TILES):
        rows[pl.ds(t, 1)] = sums[t]
    amount = joined(rows[...], flags, jnp.add, 0.0)
    out[g] = fold_lanes(total) / amount
    lse[g] = jnp.broadcast_to(top + jnp.log(amount), (8, LANES))


def attend_back_group(
    g, me, kv, queries, grads, lse, inner, flags, tall, dq, dkv,
    keys, values, scores, lse_rows, inner_rows,
):
    pack_all(g, me, kv, tall, keys, values)
    score_all(keys, queries[g], scores)
    lse_rows[...] = tile_rows(flags, lse[g][:1])
    inner_rows[...] = tile_rows(flags, inner[g][:1])
    total = jnp.zeros((256, LANES), jnp.float32)
    for c in range(TILES // CHUNK):
        spot = pl.ds(64 * CHUNK * c, 64 * CHUNK)
        grad_probs = dot_cols(values[spot], grads[g])
        probs, rest = [], []
        for i in range(CHUNK):
            t = c * CHUNK + i
            p = jnp.exp(scores[pl.ds(64 * t, 64)] - lse_rows[pl.ds(t, 1)])
            probs.append(p.astype(jnp.bfloat16))
            rest.append(
                (p * (grad_probs[64 * i : 64 * i + 64] - inner_rows[pl.ds(t, 1)])).astype(jnp.bfloat16)
            )
        probs = jnp.concatenate(probs, axis=0)
        rest = jnp.concatenate(rest, axis=0)
        total = total + dot_rows(keys[spot], rest)
        to_keys = jnp.dot(rest, queries[g], preferred_element_type=jnp.float32)
        to_values = jnp.dot(probs, grads[g], preferred_element_type=jnp.float32)
        left = lax.broadcasted_iota(jnp.int32, (64, 128), 1) < 64
        for i in range(CHUNK):
            t = c * CHUNK + i
            k0 = to_keys[64 * i : 64 * i + 64, :128]
            k1 = to_keys[64 * i : 64 * i + 64, 128:]
            v0 = to_values[64 * i : 64 * i + 64, :128]
            v1 = to_values[64 * i : 64 * i + 64, 128:]
            a = jnp.where(left, pltpu.roll(k0, 64, 1), v0)
            if t < TILES - 1:
                use_a = jnp.broadcast_to(tall[t][:1] > 0.5, (64, 128))
                lo = jnp.where(left, k0, pltpu.roll(v0, 64, 1)) + jnp.where(use_a, a, 0.0)
                hi = jnp.where(use_a, 0.0, jnp.where(left, k1, pltpu.roll(v1, 64, 1)))
                dkv[g, t // 8, (t // 2) % 4, t % 2, :64] = lo.astype(jnp.bfloat16)
                dkv[g, t // 8, (t // 2) % 4, t % 2, 64:] = hi.astype(jnp.bfloat16)
            else:
                spot = (g, me[1], me[2], me[3], pl.ds(0, 64))
                dkv[spot] = (dkv[spot].astype(jnp.float32) + a).astype(jnp.bfloat16)
    dq[g] = fold_lanes(total)


def weight_gather(
    me, source, whole, sends, recvs, swap_sends, swap_recvs, own_sem, skip=False
):
    def region(k, phase, at, core):
        index = [at[0], at[1], at[2]]
        for i in range(phase):
            axis = (k + i) % 3
            index[axis] = pl.ds(1, 3) if skip and axis == 0 else slice(None)
        return whole.at[tuple(index) + (core, pl.ds(16 * k, 16))]

    def has(k, phase, y):
        return None if not skip or phase > -k % 3 else y != 0

    def copy(src, dst, k, phase, s):
        return pltpu.make_async_remote_copy(
            src_ref=src, dst_ref=dst,
            send_sem=sends.at[k, phase, s - 1], recv_sem=recvs.at[k, phase, s - 1],
            device_id=device(*moved(me, (k + phase) % 3, s)), device_id_type=MESH)

    def send(k, phase, s, what):
        spot = region(k, phase, me, me[3])
        made = copy(spot if phase else source.at[pl.ds(16 * k, 16)], spot, k, phase, s)
        only(has(k, phase, me[0]), made.start if what == "start" else made.wait_send)

    def land(k, phase, s):
        there = moved(me, (k + phase) % 3, -s)
        spot = region(k, phase, there, me[3])
        only(has(k, phase, there[0]), copy(spot, spot, k, phase, s).wait_recv)

    def relay_copy(k, i, at, what):
        axis = (k + 2) % 3
        index = [at[0], at[1], at[2]]
        for j in (k, (k + 1) % 3):
            index[j] = pl.ds(1, 3) if skip and j == 0 else slice(None)
        index[1 if k < 2 else 2] = pl.ds(2 * i, 2)
        spot = whole.at[tuple(index) + (me[3], pl.ds(16 * k, 16))]
        made = pltpu.make_async_remote_copy(
            src_ref=spot, dst_ref=spot,
            send_sem=sends.at[k, 2, 1 + 2 * i], recv_sem=recvs.at[k, 2, 1 + 2 * i],
            device_id=device(*moved(me, axis, 3 if i else 1)), device_id_type=MESH)
        act = {"start": made.start, "sent": made.wait_send, "landed": made.wait_recv}
        only(has(k, 2, at[0]), act[what])

    def relayed(k, i):
        return moved(me, (k + 2) % 3, 1 if i else 3)

    def swap(k, s, core, what):
        there = moved(me, (k + 2) % 3, -s)
        spot = region(k, 2, there, core)
        made = pltpu.make_async_remote_copy(
            src_ref=spot, dst_ref=spot,
            send_sem=swap_sends.at[k, s], recv_sem=swap_recvs.at[k, s],
            device_id=device(*sibling(me)), device_id_type=MESH)
        act = {"start": made.start, "sent": made.wait_send, "landed": made.wait_recv}
        only(has(k, 2, there[0]), act[what])

    def begin():
        own = pltpu.make_async_copy(source, whole.at[me], own_sem)
        own.start()
        for k in range(3):
            for s in (2, 1, 3):
                send(k, 0, s, "start")
        own.wait()

    def forward(phase):
        for k in range(3):
            for s in (1, 3, 2):
                land(k, phase - 1, s)
            for s in (1, 3) if phase == 2 else (2, 1, 3):
                send(k, phase, s, "start")
            if phase == 2:
                swap(k, 0, me[3], "start")

    def relay():
        for i, s in enumerate((1, 3)):
            for k in range(3):
                land(k, 2, s)
                relay_copy(k, i, relayed(k, i), "start")
                swap(k, s, me[3], "start")

    def exchange():
        for k in range(3):
            for i in range(2):
                relay_copy(k, i, moved(me, (k + 2) % 3, 2), "landed")
            swap(k, 2, me[3], "start")

    def arrive():
        for k in range(3):
            for s in range(4):
                swap(k, s, 1 - me[3], "landed")

    def finish():
        for k in range(3):
            for phase in range(3):
                for s in (1, 3) if phase == 2 else (1, 2, 3):
                    send(k, phase, s, "sent")
            for i in range(2):
                relay_copy(k, i, relayed(k, i), "sent")
            for s in range(4):
                swap(k, s, me[3], "sent")

    return begin, forward, relay, exchange, arrive, finish


def only(condition, act):
    if condition is None:
        act()
    else:
        pl.when(condition)(act)


WEIGHT_GATHER_SEMS = [
    pltpu.SemaphoreType.DMA((3, 3, 4)),
    pltpu.SemaphoreType.DMA((3, 3, 4)),
    pltpu.SemaphoreType.DMA((3, 4)),
    pltpu.SemaphoreType.DMA((3, 4)),
    pltpu.SemaphoreType.DMA,
]
WHOLE = jax.ShapeDtypeStruct((4, 4, 4, 2, 48, MODEL_WIDTH), jnp.bfloat16)
ALL_PEERS = tuple((a, s) for a in range(3) for s in (1, 2, 3))


def greet_all(me):
    greet([moved(me, a, s) for a, s in ALL_PEERS] + [sibling(me)])


def row_gather(me, own, kv, sends, recvs, swap_sends, swap_recvs, own_sems):
    def region(g, k, phase, at, core):
        index = [at[1], at[2]]
        if phase >= 1:
            index[1 - k] = slice(None)
        return kv.at[(g,) + tuple(index) + (core, pl.ds(64 * k, 64))]

    def axis_of(k, phase):
        return 1 + (1 - k + phase) % 2

    def copy(src, dst, g, k, phase, s):
        return pltpu.make_async_remote_copy(
            src_ref=src, dst_ref=dst,
            send_sem=sends.at[g, k, phase, s - 1], recv_sem=recvs.at[g, k, phase, s - 1],
            device_id=device(*moved(me, axis_of(k, phase), s)), device_id_type=MESH)

    def send(g, k, phase, s):
        spot = region(g, k, phase, me, me[3])
        return copy(spot if phase else own.at[g, pl.ds(64 * k, 64)], spot, g, k, phase, s)

    def landed(g, k, phase, s):
        spot = region(g, k, phase, moved(me, axis_of(k, phase), -s), me[3])
        return copy(spot, spot, g, k, phase, s)

    def relay_copy(g, k, i, at):
        index = [at[1], at[2]]
        index[1 - k] = pl.ds(2 * i, 2)
        spot = kv.at[(g,) + tuple(index) + (me[3], pl.ds(64 * k, 64))]
        return pltpu.make_async_remote_copy(
            src_ref=spot, dst_ref=spot,
            send_sem=sends.at[g, k, 1, 1 + 2 * i], recv_sem=recvs.at[g, k, 1, 1 + 2 * i],
            device_id=device(*moved(me, axis_of(k, 1), 3 if i else 1)), device_id_type=MESH)

    def relayed(k, i):
        return moved(me, axis_of(k, 1), 1 if i else 3)

    def swap(g, k, s, core):
        spot = region(g, k, 1, moved(me, axis_of(k, 1), -s), core)
        return pltpu.make_async_remote_copy(
            src_ref=spot, dst_ref=spot,
            send_sem=swap_sends.at[g, k, s], recv_sem=swap_recvs.at[g, k, s],
            device_id=device(*sibling(me)), device_id_type=MESH)

    def keep(g):
        return pltpu.make_async_copy(own.at[g], kv.at[g, me[1], me[2], me[3]], own_sems.at[g])

    def begin(g):
        for s in (2, 1, 3):
            for k in range(2):
                send(g, k, 0, s).start()
        keep(g).start()

    def forward(g):
        keep(g).wait()
        for k in range(2):
            for s in (1, 3, 2):
                landed(g, k, 0, s).wait_recv()
            for s in (1, 3):
                send(g, k, 1, s).start()
            swap(g, k, 0, me[3]).start()

    def relay(g):
        for i, s in enumerate((1, 3)):
            for k in range(2):
                landed(g, k, 1, s).wait_recv()
                relay_copy(g, k, i, relayed(k, i)).start()
                swap(g, k, s, me[3]).start()

    def arrive(g):
        for k in range(2):
            for i in range(2):
                relay_copy(g, k, i, moved(me, axis_of(k, 1), 2)).wait_recv()
            swap(g, k, 2, me[3]).start()
        for k in range(2):
            for s in range(4):
                swap(g, k, s, 1 - me[3]).wait_recv()

    def finish(g):
        for k in range(2):
            for phase in range(2):
                for s in (1, 3) if phase else (1, 2, 3):
                    send(g, k, phase, s).wait_send()
            for i in range(2):
                relay_copy(g, k, i, relayed(k, i)).wait_send()
            for s in range(4):
                swap(g, k, s, me[3]).wait_send()

    return begin, forward, relay, arrive, finish


def weight_reduce(
    me, grads, halves, landed_a, sum_a, landed_b, sum_b, landed_c,
    swap_sends, swap_recvs, sends, recvs,
):
    axes = ((2, 1, 0), (0, 2, 1), (1, 0, 2))

    def swap(y):
        return pltpu.make_async_remote_copy(
            src_ref=grads.at[y, :, :, 1 - me[3]], dst_ref=halves.at[y],
            send_sem=swap_sends.at[y], recv_sem=swap_recvs.at[y],
            device_id=device(*sibling(me)), device_id_type=MESH)

    def copy(stage, src, dst, k, s, peer):
        return pltpu.make_async_remote_copy(
            src_ref=src, dst_ref=dst,
            send_sem=sends.at[stage, k, s - 1], recv_sem=recvs.at[stage, k, s - 1],
            device_id=device(*peer), device_id_type=MESH)

    def send(stage, k, s):
        axis = axes[k][stage]
        peer = moved(me, axis, s)
        if stage == 0:
            index = [slice(None)] * 3
            index[axis] = peer[axis]
            return copy(0, halves.at[tuple(index) + (pl.ds(16 * k, 16),)], landed_a.at[k, s - 1], k, s, peer)
        if stage == 1:
            index = [slice(None)] * 2
            index[sorted(axes[k][1:]).index(axis)] = peer[axis]
            return copy(1, sum_a.at[(k,) + tuple(index)], landed_b.at[k, s - 1], k, s, peer)
        return copy(2, sum_b.at[k, peer[axis]], landed_c.at[k, s - 1], k, s, peer)

    def halve(y):
        swap(y).wait_recv()
        for x in range(4):
            for z in range(4):
                halves[y, x, z] = (
                    grads[y, x, z, me[3]].astype(jnp.float32) + halves[y, x, z].astype(jnp.float32)
                ).astype(jnp.bfloat16)

    def begin():
        for k in range(3):
            for s in (2, 1, 3):
                send(0, k, s).start()

    def second():
        for k in range(3):
            for s in (1, 3, 2):
                send(0, k, s).wait_recv()
            axis = axes[k][0]
            for i in range(4):
                for j in range(4):
                    at = [i, j]
                    at.insert(axis, me[axis])
                    total = halves[tuple(at) + (pl.ds(16 * k, 16),)].astype(jnp.float32)
                    for s in range(3):
                        total = total + landed_a[k, s, i, j].astype(jnp.float32)
                    sum_a[k, i, j] = total.astype(jnp.bfloat16)
            for s in (2, 1, 3):
                send(1, k, s).start()

    def third():
        for k in range(3):
            for s in (1, 3, 2):
                send(1, k, s).wait_recv()
            rest = sorted(axes[k][1:])
            for i in range(4):
                at = [i, i]
                at[rest.index(axes[k][1])] = me[axes[k][1]]
                total = sum_a[(k,) + tuple(at)].astype(jnp.float32)
                for s in range(3):
                    total = total + landed_b[k, s, i].astype(jnp.float32)
                sum_b[k, i] = total.astype(jnp.bfloat16)
            for s in (2, 1, 3):
                send(2, k, s).start()

    def finish(planes, out):
        for k in range(3):
            for s in (1, 3, 2):
                send(2, k, s).wait_recv()
            total = sum_b[k, me[axes[k][2]]].astype(jnp.float32)
            for s in range(3):
                total = total + landed_c[k, s].astype(jnp.float32)
            out[pl.ds(16 * k, 16)] = total
        for y in planes:
            swap(y).wait_send()
        for stage in range(3):
            for k in range(3):
                for s in (1, 2, 3):
                    send(stage, k, s).wait_send()

    return swap, halve, begin, second, third, finish


def weight_reduce_scratch():
    bf, w = jnp.bfloat16, MODEL_WIDTH
    return [
        pltpu.VMEM((4, 4, 4, 2, 48, w), bf),
        pltpu.VMEM((4, 4, 4, 48, w), bf),
        pltpu.VMEM((3, 3, 4, 4, 16, w), bf),
        pltpu.VMEM((3, 4, 4, 16, w), bf),
        pltpu.VMEM((3, 3, 4, 16, w), bf),
        pltpu.VMEM((3, 4, 16, w), bf),
        pltpu.VMEM((3, 3, 16, w), bf),
        pltpu.SemaphoreType.DMA((4,)),
        pltpu.SemaphoreType.DMA((4,)),
        pltpu.SemaphoreType.DMA((3, 3, 3)),
        pltpu.SemaphoreType.DMA((3, 3, 3)),
    ]


def row_reduce(
    me, terms, out, halves, landed_a, sum_a, landed_b, swap_sends, swap_recvs, sends, recvs
):
    axes = ((2, 1), (1, 2))

    def swap(g):
        return pltpu.make_async_remote_copy(
            src_ref=terms.at[g, :, :, 1 - me[3]], dst_ref=halves.at[g],
            send_sem=swap_sends.at[g], recv_sem=swap_recvs.at[g],
            device_id=device(*sibling(me)), device_id_type=MESH)

    def send(stage, g, k, s):
        axis = axes[k][stage]
        peer = moved(me, axis, s)
        if stage == 0:
            index = [slice(None)] * 2
            index[axis - 1] = peer[axis]
            src = halves.at[(g,) + tuple(index) + (pl.ds(64 * k, 64),)]
            dst = landed_a.at[g, k, s - 1]
        else:
            src = sum_a.at[g, k, peer[axis]]
            dst = landed_b.at[g, k, s - 1]
        return pltpu.make_async_remote_copy(
            src_ref=src, dst_ref=dst,
            send_sem=sends.at[stage, g, k, s - 1], recv_sem=recvs.at[stage, g, k, s - 1],
            device_id=device(*peer), device_id_type=MESH)

    def begin(g):
        swap(g).start()

    def second(g):
        swap(g).wait_recv()
        for x in range(4):
            for z in range(4):
                halves[g, x, z] = (
                    terms[g, x, z, me[3]].astype(jnp.float32) + halves[g, x, z].astype(jnp.float32)
                ).astype(jnp.bfloat16)
        for s in (2, 1, 3):
            for k in range(2):
                send(0, g, k, s).start()

    def third(g):
        for k in range(2):
            for s in (1, 3, 2):
                send(0, g, k, s).wait_recv()
            axis = axes[k][0]
            for i in range(4):
                at = [i]
                at.insert(axis - 1, me[axis])
                total = halves[(g,) + tuple(at) + (pl.ds(64 * k, 64),)].astype(jnp.float32)
                for s in range(3):
                    total = total + landed_a[g, k, s, i].astype(jnp.float32)
                sum_a[g, k, i] = total.astype(jnp.bfloat16)
            for s in (2, 1, 3):
                send(1, g, k, s).start()

    def finish(g):
        for k in range(2):
            for s in (1, 3, 2):
                send(1, g, k, s).wait_recv()
            total = sum_a[g, k, me[axes[k][1]]].astype(jnp.float32)
            for s in range(3):
                total = total + landed_b[g, k, s].astype(jnp.float32)
            out[g, pl.ds(64 * k, 64)] = total

    def drain(g):
        swap(g).wait_send()
        for stage in range(2):
            for k in range(2):
                for s in (1, 2, 3):
                    send(stage, g, k, s).wait_send()

    return begin, second, third, finish, drain


def row_reduce_scratch():
    bf = jnp.bfloat16
    return [
        pltpu.VMEM((3, 4, 4, 128, 128), bf),
        pltpu.VMEM((3, 2, 3, 4, 64, 128), bf),
        pltpu.VMEM((3, 2, 4, 64, 128), bf),
        pltpu.VMEM((3, 2, 3, 64, 128), bf),
        pltpu.SemaphoreType.DMA((3,)),
        pltpu.SemaphoreType.DMA((3,)),
        pltpu.SemaphoreType.DMA((2, 3, 2, 3)),
        pltpu.SemaphoreType.DMA((2, 3, 2, 3)),
    ]


def left_lanes():
    return lax.broadcasted_iota(jnp.int32, (128, 128), 1) < 64


def swapped(tile):
    low = lax.broadcasted_iota(jnp.int32, tile.shape, 1) % 64 < 32
    return jnp.where(low, pltpu.roll(tile, 96, 1), pltpu.roll(tile, 32, 1))


def spread_tile(spots, tile, j):
    other = pltpu.roll(tile, 64, 1)
    left = left_lanes()
    for i in range(2):
        head = 2 * j + i
        if head >= QUERY_HEADS:
            continue
        a = jnp.where(left, tile if i == 0 else other, 0.0).astype(jnp.bfloat16)
        b = jnp.where(left, 0.0, other if i == 0 else tile).astype(jnp.bfloat16)
        g, at = head // 3, 128 * (head % 3)
        spots[g, at : at + 64, :128] = b[:64]
        spots[g, at : at + 64, 128:] = a[64:]
        spots[g, at + 64 : at + 128, :128] = a[64:]
        spots[g, at + 64 : at + 128, 128:] = jnp.zeros((64, 128), jnp.bfloat16)


def group_weights(first, g):
    return jnp.concatenate(
        [first[0, 576 + 64 * g : 640 + 64 * g], first[0, 768 + 64 * g : 832 + 64 * g]], axis=0
    )


def inverse_root(values):
    return lax.rsqrt(jnp.mean(values * values, axis=-1, keepdims=True) + EPSILON)


HALF_ROWS = ((0, 32), (32, 16))


SAVED = (
    ((128, MODEL_WIDTH), jnp.bfloat16),
    ((3, LANES, 256), jnp.bfloat16),
    ((3, 4, 4, 2, 128, 128), jnp.bfloat16),
    ((3, 64, LANES), jnp.float32),
    ((3, 8, LANES), jnp.float32),
    ((MODEL_WIDTH, 128), jnp.bfloat16),
    ((128, MODEL_WIDTH), jnp.float32),
    ((128, MODEL_WIDTH), jnp.bfloat16),
    ((128, FEEDFORWARD_SIZE), jnp.float32),
    ((128, FEEDFORWARD_SIZE), jnp.float32),
    ((128, FEEDFORWARD_SIZE), jnp.bfloat16),
    ((128, MODEL_WIDTH), jnp.float32),
)


def sum_everywhere(me, parts, landed, sends, recvs):
    axes = (None, 2, 1, 0)

    def copy(stage, s):
        peer = sibling(me) if stage == 0 else moved(me, axes[stage], s)
        return pltpu.make_async_remote_copy(
            src_ref=parts.at[stage], dst_ref=landed.at[stage, s - 1],
            send_sem=sends.at[stage, s - 1], recv_sem=recvs.at[stage, s - 1],
            device_id=device(*peer), device_id_type=MESH)

    def steps(stage):
        return (1,) if stage == 0 else (2, 1, 3)

    def begin(value):
        parts[0] = value
        copy(0, 1).start()

    def step(stage):
        total = parts[stage]
        for s in steps(stage):
            copy(stage, s).wait_recv()
            total = total + landed[stage, s - 1]
        if stage < 3:
            parts[stage + 1] = total
            for s in steps(stage + 1):
                copy(stage + 1, s).start()
        return total

    def finish():
        for stage in range(4):
            for s in steps(stage):
                copy(stage, s).wait_send()

    return begin, step, finish


def first_gather(me, source, whole, stage, sends, recvs, swap_sends, swap_recvs, y_sends, y_recvs, own_sems):
    def along_y(s, y):
        return pltpu.make_async_remote_copy(
            src_ref=source, dst_ref=stage.at[y],
            send_sem=y_sends.at[s - 1], recv_sem=y_recvs.at[s - 1],
            device_id=device(*moved(me, 0, s)), device_id_type=MESH)

    def region(k, phase, at, core):
        index = [at[1], at[2]]
        if phase:
            index[k] = slice(None)
        return whole.at[tuple(index) + (core, pl.ds(*HALF_ROWS[k]))]

    def copy(src, dst, k, phase, s):
        return pltpu.make_async_remote_copy(
            src_ref=src, dst_ref=dst,
            send_sem=sends.at[k, phase, s - 1], recv_sem=recvs.at[k, phase, s - 1],
            device_id=device(*moved(me, 1 + (k + phase) % 2, s)), device_id_type=MESH)

    def send(k, phase, s):
        spot = region(k, phase, me, me[3])
        return copy(spot if phase else stage.at[0, pl.ds(*HALF_ROWS[k])], spot, k, phase, s)

    def landed(k, phase, s):
        spot = region(k, phase, moved(me, 1 + (k + phase) % 2, -s), me[3])
        return copy(spot, spot, k, phase, s)

    def swap(k, s, core):
        spot = region(k, 1, moved(me, 1 + (k + 1) % 2, -s), core)
        return pltpu.make_async_remote_copy(
            src_ref=spot, dst_ref=spot,
            send_sem=swap_sends.at[k, s], recv_sem=swap_recvs.at[k, s],
            device_id=device(*sibling(me)), device_id_type=MESH)

    own = pltpu.make_async_copy(source, stage.at[me[0]], own_sems.at[0])
    keep = pltpu.make_async_copy(stage.at[0], whole.at[me[1], me[2], me[3]], own_sems.at[1])

    def begin():
        for s in (2, 1, 3):
            along_y(s, me[0]).start()
        own.start()

    def spread():
        own.wait()
        for s in (1, 3, 2):
            along_y(s, (me[0] - s) % RING).wait_recv()
        for k in range(2):
            for s in (2, 1, 3):
                send(k, 0, s).start()
        keep.start()

    def forward():
        keep.wait()
        for k in range(2):
            for s in (1, 3, 2):
                landed(k, 0, s).wait_recv()
            for s in (2, 1, 3):
                send(k, 1, s).start()
            swap(k, 0, me[3]).start()

    def exchange():
        for s in (1, 3, 2):
            for k in (1, 0):
                landed(k, 1, s).wait_recv()
                swap(k, s, me[3]).start()

    def arrive():
        for k in range(2):
            for s in range(4):
                swap(k, s, 1 - me[3]).wait_recv()

    def finish():
        for s in (1, 2, 3):
            along_y(s, me[0]).wait_send()
        for k in range(2):
            for phase in range(2):
                for s in (1, 2, 3):
                    send(k, phase, s).wait_send()
            for s in range(4):
                swap(k, s, me[3]).wait_send()

    return begin, spread, forward, exchange, arrive, finish


def find_flags(blocks, number, flags, tall):
    column = jnp.broadcast_to(blocks, (128, 128)).T[:40]
    place_of = lax.broadcasted_iota(jnp.int32, (40, 128), 0)
    before = jnp.logical_or(place_of >= TILES - 1, column < number[:, :128])
    before = jnp.where(before, 1.0, 0.0)
    flags[...] = jnp.concatenate([before] * 3, axis=1)
    for t in range(40):
        tall[t] = jnp.broadcast_to(before[t : t + 1], (8, 128))


def own_block(positions):
    start = jnp.broadcast_to(positions[:, :1], (1, MODEL_WIDTH))
    block = lax.shift_right_logical(start, jnp.full(start.shape, 6, jnp.int32))
    return jnp.minimum(block, 63 - block).astype(jnp.float32), jnp.where(block >= 32, 1.0, 0.0)


def wide_turns(cosine_t, sine_t):
    cos, sin = cosine_t[...], sine_t[...]
    return jnp.concatenate([cos] * 4, axis=0).T, jnp.concatenate([-sin, sin] * 2, axis=0).T


def in_turn(rows, turn):
    other = jnp.concatenate([rows[64:], rows[:64]], axis=0)
    return jnp.where(jnp.broadcast_to(turn, rows.shape) > 0.5, other, rows)


def flatten(first, planes):
    for j in range(32):
        first[0, 48 * j : 48 * j + 48] = planes[j // 8, (j // 2) % 4, j % 2]


def forward_kernel(
    hidden, params, gain_part, positions, cosine_t, sine_t,
    result, gains, flags, tall, first_out, whole0_out, whole1_out, *refs
):
    count = len(SAVED)
    saved_out, saved = refs[:count], refs[count : 2 * count]
    (
        keys, values, scores, rows, first, planes, stage, mix, whole0, whole1, parts, landed, owns,
        spaced,
    ) = refs[2 * count : 2 * count + 14]
    sems = refs[2 * count + 14 :]
    save_sems, row_sems, first_sems = sems[0], sems[1:6], sems[6:13]
    sum_sems, mix_sem = sems[13:15], sems[15]
    weight_sems = (sems[16:21], sems[21:26])
    me = place()
    for y in range(2):
        @pl.when((me[0] == 0) == (y == 0))
        def _():
            pltpu.make_async_copy(params.at[1 - y], mix, mix_sem).start()
    number, turn = own_block(positions)
    x = in_turn(hidden[...].astype(jnp.float32).T, turn)
    scaled = x * inverse_root(x)
    greet_all(me)
    g_begin, g_step, g_finish = sum_everywhere(me, parts, landed, *sum_sems)
    f_begin, f_spread, f_forward, f_exchange, f_arrive, f_finish = first_gather(
        me, params.at[0], planes, stage, *first_sems
    )
    weights = (
        weight_gather(me, mix, whole0, *weight_sems[0]),
        weight_gather(me, params.at[1], whole1, *weight_sems[1], skip=True),
    )
    saves = []

    def save(layer, i):
        copy = pltpu.make_async_copy(
            saved[i].at[layer], saved_out[i].at[layer], save_sems.at[layer, i]
        )
        copy.start()
        saves.append(copy)

    def save_as(i, src, dst):
        copy = pltpu.make_async_copy(src, dst, save_sems.at[2, i])
        copy.start()
        saves.append(copy)

    f_begin()
    spaced[...] = jnp.zeros(spaced.shape, jnp.float32)
    lane = lax.broadcasted_iota(jnp.int32, (1, MODEL_WIDTH), 1)
    at = 9 * (32 * lax.axis_index("fsdp") + lax.axis_index("ctx"))
    own_gains = gain_part[...].astype(jnp.float32)
    for r in range(2 * LAYERS):
        row = jnp.zeros((1, MODEL_WIDTH), jnp.float32)
        for j in range(9):
            value = jnp.broadcast_to(own_gains[r // 2 : r // 2 + 1, j : j + 1], row.shape)
            row = jnp.where(lane + MODEL_WIDTH * (r % 2) == at + j, value, row)
        spaced[r : r + 1] = row
    spaced[4:5] = jnp.where(lane == lax.axis_index("ctx"), number, 0.0)
    g_begin(spaced[...])
    pltpu.make_async_copy(params.at[0], mix, mix_sem).wait()
    weights[0][0]()
    f_spread()
    g_step(0)
    g_step(1)
    f_forward()
    weights[0][1](1)
    blocks = g_step(2)
    find_flags(blocks[4:5, :128], number, flags, tall)
    gains[...] = g_step(3)
    f_exchange()
    f_arrive()
    flatten(first, planes)
    save_as(0, first, first_out)

    left = left_lanes()
    cos, sin = wide_turns(cosine_t, sine_t)
    for layer in range(LAYERS):
        whole = (whole0, whole1)[layer]
        w_begin, w_forward, w_relay, w_exchange, w_arrive, w_finish = weights[layer]
        n1, queries, kv, turned, lse, mixed, middle, n2, gate, up, product, start = [
            r.at[layer] for r in saved
        ]
        own = owns.at[layer]
        begin, forward, relay, arrive, finish = row_gather(
            me, own, kv, *[s.at[layer] for s in row_sems]
        )
        normed = (scaled * gains[2 * layer : 2 * layer + 1]).astype(jnp.bfloat16)
        n1[...] = normed
        start[...] = x
        for g in range(3):
            tile = dot_cols(normed, group_weights(first, g))
            tile = tile * jnp.where(left, cos, 1.0) + swapped(tile) * jnp.where(left, sin, 0.0)
            own[g] = tile.astype(jnp.bfloat16)
            begin(g)
        for j in range(5):
            tile = dot_cols(normed, first[0, 128 * j : 128 * j + 128])
            tile = (tile * cos + swapped(tile) * sin) * HEAD_SIZE ** (-0.5)
            spread_tile(queries, tile, j)
        for i in (0, 1, 11):
            save(layer, i)
        forward(0)
        forward(1)
        relay(0)
        forward(2)
        relay(1)

        def one(g, carry):
            arrive(g)

            def between():
                @pl.when(g == 0)
                def _():
                    relay(2)
                    w_forward(2)

                @pl.when(g == 2)
                def _():
                    w_relay()

            attend_group(
                g, me, kv, queries, flags, tall, turned, lse, keys, values, scores, rows, between
            )
            return carry

        lax.fori_loop(0, 3, one, 0)
        w_exchange()
        for i in (2, 3, 4):
            save(layer, i)
        for g in range(3):
            for h in range(3):
                mixed[64 * (3 * g + h) : 64 * (3 * g + h) + 64] = turned[
                    g, :, 128 * h : 128 * h + 128
                ].astype(jnp.bfloat16)
        mid = x + dot_rows(mixed[...], first[0, 960:1536])
        middle[...] = mid
        normed = (mid * inverse_root(mid) * gains[2 * layer + 1 : 2 * layer + 2]).astype(jnp.bfloat16)
        n2[...] = normed
        for i in (5, 6, 7):
            save(layer, i)
        w_arrive()
        if layer == 0:
            weights[1][0]()
        save_as(1 + layer, whole, (whole0_out, whole1_out)[layer])
        total = mid
        for i in range(4):
            part = pl.ds(384 * i, 384)
            gate_values = dot_cols(normed, whole[1, i].reshape(384, MODEL_WIDTH))
            up_values = dot_cols(normed, whole[2, i].reshape(384, MODEL_WIDTH))
            rounded = (gate_values * jax.nn.sigmoid(gate_values) * up_values).astype(jnp.bfloat16)
            gate[:, part] = gate_values
            up[:, part] = up_values
            product[:, part] = rounded
            total = total + jnp.dot(
                rounded, whole[3, i].reshape(384, MODEL_WIDTH), preferred_element_type=jnp.float32
            )
        for i in (8, 9, 10):
            save(layer, i)
        if layer == 0:
            weights[1][1](1)
            x = total
            scaled = x * inverse_root(x)
            saves[0].wait()
            saves.pop(0)
            flatten(first, whole0.at[0])
        else:
            result[...] = in_turn(total, turn).T.astype(jnp.bfloat16)
        for g in range(3):
            finish(g)
    g_finish()
    f_finish()
    for w in weights:
        w[5]()
    for copy in saves:
        copy.wait()


TURNED_BF16 = jax.ShapeDtypeStruct((MODEL_WIDTH, 128), jnp.bfloat16)
VMEM_SPEC = pl.BlockSpec(memory_space=pltpu.VMEM)
HBM_SPEC = pl.BlockSpec(memory_space=pl.ANY)


def forward_pass(hidden, params, gains, positions, turns):
    bf, w = jnp.bfloat16, MODEL_WIDTH
    dma = pltpu.SemaphoreType.DMA
    outs = pl.pallas_call(
        forward_kernel,
        out_shape=(
            TURNED_BF16,
            jax.ShapeDtypeStruct((8, w), jnp.float32),
            jax.ShapeDtypeStruct((40, LANES), jnp.float32),
            jax.ShapeDtypeStruct((40, 8, 128), jnp.float32),
            jax.ShapeDtypeStruct((1, 1536, w), bf),
            WHOLE,
            WHOLE,
        ) + tuple(jax.ShapeDtypeStruct((LAYERS,) + shape, dtype) for shape, dtype in SAVED),
        in_specs=[VMEM_SPEC, HBM_SPEC] + [VMEM_SPEC] * 4,
        out_specs=(VMEM_SPEC,) * 4 + (HBM_SPEC,) * (3 + len(SAVED)),
        scratch_shapes=[pltpu.VMEM((LAYERS,) + shape, dtype) for shape, dtype in SAVED] + [
            pltpu.VMEM((64 * TILES, 256), bf),
            pltpu.VMEM((64 * TILES, 256), bf),
            pltpu.VMEM((64 * TILES, LANES), jnp.float32),
            pltpu.VMEM((40, LANES), jnp.float32),
            pltpu.VMEM((1, 1536, w), bf),
            pltpu.VMEM((4, 4, 2, 48, w), bf),
            pltpu.VMEM((4, 48, w), bf),
            pltpu.VMEM((48, w), bf),
            pltpu.VMEM(WHOLE.shape, bf),
            pltpu.VMEM(WHOLE.shape, bf),
            pltpu.VMEM((4, 8, w), jnp.float32),
            pltpu.VMEM((4, 3, 8, w), jnp.float32),
            pltpu.VMEM((LAYERS, 3, 128, 128), bf),
            pltpu.VMEM((8, w), jnp.float32),
            dma((3, len(SAVED))),
            dma((LAYERS, 3, 2, 2, 4)),
            dma((LAYERS, 3, 2, 2, 4)),
            dma((LAYERS, 3, 2, 4)),
            dma((LAYERS, 3, 2, 4)),
            dma((LAYERS, 3)),
            dma((2, 2, 3)),
            dma((2, 2, 3)),
            dma((2, 4)),
            dma((2, 4)),
            dma((3,)),
            dma((3,)),
            dma((2,)),
            dma((4, 3)),
            dma((4, 3)),
            dma,
        ] + WEIGHT_GATHER_SEMS * 2,
        compiler_params=pltpu.CompilerParams(
            collective_id=1, has_side_effects=True, vmem_limit_bytes=58 * 2**20
        ),
        name="forward_pass",
    )(hidden, params, gains, positions, *turns)
    return outs[:7], outs[7:]


def norm_back(grad_normed, values, gain):
    inverse = inverse_root(values)
    unit = values * inverse
    grad_gain = jnp.sum(grad_normed * unit, axis=0, keepdims=True)
    scaled = grad_normed * gain
    grad_values = inverse * (
        scaled - unit * jnp.mean(scaled * unit, axis=-1, keepdims=True)
    )
    return grad_values, grad_gain


def products_first(gq, gkv, mixed, n1, gb):
    parts = [jnp.dot(gq[...], n1[...], preferred_element_type=jnp.float32)]
    both = [dot_rows(gkv[g], n1[...]) for g in range(3)]
    parts.append(jnp.concatenate([m[:64] for m in both], axis=0))
    parts.append(jnp.concatenate([m[64:] for m in both], axis=0))
    parts.append(jnp.dot(mixed[...], gb[...], preferred_element_type=jnp.float32))
    return [
        p.astype(jnp.bfloat16).reshape(p.shape[0] // 48, 48, MODEL_WIDTH) for p in parts
    ]


BIG = (2, 8, 9, 10)


def last_reduce(me, grads, halves, landed_a, sum_a, landed_b, sum_b, landed_y, swap_sends, swap_recvs, sends, recvs, y_sends, y_recvs):
    def swap(x):
        return pltpu.make_async_remote_copy(
            src_ref=grads.at[x, :, 1 - me[3]], dst_ref=halves.at[x],
            send_sem=swap_sends.at[x], recv_sem=swap_recvs.at[x],
            device_id=device(*sibling(me)), device_id_type=MESH)

    def copy(stage, src, dst, k, s):
        return pltpu.make_async_remote_copy(
            src_ref=src, dst_ref=dst,
            send_sem=sends.at[stage, k, s - 1], recv_sem=recvs.at[stage, k, s - 1],
            device_id=device(*moved(me, 1 + (k + 1 + stage) % 2, s)), device_id_type=MESH)

    def send(stage, k, s):
        axis = 1 + (k + 1 + stage) % 2
        to = moved(me, axis, s)[axis]
        rows = pl.ds(*HALF_ROWS[k])
        if stage == 0:
            index = [slice(None)] * 2
            index[axis - 1] = to
            return copy(0, halves.at[tuple(index) + (rows,)], landed_a.at[s - 1, :, rows], k, s)
        return copy(1, sum_a.at[to, rows], landed_b.at[s - 1, rows], k, s)

    def along_y(s):
        return pltpu.make_async_remote_copy(
            src_ref=sum_b, dst_ref=landed_y.at[s - 1],
            send_sem=y_sends.at[s - 1], recv_sem=y_recvs.at[s - 1],
            device_id=device(*moved(me, 0, s)), device_id_type=MESH)

    def begin():
        for x in range(4):
            swap(x).wait_recv()
            for z in range(4):
                halves[x, z] = (
                    grads[x, z, me[3]].astype(jnp.float32) + halves[x, z].astype(jnp.float32)
                ).astype(jnp.bfloat16)
        for s in (2, 1, 3):
            for k in range(2):
                send(0, k, s).start()

    def second():
        for k in (1, 0):
            rows = pl.ds(*HALF_ROWS[k])
            for s in (1, 3, 2):
                send(0, k, s).wait_recv()
            axis = 1 + (k + 1) % 2
            for i in range(4):
                spot = [i]
                spot.insert(axis - 1, me[axis])
                total = halves[tuple(spot) + (rows,)].astype(jnp.float32)
                for s in range(3):
                    total = total + landed_a[s, i, rows].astype(jnp.float32)
                sum_a[i, rows] = total.astype(jnp.bfloat16)
            for s in (2, 1, 3):
                send(1, k, s).start()

    def third():
        for k in (1, 0):
            rows = pl.ds(*HALF_ROWS[k])
            for s in (1, 3, 2):
                send(1, k, s).wait_recv()
            total = sum_a[me[1 + k % 2], rows].astype(jnp.float32)
            for s in range(3):
                total = total + landed_b[s, rows].astype(jnp.float32)
            sum_b[rows] = total.astype(jnp.bfloat16)
        for s in (2, 1, 3):
            along_y(s).start()

    def finish(out):
        total = sum_b[...].astype(jnp.float32)
        for s in (1, 3, 2):
            along_y(s).wait_recv()
            total = total + landed_y[s - 1].astype(jnp.float32)
        out[...] = total
        for x in range(4):
            swap(x).wait_send()
        for s in (1, 2, 3):
            along_y(s).wait_send()
            for stage in range(2):
                for k in range(2):
                    send(stage, k, s).wait_send()

    return swap, begin, second, third, finish


def backward_kernel(
    cotangent, positions, first0, first1, rest0, rest1,
    gains, cosine_t, sine_t, flags, tall, *refs
):
    count = len(SAVED)
    kept, refs = refs[:count], refs[count:]
    grad_hidden, owned, gain_sums = refs[:3]
    (
        keys, values, scores, lse_rows, inner_rows, dkv, spots, inner, dq, sums, ggate, gup,
        firsts, whole, gq, gkv, gb, gain_terms, reduced, load_sems, free_sem,
    ) = refs[3:24]
    row_refs = refs[24:32]
    weight_refs = refs[32:43]
    last_refs = refs[43:55]
    sum_refs = refs[55:59]
    saved = refs[59:]
    me = place()
    peers = [moved(me, a, s) for a, s in ALL_PEERS] + [sibling(me)]

    def view(layer, i):
        return saved[i] if i in BIG else saved[i].at[layer]

    def load(layer, i):
        return pltpu.make_async_copy(kept[i].at[layer], view(layer, i), load_sems.at[layer, i])

    def load_rest(layer):
        return pltpu.make_async_copy(
            (rest0, rest1)[layer].at[pl.ds(1, 3)], whole, load_sems.at[layer, count]
        )

    def load_first(layer):
        return pltpu.make_async_copy(
            (first0, first1)[layer].at[0], firsts.at[layer], load_sems.at[layer, count + 1]
        )

    load_rest(1).start()
    for i in (8, 9, 10, 7, 6, 3, 0, 1, 4, 5, 2, 11):
        load(1, i).start()
    load_first(1).start()
    load_first(0).start()
    for i in range(count):
        if i not in BIG:
            load(0, i).start()
    greet(peers)
    begin, second, third, finish, drain = row_reduce(me, dkv, sums, *row_refs)
    swap, halve, w_begin, w_second, w_third, w_finish = weight_reduce(me, *weight_refs)
    grads, halves = weight_refs[0], weight_refs[1]
    l_swap, l_begin, l_second, l_third, l_finish = last_reduce(me, grads.at[0], *last_refs)
    g_begin, g_step, g_finish = sum_everywhere(me, *sum_refs)
    left = left_lanes()
    cos, sin = wide_turns(cosine_t, sine_t)
    cos, sin = jnp.where(left, cos, 1.0), jnp.where(left, sin, 0.0)
    gain_terms[...] = jnp.zeros(gain_terms.shape, jnp.float32)
    turn = own_block(positions)[1]
    gr = in_turn(cotangent[...].astype(jnp.float32).T, turn)

    def first_products(layer, done):
        at = 0
        for cut in products_first(gq, gkv, view(layer, 5), view(layer, 0), gb):
            for i in range(cut.shape[0]):
                j = at + i
                grads[0, j // 8, (j // 2) % 4, j % 2] = cut[i]
                done(j)
            at += cut.shape[0]

    for layer in (1, 0):
        n1, queries, kv, turned, lse, mixed, middle, n2, gate, up, product, start = [
            view(layer, i) for i in range(count)
        ]
        first = firsts.at[layer]
        order = (1, 2, 3) if layer == 1 else (1, 2, 3, 0)
        load_rest(layer).wait()
        for i in (8, 9, 10, 7, 6):
            load(layer, i).wait()
        gd = gr.astype(jnp.bfloat16)
        normed = n2[...]
        grad_normed = jnp.zeros((128, MODEL_WIDTH), jnp.float32)
        for i in range(4):
            part = pl.ds(384 * i, 384)
            grad_product = dot_cols(gd, whole[2, i])
            gate_values, up_values = gate[:, part], up[:, part]
            s = jax.nn.sigmoid(gate_values)
            gg = (
                grad_product * up_values * (s * (1.0 + gate_values * (1.0 - s)))
            ).astype(jnp.bfloat16)
            gu = (grad_product * (gate_values * s)).astype(jnp.bfloat16)
            ggate[:, part] = gg
            gup[:, part] = gu
            grad_normed = grad_normed + jnp.dot(
                gg, whole[0, i], preferred_element_type=jnp.float32
            ) + jnp.dot(gu, whole[1, i], preferred_element_type=jnp.float32)
        if layer == 0:
            w_finish((1, 2, 3), reduced.at[1])
            for peer in peers:
                pl.semaphore_signal(
                    free_sem, inc=1, device_id=device(*peer), device_id_type=MESH
                )
            first_products(1, lambda j: None)
        for y, source, right in ((1, ggate, normed), (2, gup, normed), (3, product, gd)):
            for i in range(4):
                flat = dot_rows(source[:, 384 * i : 384 * i + 384], right).astype(jnp.bfloat16)
                grads[y, i] = flat.reshape(4, 2, 48, MODEL_WIDTH)
            if layer == 1:
                swap(y).start()
        if layer == 1:
            load_rest(0).start()
            for i in (8, 9, 10):
                load(0, i).start()
        grad_middle, grad_gain = norm_back(
            grad_normed, middle[...], gains[2 * layer + 1 : 2 * layer + 2]
        )
        gain_terms[2 * layer + 1 : 2 * layer + 2] = grad_gain
        grad_middle = grad_middle + gr
        branch = grad_middle.astype(jnp.bfloat16)
        gb[...] = branch
        load_first(layer).wait()
        for i in (3, 0, 1, 4, 5, 11):
            load(layer, i).wait()
        for j in range(5):
            width = min(128, 576 - 128 * j)
            tile = dot_cols(branch, first[960 + 128 * j : 960 + 128 * j + width])
            if width < 128:
                tile = jnp.concatenate([tile, jnp.zeros((128, 128 - width), jnp.float32)], axis=1)
            spread_tile(spots, tile, j)
        for g in range(3):
            for h in range(3):
                at = 64 * (3 * g + h)
                grad_turned = dot_cols(first[960 + at : 1024 + at], branch)
                grad_turned = grad_turned.astype(jnp.bfloat16).astype(jnp.float32)
                row = jnp.sum(
                    turned[g, :, 128 * h : 128 * h + 128] * grad_turned, axis=0, keepdims=True
                )
                inner[g, :, 128 * h : 128 * h + 128] = jnp.broadcast_to(row, (8, 128))
        load(layer, 2).wait()
        if layer == 0:
            pl.semaphore_wait(free_sem, len(peers))
            for y in order:
                swap(y).start()

        def one(g, carry):
            attend_back_group(
                g, me, kv, queries, spots, lse, inner, flags, tall, dq, dkv,
                keys, values, scores, lse_rows, inner_rows,
            )
            begin(g)

            @pl.when(g == 0)
            def _():
                for y in order:
                    halve(y)
                if layer == 1:
                    halves[0] = jnp.zeros(halves.shape[1:], jnp.bfloat16)
                w_begin()

            @pl.when(g == 1)
            def _():
                second(0)

            @pl.when(g == 2)
            def _():
                third(0)
                second(1)

            return carry

        lax.fori_loop(0, 3, one, 0)
        if layer == 1:
            load(0, 2).start()
        second(2)
        third(1)
        for g in range(3):
            for h in range(3):
                rows = dq[g, :, 128 * h : 128 * h + 128] * HEAD_SIZE ** (-0.5)
                a, b = rows[:32], rows[32:]
                at = 64 * (3 * g + h)
                gq[at : at + 32] = (a * cosine_t[...] + b * sine_t[...]).astype(jnp.bfloat16)
                gq[at + 32 : at + 64] = (b * cosine_t[...] - a * sine_t[...]).astype(jnp.bfloat16)
        third(2)
        w_second()
        grad_normed = dot_rows(gq[...], first[:576])
        for g in range(3):
            finish(g)
            tile = sums[g]
            tile = (tile * cos - swapped(tile) * sin).astype(jnp.bfloat16)
            gkv[g] = tile
            weights = jnp.concatenate(
                [first[576 + 64 * g : 640 + 64 * g], first[768 + 64 * g : 832 + 64 * g]], axis=0
            )
            grad_normed = grad_normed + jnp.dot(tile, weights, preferred_element_type=jnp.float32)
        if layer == 0:
            swap(0).wait_send()
            first_products(0, lambda j: l_swap(j // 8).start() if j % 8 == 7 else None)
        w_third()
        grad_values, grad_gain = norm_back(
            grad_normed, start[...], gains[2 * layer : 2 * layer + 1]
        )
        gain_terms[2 * layer : 2 * layer + 1] = grad_gain
        gr = grad_values + grad_middle
        for g in range(3):
            drain(g)
    grad_hidden[...] = in_turn(gr, turn).T
    g_begin(gain_terms[...])
    l_begin()
    g_step(0)
    l_second()
    g_step(1)
    l_third()
    w_finish((1, 2, 3), reduced.at[0])
    g_step(2)
    gain_sums[...] = g_step(3)
    l_finish(reduced.at[2])
    g_finish()
    at_front = jnp.broadcast_to(me[0], (48, MODEL_WIDTH)) == 0
    owned[0] = jnp.where(at_front, reduced[2], reduced[0])
    owned[1] = jnp.where(at_front, reduced[0], reduced[1])


def backward_pass(cotangent, positions, first, whole0, whole1, gains, turns, flags, kept):
    planes, rows = (4, 1536, MODEL_WIDTH), (4, 4, 384, MODEL_WIDTH)
    bf, w = jnp.bfloat16, MODEL_WIDTH
    dma = pltpu.SemaphoreType.DMA
    return pl.pallas_call(
        backward_kernel,
        out_shape=(
            jax.ShapeDtypeStruct((w, 128), jnp.float32),
            jax.ShapeDtypeStruct((LAYERS, 48, w), jnp.float32),
            jax.ShapeDtypeStruct((8, w), jnp.float32),
        ),
        in_specs=[VMEM_SPEC] * 2 + [HBM_SPEC] * 4 + [VMEM_SPEC] * 5 + [HBM_SPEC] * len(SAVED),
        out_specs=(VMEM_SPEC,) * 3,
        scratch_shapes=[
            pltpu.VMEM((64 * TILES, 256), bf),
            pltpu.VMEM((64 * TILES, 256), bf),
            pltpu.VMEM((64 * TILES, LANES), jnp.float32),
            pltpu.VMEM((40, LANES), jnp.float32),
            pltpu.VMEM((40, LANES), jnp.float32),
            pltpu.VMEM((3, 4, 4, 2, 128, 128), bf),
            pltpu.VMEM((3, LANES, 256), bf),
            pltpu.VMEM((3, 8, LANES), jnp.float32),
            pltpu.VMEM((3, 64, LANES), jnp.float32),
            pltpu.VMEM((3, 128, 128), jnp.float32),
            pltpu.VMEM((128, FEEDFORWARD_SIZE), bf),
            pltpu.VMEM((128, FEEDFORWARD_SIZE), bf),
            pltpu.VMEM((LAYERS, 1536, w), bf),
            pltpu.VMEM((3, 4, 384, w), bf),
            pltpu.VMEM((w, 128), bf),
            pltpu.VMEM((3, 128, 128), bf),
            pltpu.VMEM((128, w), bf),
            pltpu.VMEM((8, w), jnp.float32),
            pltpu.VMEM((3, 48, w), jnp.float32),
            dma((LAYERS, len(SAVED) + 2)),
            pltpu.SemaphoreType.REGULAR,
        ] + row_reduce_scratch() + weight_reduce_scratch() + [
            pltpu.VMEM((4, 4, 48, w), bf),
            pltpu.VMEM((3, 4, 48, w), bf),
            pltpu.VMEM((4, 48, w), bf),
            pltpu.VMEM((3, 48, w), bf),
            pltpu.VMEM((48, w), bf),
            pltpu.VMEM((3, 48, w), bf),
            dma((4,)),
            dma((4,)),
            dma((2, 2, 3)),
            dma((2, 2, 3)),
            dma((3,)),
            dma((3,)),
            pltpu.VMEM((4, 8, w), jnp.float32),
            pltpu.VMEM((4, 3, 8, w), jnp.float32),
            dma((4, 3)),
            dma((4, 3)),
        ] + [
            pltpu.VMEM(shape if i in BIG else (LAYERS,) + shape, dtype)
            for i, (shape, dtype) in enumerate(SAVED)
        ],
        compiler_params=pltpu.CompilerParams(
            collective_id=2, has_side_effects=True, vmem_limit_bytes=62 * 2**20
        ),
        name="backward_pass",
    )(
        cotangent, positions, first, whole0.reshape(planes), whole0.reshape(rows),
        whole1.reshape(rows), gains, *turns, *flags, *kept
    )


def turn_tables(places):
    half = HEAD_SIZE // 2
    frequency = 1.0 / THETA ** (2 * jnp.arange(half).astype(jnp.float32) / HEAD_SIZE)
    phases = frequency[:, None] * places.astype(jnp.float32)[None, :]
    return jnp.cos(phases), jnp.sin(phases)


def on_device(hidden_in, positions, params, gains, cotangent):
    places = positions[0]
    turn = places[0] >= SEQ_LEN // 2
    turns = turn_tables(jnp.where(turn, jnp.concatenate([places[64:], places[:64]]), places))
    main, kept = forward_pass(hidden_in[0].T, params, gains, positions, turns)
    hidden_out, gain_rows, flags = main[0], main[1], main[2:4]
    grad_in, owned, gain_sums = backward_pass(
        cotangent[0].T, positions, *main[4:7], gain_rows, turns, flags, kept
    )
    index = lax.axis_index("fsdp") * 32 + lax.axis_index("ctx")
    gain_sums = gain_sums[:4].reshape(LAYERS, 2 * MODEL_WIDTH)
    owned_gains = lax.dynamic_slice(gain_sums, (0, index * 9), (LAYERS, 9))
    return (hidden_out.T[None], grad_in.T[None], owned, owned_gains)


def solution(mesh):
    return jax.shard_map(
        on_device,
        mesh=mesh,
        in_specs=(
            P("fsdp", "ctx", None),
            P("fsdp", "ctx"),
            P(None, ("fsdp", "ctx"), None),
            P(None, ("fsdp", "ctx")),
            P("fsdp", "ctx", None),
        ),
        out_specs=(
            P("fsdp", "ctx", None),
            P("fsdp", "ctx", None),
            P(None, ("fsdp", "ctx"), None),
            P(None, ("fsdp", "ctx")),
        ),
        check_vma=False,
    )
```
